128 devices in a mesh: band: 8 (over z, core), patch: 16 (over y, x).
Axes of the slice: x: 4, y: 4, z: 4, core: 2. Of those that a mesh axis runs over, the one named last changes fastest.
Arguments:
- grid_latent: bfloat16 [16384, 512], P(('band', 'patch')), may hold values from -6 to 6
- mesh_latent: bfloat16 [16384, 512], P(('band', 'patch')), may hold values from -6 to 6
- weights: bfloat16 [20, 512, 512], replicated, may hold values from -0.25 to 0.25
- enc_dev: int32 [49152, 1], P(('band', 'patch')), may hold values from 0 to 127; in each aligned block of 384 rows (0 to 383, 384 to 767, ...) at most 6 rows name the same one
- enc_row: int32 [49152], P(('band', 'patch')), may hold values from 0 to 127
- enc_dst: int32 [49152], P(('band', 'patch')), may hold values from 0 to 127
- proc_dev: int32 [49152, 1], P(('band', 'patch')), may hold values from 0 to 127; in each aligned block of 384 rows (0 to 383, 384 to 767, ...) at most 6 rows name the same one
- proc_row: int32 [49152], P(('band', 'patch')), may hold values from 0 to 127
- proc_dst: int32 [49152], P(('band', 'patch')), may hold values from 0 to 127
- loc_src: int32 [32768], P(('band', 'patch')), may hold values from 0 to 127
- loc_dst: int32 [32768], P(('band', 'patch')), may hold values from 0 to 127
- dec_dev: int32 [49152, 1], P(('band', 'patch')), may hold values from 0 to 127; in each aligned block of 384 rows (0 to 383, 384 to 767, ...) at most 6 rows name the same one
- dec_row: int32 [49152], P(('band', 'patch')), may hold values from 0 to 127
Outputs:
- decoded: bfloat16 [16384, 512], P(('band', 'patch'))
The draws below stay inside these ranges and needn't reach their ends.
Inputs may be any that keep to these rules, and one draw needn't show every extreme that they name: `enc_dev`: among the rows of one device, no device number appears more than 6 times. `proc_dev`: among the rows of one device, no device number appears more than 6 times. `dec_dev`: among the rows of one device, no device number appears more than 6 times.
All inputs are finite; a program needn't handle non-finite values.
Results may differ from the reference program's by a relative error of at most 0.013.
Values may be sent and summed in bfloat16 or wider, within the bound.
No kernel may reach another device: no remote copies, remote signals or barrier semaphores. Data moves between devices by JAX's collectives and lax.ppermute only.
A program may use at most 128 MiB of HBM per device.

```python
import math
import jax
import jax.numpy as jnp
import numpy as np
from jax import lax

L = 512
G_DEV = 128
M_DEV = 128
NW = 20
EDGES = 384
E_LOC = 256
CAP = 6
GRID = 16384
MESH = 16384
DEVICES = 128


def place_ends(drawn, key, least, high):
    spot = [jax.random.randint(jax.random.fold_in(key, axis), (), 0, length) for axis, length in enumerate(drawn.shape)]
    main_axis = drawn.shape.index(max(drawn.shape))
    beside = spot[:main_axis] + [(spot[main_axis] + 1) % drawn.shape[main_axis]] + spot[main_axis + 1:]
    return drawn.at[tuple(spot)].set(least).at[tuple(beside)].set(high)


def block_scale(own_key, extent, cuts, smallest, largest):
    level, own = 1.0, jax.random.fold_in(own_key, 6)
    for dim, blocks in cuts:
        draws = jnp.exp(jax.random.uniform(jax.random.fold_in(own, dim), (blocks,), jnp.float32, smallest / len(cuts), largest / len(cuts)))
        level = level * jnp.repeat(draws, extent[dim] // blocks).reshape([-1 if axis == dim else 1 for axis in range(len(extent))])
    return level


def routed_block(stream_key, own, number, rows, count, top, limit, skew):
    sequence = jax.random.permutation(stream_key, count)
    heavy_load, common = portions_of(count, rows * top, limit, skew, True), portions_of(count, rows * top, limit, skew, False)
    places = jnp.arange(count)

    def named(lengths, offset_by):
        used = int((lengths > 0).sum())
        fixed = max(1, used // 4)
        passed = fixed + (places - fixed + offset_by * (used - fixed)) % max(1, count - fixed)
        return jnp.zeros((count,), jnp.int32).at[sequence[jnp.where(places < fixed, places, passed)]].set(jnp.asarray(lengths, jnp.int32))

    lengths = jnp.where(number % 4 == 0, named(heavy_load, number // 4), named(common, number - number // 4 - 1))
    mixed = jax.random.permutation(jax.random.fold_in(own, 3), count)
    giver, taker = mixed[0:count // 2 * 2:2], mixed[1:count // 2 * 2:2]
    slack = jnp.minimum(lengths[giver] - 1, limit - lengths[taker]) // 2
    slack = jnp.where((giver == sequence[0]) | (taker == sequence[0]) | (lengths[taker] == 0), 0, jnp.maximum(slack, 0))
    passed = jax.random.randint(jax.random.fold_in(own, 4), (count // 2,), 0, 1 << 20) % (slack + 1)
    lengths = lengths.at[giver].add(-passed).at[taker].add(passed)
    labels = jnp.searchsorted(jnp.cumsum(lengths), jnp.arange(rows * top), side="right").astype(jnp.int32)
    table = labels.reshape(top, rows).T
    table = table[jax.random.permutation(jax.random.fold_in(own, 1), rows)]
    offset_by = jax.random.randint(jax.random.fold_in(own, 2), (rows, 1), 0, top)
    return jnp.take_along_axis(table, (jnp.arange(top)[None, :] + offset_by) % top, axis=1)


def portions_of(amount, total, bound, lean, full):
    loads = [(1 << 20) // math.isqrt(grade ** lean) + 1 for grade in range(1, amount + 1)]
    largest = bound if full else min(bound, max(-(-total // amount), total * loads[0] // sum(loads)))
    least = 1 if total - largest >= amount - 1 else 0
    holding, surplus = [largest] + [least] * (amount - 1), total - largest - least * (amount - 1)
    while surplus > 0:
        free = [i for i in range(1, amount) if holding[i] < largest] or [i for i in range(1, amount) if holding[i] < bound]
        mass, budget = sum([loads[i] for i in free]), surplus
        for i in free:
            addition = min(bound - holding[i], max(1, budget * loads[i] // mass), surplus)
            holding[i] = holding[i] + addition
            surplus = surplus - addition
    return np.array(holding)


def bell_draw(key, dims, scale, reach, cuts=(), held_as=jnp.bfloat16):
    entries = scale * jax.random.normal(key, dims, jnp.float32)
    if cuts:
        entries = entries * block_scale(key, dims, cuts, -0.22, 0.18)
    return jnp.clip(entries, -reach, reach).astype(held_as)


def setup_inputs(seed: int = 0) -> dict:
    streams_of = jax.random.split(jax.random.key(seed), 14)
    grid_latent = bell_draw(streams_of[0], (GRID, L), 1.0, 6.0, ((0, 128),))
    mesh_latent = bell_draw(streams_of[1], (MESH, L), 1.0, 6.0, ((0, 128),))
    weights = bell_draw(streams_of[2], (NW, L, L), L ** -0.5, 0.25)
    enc_dev_keys = jax.random.split(jax.random.fold_in(streams_of[3], 1), (DEVICES * EDGES) // EDGES)
    enc_dev_turns = jax.random.permutation(jax.random.fold_in(streams_of[3], 3), (DEVICES * EDGES) // EDGES)
    enc_dev = jax.vmap(lambda own, number: routed_block(jax.random.fold_in(streams_of[3], 2), own, number, EDGES, DEVICES, 1, CAP, 2))(enc_dev_keys, enc_dev_turns).reshape((DEVICES * EDGES, 1))
    enc_row = place_ends(jax.random.randint(streams_of[4], (DEVICES * EDGES,), 0, G_DEV), jax.random.fold_in(streams_of[4], 1), 0, G_DEV - 1).astype(jnp.int32)
    enc_dst = place_ends(jax.random.randint(streams_of[5], (DEVICES * EDGES,), 0, M_DEV), jax.random.fold_in(streams_of[5], 1), 0, M_DEV - 1).astype(jnp.int32)
    proc_dev_keys = jax.random.split(jax.random.fold_in(streams_of[6], 1), (DEVICES * EDGES) // EDGES)
    proc_dev_turns = jax.random.permutation(jax.random.fold_in(streams_of[6], 3), (DEVICES * EDGES) // EDGES)
    proc_dev = jax.vmap(lambda own, number: routed_block(jax.random.fold_in(streams_of[6], 2), own, number, EDGES, DEVICES, 1, CAP, 2))(proc_dev_keys, proc_dev_turns).reshape((DEVICES * EDGES, 1))
    proc_row = place_ends(jax.random.randint(streams_of[7], (DEVICES * EDGES,), 0, M_DEV), jax.random.fold_in(streams_of[7], 1), 0, M_DEV - 1).astype(jnp.int32)
    proc_dst = place_ends(jax.random.randint(streams_of[8], (DEVICES * EDGES,), 0, M_DEV), jax.random.fold_in(streams_of[8], 1), 0, M_DEV - 1).astype(jnp.int32)
    loc_src = place_ends(jax.random.randint(streams_of[9], (DEVICES * E_LOC,), 0, M_DEV), jax.random.fold_in(streams_of[9], 1), 0, M_DEV - 1).astype(jnp.int32)
    loc_dst = place_ends(jax.random.randint(streams_of[10], (DEVICES * E_LOC,), 0, M_DEV), jax.random.fold_in(streams_of[10], 1), 0, M_DEV - 1).astype(jnp.int32)
    dec_dev_keys = jax.random.split(jax.random.fold_in(streams_of[11], 1), (DEVICES * EDGES) // EDGES)
    dec_dev_turns = jax.random.permutation(jax.random.fold_in(streams_of[11], 3), (DEVICES * EDGES) // EDGES)
    dec_dev = jax.vmap(lambda own, number: routed_block(jax.random.fold_in(streams_of[11], 2), own, number, EDGES, DEVICES, 1, CAP, 2))(dec_dev_keys, dec_dev_turns).reshape((DEVICES * EDGES, 1))
    dec_row = place_ends(jax.random.randint(streams_of[12], (DEVICES * EDGES,), 0, M_DEV), jax.random.fold_in(streams_of[12], 1), 0, M_DEV - 1).astype(jnp.int32)
    return dict(grid_latent=grid_latent, mesh_latent=mesh_latent, weights=weights, enc_dev=enc_dev, enc_row=enc_row, enc_dst=enc_dst, proc_dev=proc_dev, proc_row=proc_row, proc_dst=proc_dst, loc_src=loc_src, loc_dst=loc_dst, dec_dev=dec_dev, dec_row=dec_row)


epsilon = 1e-05

def layer_norm(values):
    average = lax.optimization_barrier(jnp.mean(values, axis=-1, keepdims=True))
    centred = values - average
    spread = lax.optimization_barrier(jnp.mean(centred * centred, axis=-1, keepdims=True))
    return centred * lax.rsqrt(spread + epsilon)

def perceptron(pieces, first_mats, second):
    summed = jnp.dot(pieces[0], first_mats[0], preferred_element_type=jnp.float32)
    for piece, matrix in zip(pieces[1:], first_mats[1:]):
        summed = summed + jnp.dot(piece, matrix, preferred_element_type=jnp.float32)
    hidden = jax.nn.silu(summed).astype(jnp.bfloat16)
    return layer_norm(jnp.dot(hidden, second, preferred_element_type=jnp.float32))

def residual_add(base, update):
    return (base.astype(jnp.float32) + update).astype(jnp.bfloat16)

def reference(grid_latent, mesh_latent, weights, enc_dev, enc_row, enc_dst, proc_dev, proc_row, proc_dst, loc_src, loc_dst, dec_dev, dec_row):
    mesh_total = M_DEV * DEVICES
    edge_owner = jnp.arange(DEVICES * EDGES, dtype=jnp.int32) // EDGES * M_DEV
    local_owner = jnp.arange(DEVICES * E_LOC, dtype=jnp.int32) // E_LOC * M_DEV
    enc_from = enc_dev[:, 0] * G_DEV + enc_row
    enc_to = edge_owner + enc_dst
    enc_msg = perceptron((grid_latent[enc_from], mesh_latent[enc_to]), (weights[0], weights[1]), weights[2]).astype(jnp.bfloat16)
    enc_sum = jax.ops.segment_sum(enc_msg.astype(jnp.float32), enc_to, num_segments=mesh_total).astype(jnp.bfloat16)
    mesh_one = residual_add(mesh_latent, perceptron((mesh_latent, enc_sum), (weights[3], weights[4]), weights[5]))
    grid_one = residual_add(grid_latent, perceptron((grid_latent,), (weights[6],), weights[7]))
    far_from = proc_dev[:, 0] * M_DEV + proc_row
    far_to = edge_owner + proc_dst
    near_from = local_owner + loc_src
    near_to = local_owner + loc_dst
    far_msg = perceptron((mesh_one[far_from], mesh_one[far_to]), (weights[8], weights[9]), weights[10]).astype(jnp.bfloat16)
    near_msg = perceptron((mesh_one[near_from], mesh_one[near_to]), (weights[8], weights[9]), weights[10]).astype(jnp.bfloat16)
    proc_sum = jax.ops.segment_sum(far_msg.astype(jnp.float32), far_to, num_segments=mesh_total)
    proc_sum = proc_sum + jax.ops.segment_sum(near_msg.astype(jnp.float32), near_to, num_segments=mesh_total)
    proc_sum = proc_sum.astype(jnp.bfloat16)
    mesh_two = residual_add(mesh_one, perceptron((mesh_one, proc_sum), (weights[11], weights[12]), weights[13]))
    dec_from = dec_dev[:, 0] * M_DEV + dec_row
    targets = jnp.repeat(grid_one, 3, axis=0)
    dec_msg = perceptron((mesh_two[dec_from], targets), (weights[14], weights[15]), weights[16]).astype(jnp.bfloat16)
    dec_sum = lax.optimization_barrier(jnp.sum(dec_msg.astype(jnp.float32).reshape(G_DEV * DEVICES, 3, L), axis=1)).astype(jnp.bfloat16)
    return residual_add(grid_one, perceptron((grid_one, dec_sum), (weights[17], weights[18]), weights[19]))
```

```python
import functools

import jax
import jax.numpy as jnp
from jax import lax
from jax.experimental import pallas as pl
from jax.experimental.pallas import tpu as pltpu
from jax.sharding import PartitionSpec as P

AXES = ("band", "patch")
EPSILON = 1e-05
BF = jnp.bfloat16
F32 = jnp.float32
I32 = jnp.int32


def dot(a, b):
    return jnp.dot(a, b, preferred_element_type=F32)


def dot_rows(a, b):
    return lax.dot_general(a, b, (((0,), (0,)), ((), ())), preferred_element_type=F32)


def dot_lanes(a, b):
    return lax.dot_general(a, b, (((1,), (1,)), ((), ())), preferred_element_type=F32)


def iota(shape, axis):
    return lax.broadcasted_iota(I32, shape, axis)


def flag(condition):
    return jnp.where(condition, 1.0, 0.0).astype(BF)


def column(row):
    count = row.shape[1]
    same = iota((count, count), 0) == iota((count, count), 1)
    return jnp.sum(jnp.where(same, row.astype(F32), 0.0), axis=1, keepdims=True).astype(I32)


def choose(row, count):
    edges = row.shape[1]
    return flag(iota((edges, count), 1) == column(row))


def choose_t(row, count):
    return flag(iota((count, row.shape[1]), 0) == row)


def silu(v):
    return 0.5 * v * (1.0 + jnp.tanh(0.5 * v))


def finish(summed, second):
    out = dot(silu(summed).astype(BF), second)
    centred = out - jnp.mean(out, axis=-1, keepdims=True)
    spread = jnp.mean(centred * centred, axis=-1, keepdims=True)
    return centred * lax.rsqrt(spread + EPSILON)


def residual(base, update):
    return (base.astype(F32) + update).astype(BF)


def spread_rows(chosen, values):
    high = values.astype(BF)
    low = (values - high.astype(F32)).astype(BF)
    return dot(jnp.concatenate([chosen, chosen], axis=1), jnp.concatenate([high, low], axis=0))


def wanted_rows(wanted, kind, cap):
    devices, lanes = wanted.shape
    total = devices * cap
    row = iota((total, 1), 0)
    owner = jnp.floor((row.astype(F32) + 0.5) * (1.0 / cap)).astype(I32)
    slot = row - owner * cap
    expand = flag(iota((total, devices), 1) == owner)
    values = dot(expand, wanted.astype(F32).astype(BF))
    own = jnp.where(iota((total, lanes), 1) == slot + kind * cap, values, 0.0).astype(BF)
    index = dot(own, jnp.ones((lanes, lanes), BF))
    return flag(iota((total, lanes), 1).astype(F32) == index)


def ask_kernel(cap, devices, dev0, row0, dev1, row1, dev2, row2, request, slots):
    edges = dev0.shape[1]
    earlier = flag(iota((edges, edges), 0) < iota((edges, edges), 1))
    total = jnp.zeros(request.shape, F32)
    for kind, (dev, row) in enumerate(((dev0, row0), (dev1, row1), (dev2, row2))):
        source = dev[...]
        hit = iota((devices, edges), 0) == source
        hits = flag(hit)
        before = dot(hits, earlier)
        place = jnp.sum(jnp.where(hit, before, 0.0), axis=0, keepdims=True).astype(I32)
        mine = iota((request.shape[1], edges), 0) == place + kind * cap
        total = total + dot_lanes(hits, jnp.where(mine, row[...].astype(F32), 0.0).astype(BF))
        slots[kind : kind + 1, :] = source * cap + place
    request[...] = total.astype(I32)


def first_kernel(cap, devices, grid, mesh, w1, w3, w6, w7, slots, enc_dst, grid_one, target, base, pick):
    grid_one[...] = residual(grid[...], finish(dot(grid[...], w6[...]), w7[...]))
    target[...] = spread_rows(choose(enc_dst[...], mesh.shape[0]), dot(mesh[...], w1[...]))
    base[...] = dot(mesh[...], w3[...])
    pick[...] = choose(slots[0:1, :], devices * cap)


def serve_kernel(cap, wanted, table, out):
    out[...] = dot(wanted_rows(wanted[...], 0, cap), table[...]).astype(BF)


def plan_kernel(cap, devices, wanted, slots, hot1, hot2, pick1, pick2):
    hot1[...] = wanted_rows(wanted[...], 1, cap)
    hot2[...] = wanted_rows(wanted[...], 2, cap)
    pick1[...] = choose(slots[1:2, :], devices * cap)
    pick2[...] = choose(slots[2:3, :], devices * cap)


def enc_kernel(received, pick, target, base, mesh, dst, hot, w0, w2, w4, w5, mesh_one, out):
    source = dot(pick[...], received[...]).astype(BF)
    message = finish(dot(source, w0[...]) + target[...], w2[...]).astype(BF)
    summed = dot(choose_t(dst[...], mesh.shape[0]), message).astype(BF)
    update = finish(base[...] + dot(summed, w4[...]), w5[...])
    one = residual(mesh[...], update)
    mesh_one[...] = one
    out[...] = dot(hot[...], one).astype(BF)


def local_kernel(mesh_one, w8, w9, w10, w11, loc_src, loc_dst, proc_dst, target, base, partial):
    one = mesh_one[...]
    count = one.shape[0]
    ends = dot(one, w9[...])
    target[...] = spread_rows(choose(proc_dst[...], count), ends)
    base[...] = dot(one, w11[...])
    start = spread_rows(choose(loc_src[...], count), dot(one, w8[...]))
    both = start + spread_rows(choose(loc_dst[...], count), ends)
    message = finish(both, w10[...]).astype(BF)
    partial[...] = dot(choose_t(loc_dst[...], count), message)


def proc_kernel(received, pick, target, base, partial, mesh_one, dst, hot, w8, w10, w12, w13, out):
    source = dot(pick[...], received[...]).astype(BF)
    message = finish(dot(source, w8[...]) + target[...], w10[...]).astype(BF)
    summed = (partial[...] + dot(choose_t(dst[...], mesh_one.shape[0]), message)).astype(BF)
    update = finish(base[...] + dot(summed, w12[...]), w13[...])
    two = residual(mesh_one[...], update)
    out[...] = dot(hot[...], two).astype(BF)


def last_kernel(grid_one, w15, w17, target, base):
    one = grid_one[...]
    rows = target.shape[0]
    near = iota((rows, one.shape[0]), 0) - 3 * iota((rows, one.shape[0]), 1)
    target[...] = spread_rows(flag((near >= 0) & (near < 3)), dot(one, w15[...]))
    base[...] = dot(one, w17[...])


def dec_kernel(received, pick, target, base, grid_one, w14, w16, w18, w19, out):
    source = dot(pick[...], received[...]).astype(BF)
    message = finish(dot(source, w14[...]) + target[...], w16[...]).astype(BF)
    shape = (grid_one.shape[0], target.shape[0])
    near = iota(shape, 1) - 3 * iota(shape, 0)
    summed = dot(flag((near >= 0) & (near < 3)), message).astype(BF)
    update = finish(base[...] + dot(summed, w18[...]), w19[...])
    out[...] = residual(grid_one[...], update)


def run(kernel, outs, *args, macs=0):
    spec = pl.BlockSpec(memory_space=pltpu.VMEM)
    moved = sum(a.size * a.dtype.itemsize for a in list(args) + list(outs))
    result = pl.pallas_call(
        kernel,
        out_shape=tuple(outs),
        in_specs=[spec] * len(args),
        out_specs=tuple(spec for _ in outs),
        compiler_params=pltpu.CompilerParams(vmem_limit_bytes=32 * 2**20),
        cost_estimate=pl.CostEstimate(flops=2 * macs, bytes_accessed=moved, transcendentals=0),
    )(*args)
    return result


def exchange(rows, cap):
    total, width = rows.shape
    parts = rows.reshape(total // cap, cap * width // 128, 128)
    moved = lax.all_to_all(parts, AXES, split_axis=0, concat_axis=0, tiled=True)
    return moved.reshape(total, width)


def body(
    grid_latent,
    mesh_latent,
    weights,
    enc_dev,
    enc_row,
    enc_dst,
    proc_dev,
    proc_row,
    proc_dst,
    loc_src,
    loc_dst,
    dec_dev,
    dec_row,
):
    devices = lax.axis_size("band") * lax.axis_size("patch")
    edges = enc_dev.shape[0]
    cap = max(2, 2 * edges // devices)
    count, width = mesh_latent.shape
    w = [weights[k] for k in range(weights.shape[0])]

    def line(values):
        return values.reshape(1, values.size)

    def arr(shape, dtype):
        return jax.ShapeDtypeStruct(shape, dtype)

    lanes = 128
    total = devices * cap
    request, slots = run(
        functools.partial(ask_kernel, cap, devices),
        (arr((devices, lanes), I32), arr((8, edges), I32)),
        line(enc_dev), line(enc_row), line(proc_dev), line(proc_row), line(dec_dev), line(dec_row),
        macs=3 * devices * edges * (edges + lanes),
    )
    asked = request.reshape(devices, 1, lanes)
    wanted = lax.all_to_all(asked, AXES, split_axis=0, concat_axis=0, tiled=True).reshape(devices, lanes)
    grid_one, enc_target, enc_base, enc_pick = run(
        functools.partial(first_kernel, cap, devices),
        (arr(grid_latent.shape, BF), arr((edges, width), F32), arr((count, width), F32), arr((edges, total), BF)),
        grid_latent, mesh_latent, w[1], w[3], w[6], w[7], slots, line(enc_dst),
        macs=7 * count * width * width,
    )
    (served,) = run(
        functools.partial(serve_kernel, cap),
        (arr((total, width), BF),),
        wanted, grid_latent,
        macs=total * count * (width + 2 * count),
    )
    enc_rows = exchange(served, cap)
    hot1, hot2, proc_pick, dec_pick = run(
        functools.partial(plan_kernel, cap, devices),
        (arr((total, count), BF), arr((total, count), BF), arr((edges, total), BF), arr((edges, total), BF)),
        wanted, slots,
        macs=4 * total * count * count,
    )
    mesh_one, served = run(
        enc_kernel,
        (arr(mesh_latent.shape, BF), arr((total, width), BF)),
        enc_rows, enc_pick, enc_target, enc_base, mesh_latent, line(enc_dst), hot1, w[0], w[2], w[4], w[5],
        macs=edges * width * (total + 3 * width),
    )
    proc_rows = exchange(served, cap)
    proc_target, proc_base, partial = run(
        local_kernel,
        (arr((edges, width), F32), arr((count, width), F32), arr((count, width), F32)),
        mesh_one, w[8], w[9], w[10], w[11], line(loc_src), line(loc_dst), line(proc_dst),
        macs=7 * count * width * width,
    )
    (served,) = run(
        proc_kernel,
        (arr((total, width), BF),),
        proc_rows, proc_pick, proc_target, proc_base, partial, mesh_one, line(proc_dst), hot2, w[8], w[10], w[12], w[13],
        macs=edges * width * (total + 3 * width),
    )
    dec_rows = exchange(served, cap)
    dec_target, dec_base = run(
        last_kernel,
        (arr((edges, width), F32), arr((count, width), F32)),
        grid_one, w[15], w[17],
        macs=4 * count * width * width,
    )
    (decoded,) = run(
        dec_kernel,
        (arr(grid_latent.shape, BF),),
        dec_rows, dec_pick, dec_target, dec_base, grid_one, w[14], w[16], w[18], w[19],
        macs=edges * width * (total + 3 * width),
    )
    return decoded


def solution(mesh):
    rows = P(AXES, None)
    edge = P(AXES)
    in_specs = (rows, rows, P(), rows, edge, edge, rows, edge, edge, edge, edge, rows, edge)
    return jax.shard_map(body, mesh=mesh, in_specs=in_specs, out_specs=rows, check_vma=False)
```

```python
import functools

import jax
import jax.numpy as jnp
from jax import lax
from jax.experimental import pallas as pl
from jax.experimental.pallas import tpu as pltpu
from jax.sharding import PartitionSpec as P

AXES = ("band", "patch")
EPSILON = 1e-05
BF = jnp.bfloat16
F32 = jnp.float32
I32 = jnp.int32


def dot(a, b):
    return jnp.dot(a, b, preferred_element_type=F32)


def dot_rows(a, b):
    return lax.dot_general(a, b, (((0,), (0,)), ((), ())), preferred_element_type=F32)


def dot_lanes(a, b):
    return lax.dot_general(a, b, (((1,), (1,)), ((), ())), preferred_element_type=F32)


def iota(shape, axis):
    return lax.broadcasted_iota(I32, shape, axis)


def flag(condition):
    return jnp.where(condition, 1.0, 0.0).astype(BF)


def column(row):
    count = row.shape[1]
    same = iota((count, count), 0) == iota((count, count), 1)
    return jnp.sum(jnp.where(same, row.astype(F32), 0.0), axis=1, keepdims=True).astype(I32)


def choose(row, count):
    edges = row.shape[1]
    return flag(iota((edges, count), 1) == column(row))


def choose_t(row, count):
    return flag(iota((count, row.shape[1]), 0) == row)


def silu(v):
    return 0.5 * v * (1.0 + jnp.tanh(0.5 * v))


def finish(summed, second):
    out = dot(silu(summed).astype(BF), second)
    centred = out - jnp.mean(out, axis=-1, keepdims=True)
    spread = jnp.mean(centred * centred, axis=-1, keepdims=True)
    return centred * lax.rsqrt(spread + EPSILON)


def residual(base, update):
    return (base.astype(F32) + update).astype(BF)


def spread_rows(chosen, values):
    high = values.astype(BF)
    low = (values - high.astype(F32)).astype(BF)
    return dot(jnp.concatenate([chosen, chosen], axis=1), jnp.concatenate([high, low], axis=0))


def wanted_rows(wanted, kind, cap):
    devices, lanes = wanted.shape
    total = devices * cap
    row = iota((total, 1), 0)
    owner = jnp.floor((row.astype(F32) + 0.5) * (1.0 / cap)).astype(I32)
    slot = row - owner * cap
    expand = flag(iota((total, devices), 1) == owner)
    values = dot(expand, wanted.astype(F32).astype(BF))
    own = jnp.where(iota((total, lanes), 1) == slot + kind * cap, values, 0.0).astype(BF)
    index = dot(own, jnp.ones((lanes, lanes), BF))
    return flag(iota((total, lanes), 1).astype(F32) == index)


def start(sems, *pairs):
    copies = [pltpu.make_async_copy(src, dst, sems.at[n]) for n, (src, dst) in enumerate(pairs)]
    for copy in copies:
        copy.start()
    return copies


def ask_kernel(cap, devices, dev0, dev1, dev2, row0, row1, row2, request, slots, *scratch):
    lines, sems = scratch[:6], scratch[6]
    copies = start(sems, *zip((dev0, dev1, dev2, row0, row1, row2), lines))
    edges = row0.shape[0]
    earlier = flag(iota((edges, edges), 0) < iota((edges, edges), 1))
    for copy in copies:
        copy.wait()
    total = jnp.zeros(request.shape, F32)
    for kind in range(3):
        source = lines[kind][...]
        row = lines[3 + kind][...].reshape(1, edges)
        hit = iota((devices, edges), 0) == source
        hits = flag(hit)
        before = dot(hits, earlier)
        place = jnp.sum(jnp.where(hit, before, 0.0), axis=0, keepdims=True).astype(I32)
        mine = iota((request.shape[1], edges), 0) == place + kind * cap
        total = total + dot_lanes(hits, jnp.where(mine, row.astype(F32), 0.0).astype(BF))
        slots[kind : kind + 1, :] = source * cap + place
    request[...] = total.astype(I32)


def first_kernel(cap, devices, slots, grid, mesh, enc_dst, w, grid_one, target, base, pick, g, m, d, w6, w7, w1, w3, sems):
    copies = start(sems, (grid, g), (w.at[6], w6), (w.at[7], w7), (mesh, m), (w.at[1], w1), (enc_dst, d), (w.at[3], w3))
    pick[...] = choose(slots[0:1, :], devices * cap)
    for copy in copies:
        copy.wait()
    grid_one[...] = residual(g[...], finish(dot(g[...], w6[...]), w7[...]))
    dst = d[...].reshape(1, d.shape[0])
    target[...] = spread_rows(choose(dst, m.shape[0]), dot(m[...], w1[...]))
    base[...] = dot(m[...], w3[...])


def serve_kernel(cap, wanted, table, out, held, sems):
    (copy,) = start(sems, (table, held))
    hot = wanted_rows(wanted[...], 0, cap)
    copy.wait()
    out[...] = dot(hot, held[...]).astype(BF)


def plan_kernel(cap, devices, wanted, slots, hot1, hot2, pick1, pick2):
    hot1[...] = wanted_rows(wanted[...], 1, cap)
    hot2[...] = wanted_rows(wanted[...], 2, cap)
    pick1[...] = choose(slots[1:2, :], devices * cap)
    pick2[...] = choose(slots[2:3, :], devices * cap)


def enc_kernel(received, pick, target, base, hot, mesh, dst, w, mesh_one, out, w0, w2, w4, w5, m, d, sems):
    copies = start(sems, (w.at[0], w0), (w.at[2], w2), (w.at[4], w4), (w.at[5], w5), (mesh, m), (dst, d))
    source = dot(pick[...], received[...]).astype(BF)
    copies[0].wait()
    summed = dot(source, w0[...]) + target[...]
    copies[1].wait()
    message = finish(summed, w2[...]).astype(BF)
    copies[5].wait()
    summed = dot(choose_t(d[...].reshape(1, d.shape[0]), m.shape[0]), message).astype(BF)
    copies[2].wait()
    summed = base[...] + dot(summed, w4[...])
    copies[3].wait()
    copies[4].wait()
    one = residual(m[...], finish(summed, w5[...]))
    mesh_one[...] = one
    out[...] = dot(hot[...], one).astype(BF)


def local_kernel(
    mesh_one, loc_src, loc_dst, proc_dst, w, target, base, partial, w9, w8, w10, w11, s, d, p, sems
):
    copies = start(
        sems, (w.at[9], w9), (w.at[8], w8), (w.at[10], w10), (w.at[11], w11), (loc_src, s), (loc_dst, d), (proc_dst, p)
    )
    for copy in copies:
        copy.wait()
    one = mesh_one[...]
    count = one.shape[0]
    local = s.shape[0]
    ends = dot(one, w9[...])
    target[...] = spread_rows(choose(p[...].reshape(1, p.shape[0]), count), ends)
    base[...] = dot(one, w11[...])
    begin = spread_rows(choose(s[...].reshape(1, local), count), dot(one, w8[...]))
    stop = d[...].reshape(1, local)
    message = finish(begin + spread_rows(choose(stop, count), ends), w10[...]).astype(BF)
    partial[...] = dot(choose_t(stop, count), message)


def proc_kernel(
    received, pick, target, base, partial, mesh_one, hot, dst, w, out, w8, w10, w12, w13, d, sems
):
    copies = start(sems, (w.at[8], w8), (w.at[10], w10), (w.at[12], w12), (w.at[13], w13), (dst, d))
    source = dot(pick[...], received[...]).astype(BF)
    copies[0].wait()
    summed = dot(source, w8[...]) + target[...]
    copies[1].wait()
    message = finish(summed, w10[...]).astype(BF)
    copies[4].wait()
    summed = dot(choose_t(d[...].reshape(1, d.shape[0]), mesh_one.shape[0]), message)
    copies[2].wait()
    summed = base[...] + dot((partial[...] + summed).astype(BF), w12[...])
    copies[3].wait()
    two = residual(mesh_one[...], finish(summed, w13[...]))
    out[...] = dot(hot[...], two).astype(BF)


def last_kernel(grid_one, w, target, base, w15, w17, sems):
    copies = start(sems, (w.at[15], w15), (w.at[17], w17))
    one = grid_one[...]
    rows = target.shape[0]
    near = iota((rows, one.shape[0]), 0) - 3 * iota((rows, one.shape[0]), 1)
    copies[0].wait()
    target[...] = spread_rows(flag((near >= 0) & (near < 3)), dot(one, w15[...]))
    copies[1].wait()
    base[...] = dot(one, w17[...])


def dec_kernel(received, pick, target, base, grid_one, w, out, w14, w16, w18, w19, sems):
    copies = start(sems, (w.at[14], w14), (w.at[16], w16), (w.at[18], w18), (w.at[19], w19))
    source = dot(pick[...], received[...]).astype(BF)
    copies[0].wait()
    summed = dot(source, w14[...]) + target[...]
    copies[1].wait()
    message = finish(summed, w16[...]).astype(BF)
    shape = (grid_one.shape[0], target.shape[0])
    near = iota(shape, 1) - 3 * iota(shape, 0)
    summed = dot(flag((near >= 0) & (near < 3)), message).astype(BF)
    copies[2].wait()
    summed = base[...] + dot(summed, w18[...])
    copies[3].wait()
    out[...] = residual(grid_one[...], finish(summed, w19[...]))


def run(kernel, outs, near, far=(), held=(), macs=0, grant=16):
    inside = pl.BlockSpec(memory_space=pltpu.VMEM)
    outside = pl.BlockSpec(memory_space=pltpu.HBM)
    moved = sum(a.size * a.dtype.itemsize for a in list(near) + list(held) + list(outs))
    scratch = [pltpu.VMEM(a.shape, a.dtype) for a in held]
    if held:
        scratch.append(pltpu.SemaphoreType.DMA((len(held),)))
    return pl.pallas_call(
        kernel,
        out_shape=tuple(outs),
        in_specs=[inside] * len(near) + [outside] * len(far),
        out_specs=tuple(inside for _ in outs),
        scratch_shapes=scratch,
        compiler_params=pltpu.CompilerParams(vmem_limit_bytes=grant * 2**20),
        cost_estimate=pl.CostEstimate(flops=2 * macs, bytes_accessed=moved, transcendentals=0),
    )(*near, *far)


def exchange(rows, cap):
    total, width = rows.shape
    parts = rows.reshape(total // cap, cap * width // 128, 128)
    moved = lax.all_to_all(parts, AXES, split_axis=0, concat_axis=0, tiled=True)
    return moved.reshape(total, width)


def body(
    grid_latent,
    mesh_latent,
    weights,
    enc_dev,
    enc_row,
    enc_dst,
    proc_dev,
    proc_row,
    proc_dst,
    loc_src,
    loc_dst,
    dec_dev,
    dec_row,
):
    devices = lax.axis_size("band") * lax.axis_size("patch")
    edges = enc_dev.shape[0]
    cap = max(2, 2 * edges // devices)
    count, width = mesh_latent.shape

    def arr(shape, dtype):
        return jax.ShapeDtypeStruct(shape, dtype)

    lanes = 128
    total = devices * cap
    line = arr((1, edges), I32)
    row = arr((edges,), I32)
    loc = arr(loc_src.shape, I32)
    mat = arr((width, width), BF)
    nodes = arr((count, width), BF)
    nodes32 = arr((count, width), F32)
    edges32 = arr((edges, width), F32)
    pick = arr((edges, total), BF)
    hot = arr((total, count), BF)
    rows = arr((total, width), BF)
    edge_macs = edges * width * (total + 3 * width)
    request, slots = run(
        functools.partial(ask_kernel, cap, devices),
        (arr((devices, lanes), I32), arr((8, edges), I32)),
        (),
        (enc_dev.reshape(1, edges), proc_dev.reshape(1, edges), dec_dev.reshape(1, edges), enc_row, proc_row, dec_row),
        (line, line, line, row, row, row),
        macs=3 * devices * edges * (edges + lanes),
    )
    asked = request.reshape(devices, 1, lanes)
    wanted = lax.all_to_all(asked, AXES, split_axis=0, concat_axis=0, tiled=True).reshape(devices, lanes)
    grid_one, enc_target, enc_base, enc_pick = run(
        functools.partial(first_kernel, cap, devices),
        (nodes, edges32, nodes32, pick),
        (slots,),
        (grid_latent, mesh_latent, enc_dst, weights),
        (nodes, nodes, row, mat, mat, mat, mat),
        macs=7 * count * width * width,
    )
    (served,) = run(
        functools.partial(serve_kernel, cap),
        (rows,),
        (wanted,),
        (grid_latent,),
        (nodes,),
        macs=total * count * (width + 2 * count),
    )
    enc_rows = exchange(served, cap)
    hot1, hot2, proc_pick, dec_pick = run(
        functools.partial(plan_kernel, cap, devices),
        (hot, hot, pick, pick),
        (wanted, slots),
        macs=4 * total * count * count,
    )
    mesh_one, served = run(
        enc_kernel,
        (nodes, rows),
        (enc_rows, enc_pick, enc_target, enc_base, hot1),
        (mesh_latent, enc_dst, weights),
        (mat, mat, mat, mat, nodes, row),
        macs=edge_macs,
    )
    proc_rows = exchange(served, cap)
    proc_target, proc_base, partial = run(
        local_kernel,
        (edges32, nodes32, nodes32),
        (mesh_one,),
        (loc_src, loc_dst, proc_dst, weights),
        (mat, mat, mat, mat, loc, loc, row),
        macs=7 * count * width * width,
    )
    (served,) = run(
        proc_kernel,
        (rows,),
        (proc_rows, proc_pick, proc_target, proc_base, partial, mesh_one, hot2),
        (proc_dst, weights),
        (mat, mat, mat, mat, row),
        macs=edge_macs,
    )
    dec_rows = exchange(served, cap)
    dec_target, dec_base = run(
        last_kernel,
        (edges32, nodes32),
        (grid_one,),
        (weights,),
        (mat, mat),
        macs=4 * count * width * width,
    )
    (decoded,) = run(
        dec_kernel,
        (nodes,),
        (dec_rows, dec_pick, dec_target, dec_base, grid_one),
        (weights,),
        (mat, mat, mat, mat),
        macs=edge_macs,
    )
    return decoded


def solution(mesh):
    rows = P(AXES, None)
    edge = P(AXES)
    in_specs = (rows, rows, P(), rows, edge, edge, rows, edge, edge, edge, edge, rows, edge)
    return jax.shard_map(body, mesh=mesh, in_specs=in_specs, out_specs=rows, check_vma=False)
```

```python
import functools

import jax
import jax.numpy as jnp
from jax import lax
from jax.experimental import pallas as pl
from jax.experimental.pallas import tpu as pltpu
from jax.sharding import PartitionSpec as P

AXES = ("band", "patch")
EPSILON = 1e-05
LANES = 128
PARTS = 4
BF = jnp.bfloat16
F32 = jnp.float32
I32 = jnp.int32


def dot(a, b):
    return jnp.dot(a, b, preferred_element_type=F32)


def dot_lanes(a, b):
    return lax.dot_general(a, b, (((1,), (1,)), ((), ())), preferred_element_type=F32)


def iota(shape, axis):
    return lax.broadcasted_iota(I32, shape, axis)


def flag(condition):
    return jnp.where(condition, 1.0, 0.0).astype(BF)


def column(row):
    count = row.shape[1]
    same = iota((count, count), 0) == iota((count, count), 1)
    return jnp.sum(jnp.where(same, row.astype(F32), 0.0), axis=1, keepdims=True).astype(I32)


def choose(row, count):
    return flag(iota((row.shape[1], count), 1) == column(row))


def choose_t(row, count):
    return flag(iota((count, row.shape[1]), 0) == row)


def line(ref):
    return ref[...].reshape(1, ref.shape[0])


def silu(v):
    return 0.5 * v * (1.0 + jnp.tanh(0.5 * v))


def finish(summed, second):
    out = dot(silu(summed).astype(BF), second)
    centred = out - jnp.mean(out, axis=-1, keepdims=True)
    spread = jnp.mean(centred * centred, axis=-1, keepdims=True)
    return centred * lax.rsqrt(spread + EPSILON)


def residual(base, update):
    return (base.astype(F32) + update).astype(BF)


def halves(values):
    high = values.astype(BF)
    return jnp.concatenate([high, (values - high.astype(F32)).astype(BF)], axis=0)


def twice(chosen):
    return jnp.concatenate([chosen, chosen], axis=1)


def start(sems, first, *pairs):
    copies = [pltpu.make_async_copy(src, dst, sems.at[first + n]) for n, (src, dst) in enumerate(pairs)]
    for copy in copies:
        copy.start()
    return copies


def wait(*copies):
    for copy in copies:
        copy.wait()


def part(ref, n):
    size = ref.shape[0] // PARTS
    return ref.at[pl.ds(n * size, size)]


def places(source, devices):
    edges = source.shape[1]
    earlier = flag(iota((edges, edges), 0) < iota((edges, edges), 1))
    hit = iota((devices, edges), 0) == source
    hits = flag(hit)
    return jnp.sum(jnp.where(hit, dot(hits, earlier), 0.0), axis=0, keepdims=True).astype(I32), hits


def serve(asked, kind, cap, table, wide, packed, out, sems, first):
    devices = asked.shape[0]
    blocks = table.shape[1] // LANES
    for slot in range(cap):
        lane = kind * cap + slot
        rows = dot(flag(asked[:, lane : lane + 1] == iota((devices, table.shape[0]), 1)), table)
        for block in range(blocks):
            target = pl.ds(slot * blocks + block, devices, stride=cap * blocks)
            wide[target, :] = rows[:, block * LANES : (block + 1) * LANES]
    copies = []
    size = wide.shape[0] // PARTS
    for n in range(PARTS):
        packed[pl.ds(n * size, size), :] = wide[pl.ds(n * size, size), :].astype(BF)
        copies += start(sems, first + n, (part(packed, n), part(out, n)))
    return copies


def take_in(cap, packed, wide, rows):
    blocks = rows.shape[1] // LANES
    devices = rows.shape[0] // cap
    size = wide.shape[0] // PARTS
    some = devices // PARTS
    for n in range(PARTS):
        wide[pl.ds(n * size, size), :] = packed[pl.ds(n * size, size), :].astype(F32)
        for slot in range(cap):
            for block in range(blocks):
                source = pl.ds(n * size + slot * blocks + block, some, stride=cap * blocks)
                target = pl.ds(slot * devices + n * some, some)
                rows[target, block * LANES : (block + 1) * LANES] = wide[source, :].astype(BF)


def ask_kernel(cap, devices, dev0, dev1, dev2, row0, row1, row2, request, *scratch):
    lines, sems = scratch[:6], scratch[6]
    copies = start(sems, 0, *zip((dev0, dev1, dev2, row0, row1, row2), lines))
    wait(*copies)
    total = jnp.zeros(request.shape, F32)
    for kind in range(3):
        place, hits = places(lines[kind][...], devices)
        row = line(lines[3 + kind]).astype(F32)
        mine = iota((request.shape[1], row.shape[1]), 0) == place + kind * cap
        total = total + dot_lanes(hits, jnp.where(mine, row, 0.0).astype(BF))
    request[...] = total.astype(I32)


def prepare_kernel(
    devices, grid, mesh, dev0, dev1, dev2, w, one, ends, base, dec_ends, dec_base, slots,
    g, m, d0, d1, d2, w6, w7, w1, w3, w15, w17, one_v, ends_v, base_v, dec_ends_v, dec_base_v, slots_v, sems,
):
    copies = start(
        sems, 0, (dev0, d0), (dev1, d1), (dev2, d2), (mesh, m), (w.at[1], w1), (w.at[3], w3), (grid, g),
        (w.at[6], w6), (w.at[7], w7), (w.at[15], w15), (w.at[17], w17),
    )
    wait(*copies[:3])
    for kind, dev in enumerate((d0, d1, d2)):
        source = dev[...]
        slots_v[kind : kind + 1, :] = places(source, devices)[0] * devices + source
    out = start(sems, 11, (slots_v, slots))
    wait(*copies[3:5])
    ends_v[...] = halves(dot(m[...], w1[...]))
    out += start(sems, 12, (ends_v, ends))
    wait(copies[5])
    base_v[...] = dot(m[...], w3[...])
    out += start(sems, 13, (base_v, base))
    wait(*copies[6:9])
    one_v[...] = residual(g[...], finish(dot(g[...], w6[...]), w7[...]))
    out += start(sems, 14, (one_v, one))
    wait(copies[9])
    dec_ends_v[...] = halves(dot(one_v[...], w15[...]))
    out += start(sems, 15, (dec_ends_v, dec_ends))
    wait(copies[10])
    dec_base_v[...] = dot(one_v[...], w17[...])
    out += start(sems, 16, (dec_base_v, dec_base))
    wait(*out)


def serve_kernel(cap, wanted, table, out, asked, held, wide, packed, sems):
    copies = start(sems, 0, (wanted, asked), (table, held))
    wait(*copies)
    wait(*serve(asked[...], 0, cap, held[...], wide, packed, out, sems, 2))


def enc_kernel(
    cap, received, wanted, slots, dst, ends, base, mesh, w, one, out,
    asked, slot, d, ends_v, base_v, m, w0, w2, w4, w5, one_v, wide, packed, rows, sems,
):
    small = start(sems, 0, (slots, slot), (dst, d))
    copies = start(
        sems, 2, (w.at[0], w0), (ends, ends_v), (w.at[2], w2), (base, base_v), (w.at[4], w4),
        (w.at[5], w5), (mesh, m), (wanted, asked),
    )
    wait(*small)
    pick = choose(slot[0:1, :], rows.shape[0])
    to = twice(choose(line(d), m.shape[0]))
    to_t = choose_t(line(d), m.shape[0])
    take_in(cap, received, wide, rows)
    source = dot(pick, rows[...]).astype(BF)
    wait(*copies[:2])
    summed = dot(source, w0[...]) + dot(to, ends_v[...])
    wait(copies[2])
    message = finish(summed, w2[...]).astype(BF)
    summed = dot(to_t, message).astype(BF)
    wait(*copies[3:5])
    summed = base_v[...] + dot(summed, w4[...])
    wait(*copies[5:])
    one_v[...] = residual(m[...], finish(summed, w5[...]))
    sent = start(sems, 10, (one_v, one))
    sent += serve(asked[...], 1, cap, one_v[...], wide, packed, out, sems, 11)
    wait(*sent)


def local_kernel(
    one, loc_src, loc_dst, w, ends, base, partial,
    one_v, w9, w8, w10, w11, s, d, ends_v, base_v, partial_v, sems,
):
    copies = start(
        sems, 0, (one, one_v), (w.at[9], w9), (loc_src, s), (loc_dst, d), (w.at[8], w8), (w.at[10], w10),
        (w.at[11], w11),
    )
    wait(*copies[:2])
    mine = one_v[...]
    count = mine.shape[0]
    ends_v[...] = halves(dot(mine, w9[...]))
    out = start(sems, 7, (ends_v, ends))
    wait(*copies[2:5])
    begin = dot(twice(choose(line(s), count)), halves(dot(mine, w8[...])))
    stop = line(d)
    wait(copies[5])
    message = finish(begin + dot(twice(choose(stop, count)), ends_v[...]), w10[...]).astype(BF)
    partial_v[...] = dot(choose_t(stop, count), message)
    out += start(sems, 8, (partial_v, partial))
    wait(copies[6])
    base_v[...] = dot(mine, w11[...])
    out += start(sems, 9, (base_v, base))
    wait(*out)


def proc_kernel(
    cap, received, wanted, slots, dst, ends, base, partial, one, w, out,
    asked, slot, d, ends_v, base_v, partial_v, one_v, w8, w10, w12, w13, wide, packed, rows, sems,
):
    small = start(sems, 0, (slots, slot), (dst, d))
    copies = start(
        sems, 2, (w.at[8], w8), (ends, ends_v), (w.at[10], w10), (base, base_v), (w.at[12], w12),
        (partial, partial_v), (w.at[13], w13), (one, one_v), (wanted, asked),
    )
    wait(*small)
    pick = choose(slot[1:2, :], rows.shape[0])
    count = one_v.shape[0]
    to = twice(choose(line(d), count))
    to_t = choose_t(line(d), count)
    take_in(cap, received, wide, rows)
    source = dot(pick, rows[...]).astype(BF)
    wait(*copies[:2])
    summed = dot(source, w8[...]) + dot(to, ends_v[...])
    wait(copies[2])
    message = finish(summed, w10[...]).astype(BF)
    summed = dot(to_t, message)
    wait(*copies[3:6])
    summed = base_v[...] + dot((partial_v[...] + summed).astype(BF), w12[...])
    wait(*copies[6:])
    two = residual(one_v[...], finish(summed, w13[...]))
    wait(*serve(asked[...], 2, cap, two, wide, packed, out, sems, 11))


def dec_kernel(
    cap, received, slots, ends, base, one, w, out,
    slot, ends_v, base_v, one_v, w14, w16, w18, w19, wide, rows, sems,
):
    small = start(sems, 0, (slots, slot))
    copies = start(
        sems, 1, (w.at[14], w14), (ends, ends_v), (w.at[16], w16), (base, base_v), (w.at[18], w18),
        (w.at[19], w19), (one, one_v),
    )
    wait(*small)
    edges = slot.shape[1]
    count = one_v.shape[0]
    pick = choose(slot[2:3, :], rows.shape[0])
    near = iota((edges, count), 0) - 3 * iota((edges, count), 1)
    to = twice(flag((near >= 0) & (near < 3)))
    near = iota((count, edges), 1) - 3 * iota((count, edges), 0)
    to_t = flag((near >= 0) & (near < 3))
    take_in(cap, received, wide, rows)
    source = dot(pick, rows[...]).astype(BF)
    wait(*copies[:2])
    summed = dot(source, w14[...]) + dot(to, ends_v[...])
    wait(copies[2])
    message = finish(summed, w16[...]).astype(BF)
    summed = dot(to_t, message).astype(BF)
    wait(*copies[3:5])
    summed = base_v[...] + dot(summed, w18[...])
    wait(*copies[5:])
    out[...] = residual(one_v[...], finish(summed, w19[...]))


def run(kernel, outs, far, held, copies, macs=0, near_out=0, near=()):
    inside = pl.BlockSpec(memory_space=pltpu.VMEM)
    outside = pl.BlockSpec(memory_space=pltpu.HBM)
    moved = sum(a.size * a.dtype.itemsize for a in list(held) + list(outs))
    kept = len(outs) - near_out
    return pl.pallas_call(
        kernel,
        out_shape=tuple(
            pltpu.HBM(a.shape, a.dtype) if n < kept else a for n, a in enumerate(outs)
        ),
        in_specs=[inside] * len(near) + [outside] * len(far),
        out_specs=tuple(outside if n < kept else inside for n in range(len(outs))),
        scratch_shapes=[pltpu.VMEM(a.shape, a.dtype) for a in held] + [pltpu.SemaphoreType.DMA((copies,))],
        compiler_params=pltpu.CompilerParams(vmem_limit_bytes=24 * 2**20),
        cost_estimate=pl.CostEstimate(flops=2 * macs, bytes_accessed=moved, transcendentals=0),
    )(*near, *(pltpu.with_memory_space_constraint(a, pltpu.HBM) for a in far))


def exchange(rows, devices):
    parts = rows.reshape(devices, rows.shape[0] // devices, LANES)
    moved = lax.all_to_all(parts, AXES, split_axis=0, concat_axis=0, tiled=True)
    return moved.reshape(rows.shape)


def body(
    grid_latent,
    mesh_latent,
    weights,
    enc_dev,
    enc_row,
    enc_dst,
    proc_dev,
    proc_row,
    proc_dst,
    loc_src,
    loc_dst,
    dec_dev,
    dec_row,
):
    devices = lax.axis_size("band") * lax.axis_size("patch")
    edges = enc_dev.shape[0]
    cap = max(2, 2 * edges // devices)
    count, width = mesh_latent.shape
    total = devices * cap

    def arr(shape, dtype):
        return jax.ShapeDtypeStruct(shape, dtype)

    across = arr((1, edges), I32)
    row = arr((edges,), I32)
    loc = arr(loc_src.shape, I32)
    mat = arr((width, width), BF)
    nodes = arr((count, width), BF)
    nodes2 = arr((2 * count, width), BF)
    nodes32 = arr((count, width), F32)
    slot = arr((8, edges), I32)
    ask = arr((devices, LANES), I32)
    flat = arr((total * width // LANES, LANES), BF)
    flat32 = arr(flat.shape, F32)
    rows = arr((total, width), BF)
    edge_macs = edges * width * (total + 3 * width)
    devs = tuple(a.reshape(1, edges) for a in (enc_dev, proc_dev, dec_dev))
    (request,) = run(
        functools.partial(ask_kernel, cap, devices),
        (ask,),
        (*devs, enc_row, proc_row, dec_row),
        (across, across, across, row, row, row),
        6,
        macs=3 * devices * edges * (edges + LANES),
        near_out=1,
    )
    asked = request.reshape(devices, 1, LANES)
    wanted = lax.all_to_all(asked, AXES, split_axis=0, concat_axis=0, tiled=True).reshape(devices, LANES)
    grid_one, enc_ends, enc_base, dec_ends, dec_base, slots = run(
        functools.partial(prepare_kernel, devices),
        (nodes, nodes2, nodes32, nodes2, nodes32, slot),
        (grid_latent, mesh_latent, *devs, weights),
        (nodes, nodes, across, across, across) + (mat,) * 6 + (nodes, nodes2, nodes32, nodes2, nodes32, slot),
        17,
        macs=6 * count * width * width + 3 * devices * edges * edges,
    )
    (sent,) = run(
        functools.partial(serve_kernel, cap),
        (flat,),
        (wanted, grid_latent),
        (ask, nodes, flat32, flat),
        2 + PARTS,
        macs=total * count * width,
    )
    enc_rows = exchange(sent, devices)
    mesh_one, sent = run(
        functools.partial(enc_kernel, cap),
        (nodes, flat),
        (wanted, slots, enc_dst, enc_ends, enc_base, mesh_latent, weights),
        (ask, slot, row, nodes2, nodes32, nodes, mat, mat, mat, mat, nodes, flat32, flat, rows),
        11 + PARTS,
        macs=edge_macs,
        near=(enc_rows,),
    )
    proc_rows = exchange(sent, devices)
    proc_ends, proc_base, partial = run(
        local_kernel,
        (nodes2, nodes32, nodes32),
        (mesh_one, loc_src, loc_dst, weights),
        (nodes, mat, mat, mat, mat, loc, loc, nodes2, nodes32, nodes32),
        10,
        macs=7 * count * width * width,
    )
    (sent,) = run(
        functools.partial(proc_kernel, cap),
        (flat,),
        (wanted, slots, proc_dst, proc_ends, proc_base, partial, mesh_one, weights),
        (ask, slot, row, nodes2, nodes32, nodes32, nodes, mat, mat, mat, mat, flat32, flat, rows),
        11 + PARTS,
        macs=edge_macs,
        near=(proc_rows,),
    )
    dec_rows = exchange(sent, devices)
    (decoded,) = run(
        functools.partial(dec_kernel, cap),
        (nodes,),
        (slots, dec_ends, dec_base, grid_one, weights),
        (slot, nodes2, nodes32, nodes, mat, mat, mat, mat, flat32, rows),
        8,
        macs=edge_macs,
        near=(dec_rows,),
        near_out=1,
    )
    return decoded


def solution(mesh):
    rows = P(AXES, None)
    edge = P(AXES)
    in_specs = (rows, rows, P(), rows, edge, edge, rows, edge, edge, edge, edge, rows, edge)
    return jax.shard_map(body, mesh=mesh, in_specs=in_specs, out_specs=rows, check_vma=False)
```

```python
import functools

import jax
import jax.numpy as jnp
from jax import lax
from jax.experimental import pallas as pl
from jax.experimental.pallas import tpu as pltpu
from jax.sharding import PartitionSpec as P

AXES = ("band", "patch")
EPSILON = 1e-05
LANES = 128
BF = jnp.bfloat16
F32 = jnp.float32
I32 = jnp.int32


def dot(a, b):
    return jnp.dot(a, b, preferred_element_type=F32)


def dot_lanes(a, b):
    return lax.dot_general(a, b, (((1,), (1,)), ((), ())), preferred_element_type=F32)


def iota(shape, axis):
    return lax.broadcasted_iota(I32, shape, axis)


def flag(condition):
    return jnp.where(condition, 1.0, 0.0).astype(BF)


def column(row):
    count = row.shape[1]
    same = iota((count, count), 0) == iota((count, count), 1)
    return jnp.sum(jnp.where(same, row.astype(F32), 0.0), axis=1, keepdims=True).astype(I32)


def choose(row, count):
    return flag(iota((row.shape[1], count), 1) == column(row))


def choose_t(row, count):
    return flag(iota((count, row.shape[1]), 0) == row)


def line(ref):
    return ref[...].reshape(1, ref.shape[0])


def silu(v):
    return 0.5 * v * (1.0 + jnp.tanh(0.5 * v))


def finish(summed, second):
    out = dot(silu(summed).astype(BF), second)
    centred = out - jnp.mean(out, axis=-1, keepdims=True)
    spread = jnp.mean(centred * centred, axis=-1, keepdims=True)
    return centred * lax.rsqrt(spread + EPSILON)


def residual(base, update):
    return (base.astype(F32) + update).astype(BF)


def halves(values):
    high = values.astype(BF)
    return jnp.concatenate([high, (values - high.astype(F32)).astype(BF)], axis=0)


def twice(chosen):
    return jnp.concatenate([chosen, chosen], axis=1)


def start(sems, first, *pairs):
    copies = [pltpu.make_async_copy(src, dst, sems.at[first + n]) for n, (src, dst) in enumerate(pairs)]
    for copy in copies:
        copy.start()
    return copies


def wait(*copies):
    for copy in copies:
        copy.wait()


def places(source, devices):
    edges = source.shape[1]
    earlier = flag(iota((edges, edges), 0) < iota((edges, edges), 1))
    hit = iota((devices, edges), 0) == source
    hits = flag(hit)
    return jnp.sum(jnp.where(hit, dot(hits, earlier), 0.0), axis=0, keepdims=True).astype(I32), hits


def fence(ref):
    def step(n, carry):
        ref[pl.ds(pl.multiple_of(n * 8, 8), 8), :] = jnp.zeros((8, ref.shape[1]), ref.dtype)
        return carry

    lax.fori_loop(0, 2, step, 0)


def serve(asked, kind, cap, table, wide, packed, out, sem):
    devices = asked.shape[0]
    blocks = table.shape[1] // LANES
    lanes = iota((devices, table.shape[0]), 1)
    for slot in range(cap):
        lane = kind * cap + slot
        got = dot(flag(asked[:, lane : lane + 1] == lanes), table)
        for block in range(blocks):
            target = pl.ds(slot * blocks + block, devices, stride=cap * blocks)
            wide[target, :] = got[:, block * LANES : (block + 1) * LANES]
    packed[...] = wide[...].astype(BF)
    copy = pltpu.make_async_copy(packed, out, sem)
    copy.start()
    return copy


def take_in(cap, packed, wide, rows):
    blocks = rows.shape[1] // LANES
    devices = rows.shape[0] // cap
    wide[...] = packed[...].astype(F32)
    for slot in range(cap):
        for block in range(blocks):
            source = pl.ds(slot * blocks + block, devices, stride=cap * blocks)
            target = pl.ds(slot * devices, devices)
            rows[target, block * LANES : (block + 1) * LANES] = wide[source, :].astype(BF)


def whole(kept, first, count):
    return kept[first : first + count, :].astype(F32) + kept[first + count : first + 2 * count, :].astype(F32)


def ask_kernel(cap, devices, dev0, dev1, dev2, row0, row1, row2, grid, request, g, *scratch):
    lines, sems = scratch[:6], scratch[6]
    copies = start(sems, 0, *zip((dev0, dev1, dev2, row0, row1, row2), lines), (grid, g))
    wait(*copies[:6])
    total = jnp.zeros(request.shape, F32)
    for kind in range(3):
        place, hits = places(lines[kind][...], devices)
        row = line(lines[3 + kind]).astype(F32)
        mine = iota((request.shape[1], row.shape[1]), 0) == place + kind * cap
        total = total + dot_lanes(hits, jnp.where(mine, row, 0.0).astype(BF))
    request[...] = total.astype(I32)
    wait(copies[6])


def serve_kernel(cap, asked, table, out, wide, packed, sems):
    serve(asked[...], 0, cap, table[...], wide, packed, out, sems.at[0]).wait()


def prepare_kernel(
    devices, grid, mesh, dev0, dev1, dev2, dst0, dst1, w, lines, kept, ws, one,
    g, d0, d1, d2, e0, e1, w6, w7, w1, w3, one_v, sems,
):
    count = g.shape[0]
    m = kept.at[pl.ds(4 * count, count)]
    copies = start(
        sems, 0, (dev0, d0), (dev1, d1), (dev2, d2), (dst0, e0), (dst1, e1), (mesh, m), (w.at[1], w1),
        (w.at[3], w3), (grid, g), (w.at[6], w6), (w.at[7], w7), (w.at[0], ws.at[0]), (w.at[2], ws.at[1]),
    )
    wait(*copies[:5])
    for kind, dev in enumerate((d0, d1, d2)):
        source = dev[...]
        lines[kind : kind + 1, :] = places(source, devices)[0] * devices + source
    lines[3:4, :] = line(e0)
    lines[4:5, :] = line(e1)
    wait(*copies[5:7])
    kept[: 2 * count, :] = halves(dot(m[...], w1[...]))
    wait(copies[7])
    kept[2 * count : 4 * count, :] = halves(dot(m[...], w3[...]))
    wait(*copies[8:11])
    one_v[...] = residual(g[...], finish(dot(g[...], w6[...]), w7[...]))
    wait(*copies[11:], *start(sems, len(copies), (one_v, one)))


def enc_kernel(cap, received, asked, lines, kept, ws, w, one, out, w4, w5, one_v, wide, packed, rows, sems):
    copies = start(sems, 0, (w.at[4], w4), (w.at[5], w5))
    fence(wide)
    count = one_v.shape[0]
    pick = choose(lines[0:1, :], rows.shape[0])
    to = twice(choose(lines[3:4, :], count))
    to_t = choose_t(lines[3:4, :], count)
    take_in(cap, received, wide, rows)
    source = dot(pick, rows[...]).astype(BF)
    summed = dot(source, ws[0]) + dot(to, kept[: 2 * count, :])
    message = finish(summed, ws[1]).astype(BF)
    summed = dot(to_t, message).astype(BF)
    wait(copies[0])
    summed = whole(kept, 2 * count, count) + dot(summed, w4[...])
    wait(copies[1])
    mine = residual(kept[4 * count :, :], finish(summed, w5[...]))
    one_v[...] = mine
    wait(*start(sems, 2, (one_v, one)), serve(asked[...], 1, cap, mine, wide, packed, out, sems.at[3]))


def local_kernel(one, loc_src, loc_dst, w, kept, ws, w9, w11, s, d, sems):
    count = one.shape[0]
    mine = kept.at[pl.ds(6 * count, count)]
    copies = start(
        sems, 0, (one, mine), (w.at[9], w9), (loc_src, s), (loc_dst, d), (w.at[8], ws.at[0]), (w.at[10], ws.at[1]),
        (w.at[11], w11),
    )
    wait(*copies[:2])
    kept[: 2 * count, :] = halves(dot(mine[...], w9[...]))
    wait(*copies[2:5])
    begin = dot(twice(choose(line(s), count)), halves(dot(mine[...], ws[0])))
    stop = line(d)
    wait(copies[5])
    message = finish(begin + dot(twice(choose(stop, count)), kept[: 2 * count, :]), ws[1]).astype(BF)
    kept[4 * count : 6 * count, :] = halves(dot(choose_t(stop, count), message))
    wait(copies[6])
    kept[2 * count : 4 * count, :] = halves(dot(mine[...], w11[...]))


def proc_kernel(cap, received, asked, lines, kept, ws, w, out, w12, w13, wide, packed, rows, sems):
    copies = start(sems, 0, (w.at[12], w12), (w.at[13], w13))
    fence(wide)
    count = kept.shape[0] // 7
    pick = choose(lines[1:2, :], rows.shape[0])
    to = twice(choose(lines[4:5, :], count))
    to_t = choose_t(lines[4:5, :], count)
    take_in(cap, received, wide, rows)
    source = dot(pick, rows[...]).astype(BF)
    summed = dot(source, ws[0]) + dot(to, kept[: 2 * count, :])
    message = finish(summed, ws[1]).astype(BF)
    summed = (whole(kept, 4 * count, count) + dot(to_t, message)).astype(BF)
    wait(copies[0])
    summed = whole(kept, 2 * count, count) + dot(summed, w12[...])
    wait(copies[1])
    two = residual(kept[6 * count :, :], finish(summed, w13[...]))
    serve(asked[...], 2, cap, two, wide, packed, out, sems.at[2]).wait()


def last_kernel(grid_one, w, kept, ws, w15, w17, sems):
    count = grid_one.shape[0]
    one = kept.at[pl.ds(4 * count, count)]
    copies = start(
        sems, 0, (grid_one, one), (w.at[15], w15), (w.at[17], w17), (w.at[14], ws.at[0]), (w.at[16], ws.at[1])
    )
    wait(*copies[:2])
    kept[: 2 * count, :] = halves(dot(one[...], w15[...]))
    wait(copies[2])
    kept[2 * count : 4 * count, :] = halves(dot(one[...], w17[...]))
    wait(*copies[3:])


def dec_kernel(cap, received, lines, kept, ws, w, out, w18, w19, wide, rows, sems):
    copies = start(sems, 0, (w.at[18], w18), (w.at[19], w19))
    fence(wide)
    edges = lines.shape[1]
    count = kept.shape[0] // 5
    pick = choose(lines[2:3, :], rows.shape[0])
    near = iota((edges, count), 0) - 3 * iota((edges, count), 1)
    to = twice(flag((near >= 0) & (near < 3)))
    near = iota((count, edges), 1) - 3 * iota((count, edges), 0)
    to_t = flag((near >= 0) & (near < 3))
    take_in(cap, received, wide, rows)
    source = dot(pick, rows[...]).astype(BF)
    summed = dot(source, ws[0]) + dot(to, kept[: 2 * count, :])
    message = finish(summed, ws[1]).astype(BF)
    summed = dot(to_t, message).astype(BF)
    wait(copies[0])
    summed = whole(kept, 2 * count, count) + dot(summed, w18[...])
    wait(copies[1])
    out[...] = residual(kept[4 * count :, :], finish(summed, w19[...]))


def run(kernel, outs=(), near=(), far=(), held=(), copies=0, macs=0, away=(), last=False):
    inside = pl.BlockSpec(memory_space=pltpu.VMEM)
    outside = pl.BlockSpec(memory_space=pltpu.HBM)
    moved = sum(a.size * a.dtype.itemsize for a in list(held) + list(outs))
    return pl.pallas_call(
        kernel,
        out_shape=(
            *(a if last else pltpu.VMEM(a.shape, a.dtype) for a in outs),
            *(pltpu.HBM(a.shape, a.dtype) for a in away),
        ),
        in_specs=[inside] * len(near) + [outside] * len(far),
        out_specs=(inside,) * len(outs) + (outside,) * len(away),
        scratch_shapes=[pltpu.VMEM(a.shape, a.dtype) for a in held] + [pltpu.SemaphoreType.DMA((copies,))],
        compiler_params=pltpu.CompilerParams(vmem_limit_bytes=16 * 2**20),
        cost_estimate=pl.CostEstimate(flops=2 * macs, bytes_accessed=moved, transcendentals=0),
    )(
        *(pltpu.with_memory_space_constraint(a, pltpu.VMEM) for a in near),
        *(pltpu.with_memory_space_constraint(a, pltpu.HBM) for a in far),
    )


def exchange(rows, devices):
    parts = rows.reshape(devices, rows.shape[0] // devices, LANES)
    moved = lax.all_to_all(parts, AXES, split_axis=0, concat_axis=0, tiled=True)
    return moved.reshape(rows.shape)


def body(
    grid_latent,
    mesh_latent,
    weights,
    enc_dev,
    enc_row,
    enc_dst,
    proc_dev,
    proc_row,
    proc_dst,
    loc_src,
    loc_dst,
    dec_dev,
    dec_row,
):
    devices = lax.axis_size("band") * lax.axis_size("patch")
    edges = enc_dev.shape[0]
    cap = max(2, 2 * edges // devices)
    count, width = mesh_latent.shape
    total = devices * cap

    def arr(shape, dtype):
        return jax.ShapeDtypeStruct(shape, dtype)

    across = arr((1, edges), I32)
    row = arr((edges,), I32)
    loc = arr(loc_src.shape, I32)
    mat = arr((width, width), BF)
    mats = arr((2, width, width), BF)
    nodes = arr((count, width), BF)
    lines = arr((8, edges), I32)
    ask = arr((devices, LANES), I32)
    flat = arr((total * width // LANES, LANES), BF)
    flat32 = arr(flat.shape, F32)
    rows = arr((total, width), BF)
    edge_macs = edges * width * (total + 3 * width)
    devs = tuple(a.reshape(1, edges) for a in (enc_dev, proc_dev, dec_dev))

    def kept(parts):
        return arr((parts * count, width), BF)

    request, grid = run(
        functools.partial(ask_kernel, cap, devices),
        (ask, nodes),
        far=(*devs, enc_row, proc_row, dec_row, grid_latent),
        held=(across, across, across, row, row, row),
        copies=7,
        macs=3 * devices * edges * (edges + LANES),
    )
    asked = request.reshape(devices, 1, LANES)
    wanted = lax.all_to_all(asked, AXES, split_axis=0, concat_axis=0, tiled=True).reshape(devices, LANES)
    (sent,) = run(
        functools.partial(serve_kernel, cap),
        near=(wanted, grid),
        held=(flat32, flat),
        copies=1,
        macs=total * count * width,
        away=(flat,),
    )
    enc_rows = exchange(sent, devices)
    places_of, enc_kept, enc_ws, grid_one = run(
        functools.partial(prepare_kernel, devices),
        (lines, kept(5), mats),
        far=(grid_latent, mesh_latent, *devs, enc_dst, proc_dst, weights),
        held=(nodes, across, across, across, row, row, mat, mat, mat, mat, nodes),
        copies=14,
        macs=6 * count * width * width + 3 * devices * edges * edges,
        away=(nodes,),
    )
    mesh_one, sent = run(
        functools.partial(enc_kernel, cap),
        near=(enc_rows, wanted, places_of, enc_kept, enc_ws),
        far=(weights,),
        held=(mat, mat, nodes, flat32, flat, rows),
        copies=4,
        macs=edge_macs,
        away=(nodes, flat),
    )
    proc_rows = exchange(sent, devices)
    proc_kept, proc_ws = run(
        local_kernel,
        (kept(7), mats),
        far=(mesh_one, loc_src, loc_dst, weights),
        held=(mat, mat, loc, loc),
        copies=7,
        macs=7 * count * width * width,
    )
    (sent,) = run(
        functools.partial(proc_kernel, cap),
        near=(proc_rows, wanted, places_of, proc_kept, proc_ws),
        far=(weights,),
        held=(mat, mat, flat32, flat, rows),
        copies=3,
        macs=edge_macs,
        away=(flat,),
    )
    dec_rows = exchange(sent, devices)
    dec_kept, dec_ws = run(
        last_kernel,
        (kept(5), mats),
        far=(grid_one, weights),
        held=(mat, mat),
        copies=5,
        macs=2 * count * width * width,
    )
    (decoded,) = run(
        functools.partial(dec_kernel, cap),
        (nodes,),
        near=(dec_rows, places_of, dec_kept, dec_ws),
        far=(weights,),
        held=(mat, mat, flat32, rows),
        copies=2,
        macs=edge_macs,
        last=True,
    )
    return decoded


def solution(mesh):
    rows = P(AXES, None)
    edge = P(AXES)
    in_specs = (rows, rows, P(), rows, edge, edge, rows, edge, edge, edge, edge, rows, edge)
    return jax.shard_map(body, mesh=mesh, in_specs=in_specs, out_specs=rows, check_vma=False)
```

```python
import functools

import jax
import jax.numpy as jnp
from jax import lax
from jax.experimental import pallas as pl
from jax.experimental.pallas import tpu as pltpu
from jax.sharding import PartitionSpec as P

AXES = ("band", "patch")
EPSILON = 1e-05
LANES = 128
BF = jnp.bfloat16
F32 = jnp.float32
I32 = jnp.int32


def dot(a, b):
    return jnp.dot(a, b, preferred_element_type=F32)


def dot_lanes(a, b):
    return lax.dot_general(a, b, (((1,), (1,)), ((), ())), preferred_element_type=F32)


def iota(shape, axis):
    return lax.broadcasted_iota(I32, shape, axis)


def flag(condition):
    return jnp.where(condition, 1.0, 0.0).astype(BF)


def column(row):
    count = row.shape[1]
    same = iota((count, count), 0) == iota((count, count), 1)
    return jnp.sum(jnp.where(same, row.astype(F32), 0.0), axis=1, keepdims=True).astype(I32)


def choose(row, count):
    return flag(iota((row.shape[1], count), 1) == column(row))


def choose_t(row, count):
    return flag(iota((count, row.shape[1]), 0) == row)


def line(ref):
    return ref[...].reshape(1, ref.shape[0])


def silu(v):
    return 0.5 * v * (1.0 + jnp.tanh(0.5 * v))


def finish(summed, second):
    out = dot(silu(summed).astype(BF), second)
    centred = out - jnp.mean(out, axis=-1, keepdims=True)
    spread = jnp.mean(centred * centred, axis=-1, keepdims=True)
    return centred * lax.rsqrt(spread + EPSILON)


def residual(base, update):
    return (base.astype(F32) + update).astype(BF)


def start(sems, first, *pairs):
    copies = [pltpu.make_async_copy(src, dst, sems.at[first + n]) for n, (src, dst) in enumerate(pairs)]
    for copy in copies:
        copy.start()
    return copies


def wait(*copies):
    for copy in copies:
        copy.wait()


def places(source, devices):
    edges = source.shape[1]
    earlier = flag(iota((edges, edges), 0) < iota((edges, edges), 1))
    hit = iota((devices, edges), 0) == source
    hits = flag(hit)
    return jnp.sum(jnp.where(hit, dot(hits, earlier), 0.0), axis=0, keepdims=True).astype(I32), hits


def fence(ref):
    def step(n, carry):
        ref[pl.ds(pl.multiple_of(n * 8, 8), 8), :] = jnp.zeros((8, ref.shape[1]), ref.dtype)
        return carry

    lax.fori_loop(0, 2, step, 0)


def serve(asked, kind, cap, table, wide, out):
    devices = asked.shape[0]
    blocks = table.shape[1] // LANES
    lanes = iota((devices, table.shape[0]), 1)
    hot = [flag(asked[:, lane : lane + 1] == lanes) for lane in range(kind * cap, kind * cap + cap)]
    got = dot(jnp.concatenate(hot, axis=0), table)
    for slot in range(cap):
        for block in range(blocks):
            target = pl.ds(slot * blocks + block, devices, stride=cap * blocks)
            wide[target, :] = got[slot * devices : (slot + 1) * devices, block * LANES : (block + 1) * LANES]
    out[...] = wide[...].astype(BF)


def take_in(cap, devices, packed, ends, wide, rows):
    blocks = rows.shape[1] // LANES
    rows[cap * devices :, :] = ends
    wide[...] = packed[...].astype(F32)
    for slot in range(cap):
        for block in range(blocks):
            source = pl.ds(slot * blocks + block, devices, stride=cap * blocks)
            target = pl.ds(slot * devices, devices)
            rows[target, block * LANES : (block + 1) * LANES] = wide[source, :].astype(BF)


def ask_kernel(
    cap, devices, dev0, dev1, dev2, row0, row1, row2, dst0, dst1, grid, mesh, w, request, lines, table, kept,
    d0, d1, d2, r0, r1, r2, e0, e1, g, w0, w1, w3, earlier, spare, sems,
):
    count = g.shape[0]
    m = kept.at[pl.ds(2 * count, count)]
    devs, rows = (d0, d1, d2), (r0, r1, r2)
    copies = start(sems, 0, *zip((dev0, dev1, dev2, row0, row1, row2), devs + rows))
    fence(spare)
    later = start(
        sems, 6, (grid, g), (w.at[0], w0), (mesh, m), (w.at[1], w1), (w.at[3], w3), (dst0, e0), (dst1, e1)
    )
    edges = lines.shape[1]
    earlier[...] = flag(iota((edges, edges), 0) < iota((edges, edges), 1))
    fence(spare)
    wait(*copies)
    hits = [iota((devices, edges), 0) == dev[...] for dev in devs]
    before = dot(flag(jnp.concatenate(hits, axis=0)), earlier[...])
    values = []
    for kind in range(3):
        mine = jnp.where(hits[kind], before[kind * devices : (kind + 1) * devices, :], 0.0)
        place = jnp.sum(mine, axis=0, keepdims=True).astype(I32)
        lines[kind : kind + 1, :] = place * devices + devs[kind][...]
        row = line(rows[kind]).astype(F32)
        values.append(jnp.where(iota((LANES, edges), 0) == place + kind * cap, row, 0.0).astype(BF))
    hits = flag(jnp.concatenate(hits, axis=1))
    request[...] = dot_lanes(hits, jnp.concatenate(values, axis=1)).astype(I32)
    wait(*later[:2])
    table[...] = dot(g[...], w0[...]).astype(BF)
    wait(*later[2:4])
    kept[:count, :] = dot(m[...], w1[...]).astype(BF)
    wait(*later[4:])
    kept[count : 2 * count, :] = dot(m[...], w3[...]).astype(BF)
    lines[3:4, :] = line(e0)
    lines[4:5, :] = line(e1)


def serve_kernel(cap, asked, table, out, wide):
    serve(asked[...], 0, cap, table[...], wide, out)


def enc_kernel(cap, received, asked, lines, kept, w, one, out, w2, w4, w5, w8, one_v, wide, packed, rows, sems):
    copies = start(sems, 0, (w.at[2], w2))
    fence(wide)
    copies += start(sems, 1, (w.at[4], w4), (w.at[5], w5), (w.at[8], w8))
    fence(wide)
    count = one_v.shape[0]
    devices = asked.shape[0]
    pick = choose(lines[0:1, :], cap * devices)
    to = choose(lines[3:4, :], count)
    to_t = choose_t(lines[3:4, :], count)
    take_in(cap, devices, received, kept[:count, :], wide, rows)
    summed = dot(jnp.concatenate([pick, to], axis=1), rows[...])
    wait(copies[0])
    message = finish(summed, w2[...]).astype(BF)
    summed = dot(to_t, message).astype(BF)
    wait(copies[1])
    summed = kept[count : 2 * count, :].astype(F32) + dot(summed, w4[...])
    wait(copies[2])
    mine = residual(kept[2 * count :, :], finish(summed, w5[...]))
    one_v[...] = mine
    wait(copies[3])
    serve(asked[...], 1, cap, dot(mine, w8[...]).astype(BF), wide, packed)
    wait(*start(sems, 4, (one_v, one), (packed, out)))


def beside_kernel(
    one, grid, loc_src, loc_dst, w, kept, w10, dec_kept, g, w9, w8, w11, w6, w7, w15, w17, s, d, sems
):
    count = one.shape[0]
    mine = kept.at[pl.ds(3 * count, count)]
    grid_one = dec_kept.at[pl.ds(2 * count, count)]
    copies = start(
        sems, 0, (one, mine), (w.at[9], w9), (loc_src, s), (loc_dst, d), (w.at[8], w8), (w.at[10], w10),
        (w.at[11], w11), (grid, g), (w.at[6], w6), (w.at[7], w7), (w.at[15], w15), (w.at[17], w17),
    )
    wait(*copies[:2])
    kept[:count, :] = dot(mine[...], w9[...]).astype(BF)
    wait(*copies[2:5])
    start_rows = dot(mine[...], w8[...]).astype(BF)
    stop = line(d)
    both = jnp.concatenate([choose(line(s), count), choose(stop, count)], axis=1)
    summed = dot(both, jnp.concatenate([start_rows, kept[:count, :]], axis=0))
    wait(copies[5])
    message = finish(summed, w10[...]).astype(BF)
    kept[2 * count : 3 * count, :] = dot(choose_t(stop, count), message).astype(BF)
    wait(copies[6])
    kept[count : 2 * count, :] = dot(mine[...], w11[...]).astype(BF)
    wait(*copies[7:10])
    grid_one[...] = residual(g[...], finish(dot(g[...], w6[...]), w7[...]))
    wait(copies[10])
    dec_kept[:count, :] = dot(grid_one[...], w15[...]).astype(BF)
    wait(copies[11])
    dec_kept[count : 2 * count, :] = dot(grid_one[...], w17[...]).astype(BF)


def proc_kernel(cap, received, asked, lines, kept, w10, w, out, w12, w13, w14, wide, rows, sems):
    copies = start(sems, 0, (w.at[12], w12), (w.at[13], w13), (w.at[14], w14))
    fence(wide)
    count = kept.shape[0] // 4
    devices = asked.shape[0]
    pick = choose(lines[1:2, :], cap * devices)
    to = choose(lines[4:5, :], count)
    to_t = choose_t(lines[4:5, :], count)
    take_in(cap, devices, received, kept[:count, :], wide, rows)
    summed = dot(jnp.concatenate([pick, to], axis=1), rows[...])
    message = finish(summed, w10[...]).astype(BF)
    summed = (kept[2 * count : 3 * count, :].astype(F32) + dot(to_t, message)).astype(BF)
    wait(copies[0])
    summed = kept[count : 2 * count, :].astype(F32) + dot(summed, w12[...])
    wait(copies[1])
    two = residual(kept[3 * count :, :], finish(summed, w13[...]))
    wait(copies[2])
    serve(asked[...], 2, cap, dot(two, w14[...]).astype(BF), wide, out)


def dec_kernel(cap, devices, received, lines, kept, w, out, w16, w18, w19, wide, rows, sems):
    copies = start(sems, 0, (w.at[16], w16))
    fence(wide)
    copies += start(sems, 1, (w.at[18], w18), (w.at[19], w19))
    fence(wide)
    edges = lines.shape[1]
    count = kept.shape[0] // 3
    pick = choose(lines[2:3, :], cap * devices)
    near = iota((edges, count), 0) - 3 * iota((edges, count), 1)
    to = flag((near >= 0) & (near < 3))
    near = iota((count, edges), 1) - 3 * iota((count, edges), 0)
    to_t = flag((near >= 0) & (near < 3))
    take_in(cap, devices, received, kept[:count, :], wide, rows)
    summed = dot(jnp.concatenate([pick, to], axis=1), rows[...])
    wait(copies[0])
    message = finish(summed, w16[...]).astype(BF)
    summed = dot(to_t, message).astype(BF)
    wait(copies[1])
    summed = kept[count : 2 * count, :].astype(F32) + dot(summed, w18[...])
    wait(copies[2])
    out[...] = residual(kept[2 * count :, :], finish(summed, w19[...]))


def run(kernel, outs=(), near=(), far=(), held=(), copies=0, macs=0, away=(), last=False):
    inside = pl.BlockSpec(memory_space=pltpu.VMEM)
    outside = pl.BlockSpec(memory_space=pltpu.HBM)
    moved = sum(a.size * a.dtype.itemsize for a in list(held) + list(outs))
    return pl.pallas_call(
        kernel,
        out_shape=(
            *(a if last else pltpu.VMEM(a.shape, a.dtype) for a in outs),
            *(pltpu.HBM(a.shape, a.dtype) for a in away),
        ),
        in_specs=[inside] * len(near) + [outside] * len(far),
        out_specs=(inside,) * len(outs) + (outside,) * len(away),
        scratch_shapes=[pltpu.VMEM(a.shape, a.dtype) for a in held]
        + ([pltpu.SemaphoreType.DMA((copies,))] if copies else []),
        compiler_params=pltpu.CompilerParams(vmem_limit_bytes=16 * 2**20),
        cost_estimate=pl.CostEstimate(flops=2 * macs, bytes_accessed=moved, transcendentals=0),
    )(
        *(pltpu.with_memory_space_constraint(a, pltpu.VMEM) for a in near),
        *(pltpu.with_memory_space_constraint(a, pltpu.HBM) for a in far),
    )


def exchange(rows, devices):
    parts = rows.reshape(devices, rows.shape[0] // devices, LANES)
    moved = lax.all_to_all(parts, AXES, split_axis=0, concat_axis=0, tiled=True)
    return moved.reshape(rows.shape)


def body(
    grid_latent,
    mesh_latent,
    weights,
    enc_dev,
    enc_row,
    enc_dst,
    proc_dev,
    proc_row,
    proc_dst,
    loc_src,
    loc_dst,
    dec_dev,
    dec_row,
):
    devices = lax.axis_size("band") * lax.axis_size("patch")
    edges = enc_dev.shape[0]
    cap = max(2, 2 * edges // devices)
    count, width = mesh_latent.shape
    total = devices * cap

    def arr(shape, dtype):
        return jax.ShapeDtypeStruct(shape, dtype)

    across = arr((1, edges), I32)
    row = arr((edges,), I32)
    loc = arr(loc_src.shape, I32)
    mat = arr((width, width), BF)
    square = arr((edges, edges), BF)
    spare = arr((16, LANES), F32)
    nodes = arr((count, width), BF)
    lines = arr((8, edges), I32)
    ask = arr((devices, LANES), I32)
    flat = arr((total * width // LANES, LANES), BF)
    flat32 = arr(flat.shape, F32)
    rows = arr((total + count, width), BF)
    edge_macs = edges * width * (total + 3 * width)
    devs = tuple(a.reshape(1, edges) for a in (enc_dev, proc_dev, dec_dev))

    def kept(parts):
        return arr((parts * count, width), BF)

    request, places_of, table, enc_kept = run(
        functools.partial(ask_kernel, cap, devices),
        (ask, lines, nodes, kept(3)),
        far=(*devs, enc_row, proc_row, dec_row, enc_dst, proc_dst, grid_latent, mesh_latent, weights),
        held=(across,) * 3 + (row,) * 5 + (nodes, mat, mat, mat, square, spare),
        copies=13,
        macs=3 * devices * edges * (edges + LANES) + 3 * count * width * width,
    )
    asked = request.reshape(devices, 1, LANES)
    wanted = lax.all_to_all(asked, AXES, split_axis=0, concat_axis=0, tiled=True).reshape(devices, LANES)
    (sent,) = run(
        functools.partial(serve_kernel, cap),
        (flat,),
        near=(wanted, table),
        held=(flat32,),
        macs=total * count * width,
    )
    enc_rows = exchange(sent, devices)
    mesh_one, sent = run(
        functools.partial(enc_kernel, cap),
        near=(enc_rows, wanted, places_of, enc_kept),
        far=(weights,),
        held=(mat, mat, mat, mat, nodes, flat32, flat, rows),
        copies=6,
        macs=edge_macs,
        away=(nodes, flat),
    )
    proc_rows = exchange(sent, devices)
    proc_kept, w10, dec_kept = run(
        beside_kernel,
        (kept(4), mat, kept(3)),
        far=(mesh_one, grid_latent, loc_src, loc_dst, weights),
        held=(nodes,) + (mat,) * 7 + (loc, loc),
        copies=12,
        macs=11 * count * width * width,
    )
    (sent,) = run(
        functools.partial(proc_kernel, cap),
        (flat,),
        near=(proc_rows, wanted, places_of, proc_kept, w10),
        far=(weights,),
        held=(mat, mat, mat, flat32, rows),
        copies=3,
        macs=edge_macs,
    )
    dec_rows = exchange(sent, devices)
    (decoded,) = run(
        functools.partial(dec_kernel, cap, devices),
        (nodes,),
        near=(dec_rows, places_of, dec_kept),
        far=(weights,),
        held=(mat, mat, mat, flat32, rows),
        copies=3,
        macs=edge_macs,
        last=True,
    )
    return decoded


def solution(mesh):
    rows = P(AXES, None)
    edge = P(AXES)
    in_specs = (rows, rows, P(), rows, edge, edge, rows, edge, edge, edge, edge, rows, edge)
    return jax.shard_map(body, mesh=mesh, in_specs=in_specs, out_specs=rows, check_vma=False)
```

```python
import functools

import jax
import jax.numpy as jnp
from jax import lax
from jax.experimental import pallas as pl
from jax.experimental.pallas import tpu as pltpu
from jax.sharding import PartitionSpec as P

AXES = ("band", "patch")
EPSILON = 1e-05
LANES = 128
BF = jnp.bfloat16
F32 = jnp.float32
I32 = jnp.int32


def dot(a, b):
    return jnp.dot(a, b, preferred_element_type=F32)


def dot_lanes(a, b):
    return lax.dot_general(a, b, (((1,), (1,)), ((), ())), preferred_element_type=F32)


def iota(shape, axis):
    return lax.broadcasted_iota(I32, shape, axis)


def flag(condition):
    return jnp.where(condition, 1.0, 0.0).astype(BF)


def column(row):
    count = row.shape[1]
    same = iota((count, count), 0) == iota((count, count), 1)
    return jnp.sum(jnp.where(same, row.astype(F32), 0.0), axis=1, keepdims=True).astype(I32)


def choose(row, count):
    return flag(iota((row.shape[1], count), 1) == column(row))


def choose_t(row, count):
    return flag(iota((count, row.shape[1]), 0) == row)


def line(ref):
    return ref[...].reshape(1, ref.shape[0])


def silu(v):
    return 0.5 * v * (1.0 + jnp.tanh(0.5 * v))


def finish(summed, second):
    out = dot(silu(summed).astype(BF), second)
    centred = out - jnp.mean(out, axis=-1, keepdims=True)
    spread = jnp.mean(centred * centred, axis=-1, keepdims=True)
    return centred * lax.rsqrt(spread + EPSILON)


def residual(base, update):
    return (base.astype(F32) + update).astype(BF)


def start(sems, first, *pairs):
    copies = [pltpu.make_async_copy(src, dst, sems.at[first + n]) for n, (src, dst) in enumerate(pairs)]
    for copy in copies:
        copy.start()
    return copies


def wait(*copies):
    for copy in copies:
        copy.wait()


def places(source, devices):
    edges = source.shape[1]
    earlier = flag(iota((edges, edges), 0) < iota((edges, edges), 1))
    hit = iota((devices, edges), 0) == source
    hits = flag(hit)
    return jnp.sum(jnp.where(hit, dot(hits, earlier), 0.0), axis=0, keepdims=True).astype(I32), hits


def fence(ref):
    def step(n, carry):
        ref[pl.ds(pl.multiple_of(n * 8, 8), 8), :] = jnp.zeros((8, ref.shape[1]), ref.dtype)
        return carry

    lax.fori_loop(0, 2, step, 0)


def serve(asked, kind, cap, table, wide, out):
    devices = asked.shape[0]
    blocks = table.shape[1] // LANES
    lanes = iota((devices, table.shape[0]), 1)
    hot = [flag(asked[:, lane : lane + 1] == lanes) for lane in range(kind * cap, kind * cap + cap)]
    got = dot(jnp.concatenate(hot, axis=0), table)
    for slot in range(cap):
        for block in range(blocks):
            target = pl.ds(slot * blocks + block, devices, stride=cap * blocks)
            wide[target, :] = got[slot * devices : (slot + 1) * devices, block * LANES : (block + 1) * LANES]
    out[...] = wide[...].astype(BF)


def take_in(cap, devices, packed, ends, wide, rows):
    blocks = rows.shape[1] // LANES
    rows[cap * devices :, :] = ends
    wide[...] = packed[...].astype(F32)
    for slot in range(cap):
        for block in range(blocks):
            source = pl.ds(slot * blocks + block, devices, stride=cap * blocks)
            target = pl.ds(slot * devices, devices)
            rows[target, block * LANES : (block + 1) * LANES] = wide[source, :].astype(BF)


def ask_kernel(
    cap, devices, dev0, dev1, dev2, row0, row1, row2, dst0, dst1, grid, mesh, w, request, lines, table, kept, w2,
    d0, d1, d2, r0, r1, r2, e0, e1, g, w01, earlier, spare, sems,
):
    count = g.shape[0]
    edges = lines.shape[1]
    m = kept.at[pl.ds(count, count)]
    devs, rows = (d0, d1, d2), (r0, r1, r2)
    copies = start(sems, 0, *zip((dev0, dev1, dev2, row0, row1, row2), devs + rows))
    fence(spare)
    later = start(sems, 6, (grid, g), (mesh, m), (w.at[pl.ds(0, 2)], w01))
    earlier[...] = flag(iota((edges, edges), 0) < iota((edges, edges), 1))
    fence(spare)
    wait(*copies[:3])
    hits = [iota((devices, edges), 0) == dev[...] for dev in devs]
    before = dot(flag(jnp.concatenate(hits, axis=0)), earlier[...])
    last = start(sems, 9, (dst0, e0), (dst1, e1), (w.at[2], w2))
    wait(*copies[3:], *later)
    values = []
    for kind in range(3):
        mine = jnp.where(hits[kind], before[kind * devices : (kind + 1) * devices, :], 0.0)
        place = jnp.sum(mine, axis=0, keepdims=True).astype(I32)
        lines[kind : kind + 1, :] = place * devices + devs[kind][...]
        row = line(rows[kind]).astype(F32)
        values.append(jnp.where(iota((LANES, edges), 0) == place + kind * cap, row, 0.0).astype(BF))
    hits = flag(jnp.concatenate(hits, axis=1))
    request[...] = dot_lanes(hits, jnp.concatenate(values, axis=1)).astype(I32)
    table[...] = dot(g[...], w01[0]).astype(BF)
    kept[:count, :] = dot(m[...], w01[1]).astype(BF)
    wait(*last)
    lines[3:4, :] = line(e0)
    lines[4:5, :] = line(e1)


def serve_kernel(cap, asked, table, out, wide):
    serve(asked[...], 0, cap, table[...], wide, out)


def enc_kernel(cap, received, asked, lines, kept, w2, w, one, out, w345, w8, one_v, wide, packed, rows, sems):
    copies = start(sems, 0, (w.at[pl.ds(3, 3)], w345), (w.at[8], w8))
    fence(wide)
    count = one_v.shape[0]
    devices = asked.shape[0]
    pick = choose(lines[0:1, :], cap * devices)
    to = choose(lines[3:4, :], count)
    to_t = choose_t(lines[3:4, :], count)
    take_in(cap, devices, received, kept[:count, :], wide, rows)
    summed = dot(jnp.concatenate([pick, to], axis=1), rows[...])
    message = finish(summed, w2[...]).astype(BF)
    summed = dot(to_t, message).astype(BF)
    wait(*copies)
    m = kept[count:, :]
    summed = dot(jnp.concatenate([m, summed], axis=1), w345[:2].reshape(2 * m.shape[1], m.shape[1]))
    mine = residual(m, finish(summed, w345[2]))
    one_v[...] = mine
    serve(asked[...], 1, cap, dot(mine, w8[...]).astype(BF), wide, packed)
    wait(*start(sems, 2, (one_v, one), (packed, out)))


def beside_kernel(
    one, grid, loc_src, loc_dst, w, kept, w10, dec_kept, g, w9, w8, w11, w6, w7, w15, w17, s, d, sems
):
    count = one.shape[0]
    mine = kept.at[pl.ds(3 * count, count)]
    grid_one = dec_kept.at[pl.ds(2 * count, count)]
    copies = start(
        sems, 0, (one, mine), (w.at[9], w9), (loc_src, s), (loc_dst, d), (w.at[8], w8), (w.at[10], w10),
        (w.at[11], w11), (grid, g), (w.at[6], w6), (w.at[7], w7), (w.at[15], w15), (w.at[17], w17),
    )
    wait(*copies[:2])
    kept[:count, :] = dot(mine[...], w9[...]).astype(BF)
    wait(*copies[2:5])
    start_rows = dot(mine[...], w8[...]).astype(BF)
    stop = line(d)
    both = jnp.concatenate([choose(line(s), count), choose(stop, count)], axis=1)
    summed = dot(both, jnp.concatenate([start_rows, kept[:count, :]], axis=0))
    wait(copies[5])
    message = finish(summed, w10[...]).astype(BF)
    kept[2 * count : 3 * count, :] = dot(choose_t(stop, count), message).astype(BF)
    wait(copies[6])
    kept[count : 2 * count, :] = dot(mine[...], w11[...]).astype(BF)
    wait(*copies[7:10])
    grid_one[...] = residual(g[...], finish(dot(g[...], w6[...]), w7[...]))
    wait(copies[10])
    dec_kept[:count, :] = dot(grid_one[...], w15[...]).astype(BF)
    wait(copies[11])
    dec_kept[count : 2 * count, :] = dot(grid_one[...], w17[...]).astype(BF)


def proc_kernel(cap, received, asked, lines, kept, w10, w, out, ws, wide, rows, sems):
    copies = start(sems, 0, (w.at[pl.ds(12, 3)], ws))
    fence(wide)
    count = kept.shape[0] // 4
    devices = asked.shape[0]
    pick = choose(lines[1:2, :], cap * devices)
    to = choose(lines[4:5, :], count)
    to_t = choose_t(lines[4:5, :], count)
    take_in(cap, devices, received, kept[:count, :], wide, rows)
    summed = dot(jnp.concatenate([pick, to], axis=1), rows[...])
    message = finish(summed, w10[...]).astype(BF)
    summed = (kept[2 * count : 3 * count, :].astype(F32) + dot(to_t, message)).astype(BF)
    wait(*copies)
    summed = kept[count : 2 * count, :].astype(F32) + dot(summed, ws[0])
    two = residual(kept[3 * count :, :], finish(summed, ws[1]))
    serve(asked[...], 2, cap, dot(two, ws[2]).astype(BF), wide, out)


def dec_kernel(cap, devices, received, lines, kept, w, out, w16, ws, wide, rows, sems):
    copies = start(sems, 0, (w.at[16], w16))
    fence(wide)
    copies += start(sems, 1, (w.at[pl.ds(18, 2)], ws))
    fence(wide)
    edges = lines.shape[1]
    count = kept.shape[0] // 3
    pick = choose(lines[2:3, :], cap * devices)
    near = iota((edges, count), 0) - 3 * iota((edges, count), 1)
    to = flag((near >= 0) & (near < 3))
    near = iota((count, edges), 1) - 3 * iota((count, edges), 0)
    to_t = flag((near >= 0) & (near < 3))
    take_in(cap, devices, received, kept[:count, :], wide, rows)
    summed = dot(jnp.concatenate([pick, to], axis=1), rows[...])
    wait(copies[0])
    message = finish(summed, w16[...]).astype(BF)
    summed = dot(to_t, message).astype(BF)
    wait(copies[1])
    summed = kept[count : 2 * count, :].astype(F32) + dot(summed, ws[0])
    out[...] = residual(kept[2 * count :, :], finish(summed, ws[1]))


def run(kernel, outs=(), near=(), far=(), held=(), copies=0, macs=0, away=(), last=False):
    inside = pl.BlockSpec(memory_space=pltpu.VMEM)
    outside = pl.BlockSpec(memory_space=pltpu.HBM)
    moved = sum(a.size * a.dtype.itemsize for a in list(held) + list(outs))
    return pl.pallas_call(
        kernel,
        out_shape=(
            *(a if last else pltpu.VMEM(a.shape, a.dtype) for a in outs),
            *(pltpu.HBM(a.shape, a.dtype) for a in away),
        ),
        in_specs=[inside] * len(near) + [outside] * len(far),
        out_specs=(inside,) * len(outs) + (outside,) * len(away),
        scratch_shapes=[pltpu.VMEM(a.shape, a.dtype) for a in held]
        + ([pltpu.SemaphoreType.DMA((copies,))] if copies else []),
        compiler_params=pltpu.CompilerParams(vmem_limit_bytes=16 * 2**20),
        cost_estimate=pl.CostEstimate(flops=2 * macs, bytes_accessed=moved, transcendentals=0),
    )(
        *(pltpu.with_memory_space_constraint(a, pltpu.VMEM) for a in near),
        *(pltpu.with_memory_space_constraint(a, pltpu.HBM) for a in far),
    )


def exchange(rows, devices):
    parts = rows.reshape(devices, rows.shape[0] // devices, LANES)
    moved = lax.all_to_all(parts, AXES, split_axis=0, concat_axis=0, tiled=True)
    return moved.reshape(rows.shape)


def body(
    grid_latent,
    mesh_latent,
    weights,
    enc_dev,
    enc_row,
    enc_dst,
    proc_dev,
    proc_row,
    proc_dst,
    loc_src,
    loc_dst,
    dec_dev,
    dec_row,
):
    devices = lax.axis_size("band") * lax.axis_size("patch")
    edges = enc_dev.shape[0]
    cap = max(2, 2 * edges // devices)
    count, width = mesh_latent.shape
    total = devices * cap

    def arr(shape, dtype):
        return jax.ShapeDtypeStruct(shape, dtype)

    across = arr((1, edges), I32)
    row = arr((edges,), I32)
    loc = arr(loc_src.shape, I32)
    mat = arr((width, width), BF)
    square = arr((edges, edges), BF)
    spare = arr((16, LANES), F32)
    nodes = arr((count, width), BF)
    lines = arr((8, edges), I32)
    ask = arr((devices, LANES), I32)
    flat = arr((total * width // LANES, LANES), BF)
    flat32 = arr(flat.shape, F32)
    rows = arr((total + count, width), BF)
    edge_macs = edges * width * (total + 3 * width)
    devs = tuple(a.reshape(1, edges) for a in (enc_dev, proc_dev, dec_dev))

    def mats(number):
        return arr((number, width, width), BF)

    def kept(parts):
        return arr((parts * count, width), BF)

    request, places_of, table, enc_kept, w2 = run(
        functools.partial(ask_kernel, cap, devices),
        (ask, lines, nodes, kept(2), mat),
        far=(*devs, enc_row, proc_row, dec_row, enc_dst, proc_dst, grid_latent, mesh_latent, weights),
        held=(across,) * 3 + (row,) * 5 + (nodes, mats(2), square, spare),
        copies=12,
        macs=3 * devices * edges * (edges + LANES) + 3 * count * width * width,
    )
    asked = request.reshape(devices, 1, LANES)
    wanted = lax.all_to_all(asked, AXES, split_axis=0, concat_axis=0, tiled=True).reshape(devices, LANES)
    (sent,) = run(
        functools.partial(serve_kernel, cap),
        (flat,),
        near=(wanted, table),
        held=(flat32,),
        macs=total * count * width,
    )
    enc_rows = exchange(sent, devices)
    mesh_one, sent = run(
        functools.partial(enc_kernel, cap),
        near=(enc_rows, wanted, places_of, enc_kept, w2),
        far=(weights,),
        held=(mats(3), mat, nodes, flat32, flat, rows),
        copies=4,
        macs=edge_macs,
        away=(nodes, flat),
    )
    proc_rows = exchange(sent, devices)
    proc_kept, w10, dec_kept = run(
        beside_kernel,
        (kept(4), mat, kept(3)),
        far=(mesh_one, grid_latent, loc_src, loc_dst, weights),
        held=(nodes,) + (mat,) * 7 + (loc, loc),
        copies=12,
        macs=11 * count * width * width,
    )
    (sent,) = run(
        functools.partial(proc_kernel, cap),
        (flat,),
        near=(proc_rows, wanted, places_of, proc_kept, w10),
        far=(weights,),
        held=(mats(3), flat32, rows),
        copies=1,
        macs=edge_macs,
    )
    dec_rows = exchange(sent, devices)
    (decoded,) = run(
        functools.partial(dec_kernel, cap, devices),
        (nodes,),
        near=(dec_rows, places_of, dec_kept),
        far=(weights,),
        held=(mat, mats(2), flat32, rows),
        copies=2,
        macs=edge_macs,
        last=True,
    )
    return decoded


def solution(mesh):
    rows = P(AXES, None)
    edge = P(AXES)
    in_specs = (rows, rows, P(), rows, edge, edge, rows, edge, edge, edge, edge, rows, edge)
    return jax.shard_map(body, mesh=mesh, in_specs=in_specs, out_specs=rows, check_vma=False)
```

```python
import functools

import jax
import jax.numpy as jnp
from jax import lax
from jax.experimental import pallas as pl
from jax.experimental.pallas import tpu as pltpu
from jax.sharding import PartitionSpec as P

AXES = ("band", "patch")
EPSILON = 1e-05
LANES = 128
BF = jnp.bfloat16
F32 = jnp.float32
I32 = jnp.int32


def dot(a, b):
    return jnp.dot(a, b, preferred_element_type=F32)


def dot_lanes(a, b):
    return lax.dot_general(a, b, (((1,), (1,)), ((), ())), preferred_element_type=F32)


def iota(shape, axis):
    return lax.broadcasted_iota(I32, shape, axis)


def flag(condition):
    return jnp.where(condition, 1.0, 0.0).astype(BF)


def column(row):
    count = row.shape[1]
    same = iota((count, count), 0) == iota((count, count), 1)
    return jnp.sum(jnp.where(same, row.astype(F32), 0.0), axis=1, keepdims=True).astype(I32)


def choose(row, count):
    return flag(iota((row.shape[1], count), 1) == column(row))


def choose_t(row, count):
    return flag(iota((count, row.shape[1]), 0) == row)


def line(ref):
    return ref[...].reshape(1, ref.shape[0])


def silu(v):
    return 0.5 * v * (1.0 + jnp.tanh(0.5 * v))


def centred(matrix):
    wide = matrix.astype(F32)
    return (wide - jnp.mean(wide, axis=-1, keepdims=True)).astype(BF)


def finish(summed, second, zero_mean=False):
    out = dot(silu(summed).astype(BF), second)
    if not zero_mean:
        out = out - jnp.mean(out, axis=-1, keepdims=True)
    return out * lax.rsqrt(jnp.mean(out * out, axis=-1, keepdims=True) + EPSILON)


def residual(base, update):
    return (base.astype(F32) + update).astype(BF)


def start(sems, first, *pairs):
    copies = [pltpu.make_async_copy(src, dst, sems.at[first + n]) for n, (src, dst) in enumerate(pairs)]
    for copy in copies:
        copy.start()
    return copies


def wait(*copies):
    for copy in copies:
        copy.wait()


def places(source, devices):
    edges = source.shape[1]
    earlier = flag(iota((edges, edges), 0) < iota((edges, edges), 1))
    hit = iota((devices, edges), 0) == source
    hits = flag(hit)
    return jnp.sum(jnp.where(hit, dot(hits, earlier), 0.0), axis=0, keepdims=True).astype(I32), hits


def fence(ref):
    def step(n, carry):
        ref[pl.ds(pl.multiple_of(n * 8, 8), 8), :] = jnp.zeros((8, ref.shape[1]), ref.dtype)
        return carry

    lax.fori_loop(0, 2, step, 0)


def serve(asked, kind, cap, table, wide, out):
    devices = asked.shape[0]
    blocks = table.shape[1] // LANES
    lanes = iota((devices, table.shape[0]), 1)
    hot = [flag(asked[:, lane : lane + 1] == lanes) for lane in range(kind * cap, kind * cap + cap)]
    got = dot(jnp.concatenate(hot, axis=0), table)
    for slot in range(cap):
        for block in range(blocks):
            target = pl.ds(slot * blocks + block, devices, stride=cap * blocks)
            wide[target, :] = got[slot * devices : (slot + 1) * devices, block * LANES : (block + 1) * LANES]
    out[...] = wide[...].astype(BF)


def take_in(cap, devices, packed, ends, wide, rows):
    blocks = rows.shape[1] // LANES
    rows[cap * devices :, :] = ends
    wide[...] = packed[...].astype(F32)
    for slot in range(cap):
        for block in range(blocks):
            source = pl.ds(slot * blocks + block, devices, stride=cap * blocks)
            target = pl.ds(slot * devices, devices)
            rows[target, block * LANES : (block + 1) * LANES] = wide[source, :].astype(BF)


def ask_kernel(
    cap, devices, dev0, dev1, dev2, row0, row1, row2, lines, request,
    d0, d1, d2, r0, r1, r2, asking, earlier, spare, sems,
):
    edges = lines.shape[1]
    devs, rows = (d0, d1, d2), (r0, r1, r2)
    copies = start(sems, 0, *zip((dev0, dev1, dev2, row0, row1, row2), devs + rows))
    earlier[...] = flag(iota((edges, edges), 0) < iota((edges, edges), 1))
    fence(spare)
    wait(*copies)
    hits = [iota((devices, edges), 0) == dev[...] for dev in devs]
    before = dot(flag(jnp.concatenate(hits, axis=0)), earlier[...])
    values = []
    for kind in range(3):
        mine = jnp.where(hits[kind], before[kind * devices : (kind + 1) * devices, :], 0.0)
        place = jnp.sum(mine, axis=0, keepdims=True).astype(I32)
        lines[kind : kind + 1, :] = place * devices + devs[kind][...]
        row = line(rows[kind]).astype(F32)
        values.append(jnp.where(iota((LANES, edges), 0) == place + kind * cap, row, 0.0).astype(BF))
    hits = flag(jnp.concatenate(hits, axis=1))
    asking[...] = dot_lanes(hits, jnp.concatenate(values, axis=1)).astype(I32)
    wait(*start(sems, 6, (asking, request)))


def prepare_kernel(
    grid, mesh, dst0, dst1, src2, dst2, w, table, kept, w2, w10, ends, w16, dec_kept,
    g, e0, e1, e2, e3, w01, w67, w16_v, w15, w17, dec_kept_v, sems,
):
    count = g.shape[0]
    m = kept.at[pl.ds(count, count)]
    one = dec_kept_v.at[pl.ds(2 * count, count)]
    copies = start(
        sems, 0, (grid, g), (w.at[pl.ds(0, 2)], w01), (mesh, m), (w.at[16], w16_v), (w.at[pl.ds(6, 2)], w67),
        (w.at[15], w15), (w.at[17], w17), (w.at[2], w2), (w.at[10], w10), (dst0, e0), (dst1, e1), (src2, e2), (dst2, e3),
    )
    wait(*copies[:3])
    table[...] = dot(g[...], w01[0]).astype(BF)
    kept[:count, :] = dot(m[...], w01[1]).astype(BF)
    wait(copies[3])
    w16_v[...] = centred(w16_v[...])
    out = start(sems, len(copies), (w16_v, w16))
    wait(*copies[4:7])
    one[...] = residual(g[...], finish(dot(g[...], w67[0]), w67[1]))
    dec_kept_v[:count, :] = dot(one[...], w15[...]).astype(BF)
    dec_kept_v[count : 2 * count, :] = dot(one[...], w17[...]).astype(BF)
    out += start(sems, len(copies) + 1, (dec_kept_v, dec_kept))
    wait(*copies[7:])
    w2[...] = centred(w2[...])
    w10[...] = centred(w10[...])
    for n, row in enumerate((e0, e1, e2, e3)):
        ends[n : n + 1, : row.shape[0]] = line(row)
    wait(*out)


def serve_kernel(cap, asked, table, out, wide):
    serve(asked[...], 0, cap, table[...], wide, out)


def enc_kernel(
    cap, received, asked, lines, ends, kept, w2, w, out, proc_kept, w34, w5, w89, w11, wide, rows, sems
):
    copies = start(sems, 0, (w.at[pl.ds(3, 2)], w34), (w.at[5], w5))
    fence(wide)
    copies += start(sems, 2, (w.at[pl.ds(8, 2)], w89), (w.at[11], w11))
    fence(wide)
    count = kept.shape[0] // 2
    others = asked.shape[0]
    pick = choose(lines[0:1, :], cap * others)
    to = choose(ends[0:1, :], count)
    to_t = choose_t(ends[0:1, :], count)
    take_in(cap, others, received, kept[:count, :], wide, rows)
    summed = dot(jnp.concatenate([pick, to], axis=1), rows[...])
    message = finish(summed, w2[...], True).astype(BF)
    summed = dot(to_t, message).astype(BF)
    wait(copies[0])
    m = kept[count:, :]
    summed = dot(jnp.concatenate([m, summed], axis=1), w34[...].reshape(2 * m.shape[1], m.shape[1]))
    wait(copies[1])
    mine = residual(m, finish(summed, w5[...]))
    wait(*copies[2:])
    table = dot(mine, w89[0]).astype(BF)
    serve(asked[...], 1, cap, table, wide, out)
    proc_kept[:count, :] = dot(mine, w89[1]).astype(BF)
    proc_kept[count : 2 * count, :] = table
    proc_kept[2 * count : 3 * count, :] = dot(mine, w11[...]).astype(BF)
    proc_kept[3 * count :, :] = mine


def proc_kernel(
    cap, local, received, asked, lines, ends, kept, w10, w, dec_far, out, dec_kept, ws, wide, rows, sems
):
    copies = start(sems, 0, (w.at[pl.ds(12, 3)], ws))
    fence(wide)
    copies += start(sems, 1, (dec_far, dec_kept))
    fence(wide)
    count = kept.shape[0] // 4
    others = asked.shape[0]
    pick = choose(lines[1:2, :], cap * others)
    to, near_to = choose(ends[1:2, :], count), choose(ends[3:4, :local], count)
    near_from = choose(ends[2:3, :local], count)
    to_t = jnp.concatenate([choose_t(ends[1:2, :], count), choose_t(ends[3:4, :local], count)], axis=1)
    near = dot(jnp.concatenate([near_to, near_from], axis=1), kept[: 2 * count, :])
    take_in(cap, others, received, kept[:count, :], wide, rows)
    far = dot(jnp.concatenate([pick, to], axis=1), rows[...])
    message = finish(jnp.concatenate([far, near], axis=0), w10[...], True).astype(BF)
    summed = dot(to_t, message).astype(BF)
    wait(copies[0])
    summed = kept[2 * count : 3 * count, :].astype(F32) + dot(summed, ws[0])
    two = residual(kept[3 * count :, :], finish(summed, ws[1]))
    serve(asked[...], 2, cap, dot(two, ws[2]).astype(BF), wide, out)
    wait(copies[1])


def dec_kernel(cap, others, received, lines, kept, w, late, out, w16, ws, wide, rows, sems):
    copies = start(sems, 0, (late, w16))
    fence(wide)
    copies += start(sems, 1, (w.at[pl.ds(18, 2)], ws))
    fence(wide)
    edges = lines.shape[1]
    count = kept.shape[0] // 3
    pick = choose(lines[2:3, :], cap * others)
    near = iota((edges, count), 0) - 3 * iota((edges, count), 1)
    to = flag((near >= 0) & (near < 3))
    near = iota((count, edges), 1) - 3 * iota((count, edges), 0)
    to_t = flag((near >= 0) & (near < 3))
    take_in(cap, others, received, kept[:count, :], wide, rows)
    summed = dot(jnp.concatenate([pick, to], axis=1), rows[...])
    wait(copies[0])
    message = finish(summed, w16[...], True).astype(BF)
    summed = dot(to_t, message).astype(BF)
    wait(*copies[1:])
    summed = kept[count : 2 * count, :].astype(F32) + dot(summed, ws[0])
    out[...] = residual(kept[2 * count :, :], finish(summed, ws[1]))


def run(kernel, outs=(), near=(), far=(), held=(), copies=0, macs=0, away=(), last=False):
    inside = pl.BlockSpec(memory_space=pltpu.VMEM)
    outside = pl.BlockSpec(memory_space=pltpu.HBM)
    moved = sum(a.size * a.dtype.itemsize for a in list(held) + list(outs))
    return pl.pallas_call(
        kernel,
        out_shape=(
            *(a if last else pltpu.VMEM(a.shape, a.dtype) for a in outs),
            *(pltpu.HBM(a.shape, a.dtype) for a in away),
        ),
        in_specs=[inside] * len(near) + [outside] * len(far),
        out_specs=(inside,) * len(outs) + (outside,) * len(away),
        scratch_shapes=[pltpu.VMEM(a.shape, a.dtype) for a in held]
        + ([pltpu.SemaphoreType.DMA((copies,))] if copies else []),
        compiler_params=pltpu.CompilerParams(vmem_limit_bytes=16 * 2**20),
        cost_estimate=pl.CostEstimate(flops=2 * macs, bytes_accessed=moved, transcendentals=0),
    )(
        *(pltpu.with_memory_space_constraint(a, pltpu.VMEM) for a in near),
        *(pltpu.with_memory_space_constraint(a, pltpu.HBM) for a in far),
    )


def exchange(rows, devices):
    parts = rows.reshape(devices, rows.shape[0] // devices, LANES)
    moved = lax.all_to_all(parts, AXES, split_axis=0, concat_axis=0, tiled=True)
    return moved.reshape(rows.shape)


def body(
    grid_latent,
    mesh_latent,
    weights,
    enc_dev,
    enc_row,
    enc_dst,
    proc_dev,
    proc_row,
    proc_dst,
    loc_src,
    loc_dst,
    dec_dev,
    dec_row,
):
    devices = lax.axis_size("band") * lax.axis_size("patch")
    edges = enc_dev.shape[0]
    cap = max(2, 2 * edges // devices)
    count, width = mesh_latent.shape
    total = devices * cap

    def arr(shape, dtype):
        return jax.ShapeDtypeStruct(shape, dtype)

    across = arr((1, edges), I32)
    row = arr((edges,), I32)
    loc = arr(loc_src.shape, I32)
    mat = arr((width, width), BF)
    square = arr((edges, edges), BF)
    spare = arr((16, LANES), F32)
    nodes = arr((count, width), BF)
    lines = arr((8, edges), I32)
    ask = arr((devices, LANES), I32)
    flat = arr((total * width // LANES, LANES), BF)
    flat32 = arr(flat.shape, F32)
    rows = arr((total + count, width), BF)
    edge_macs = edges * width * (total + 3 * width)
    devs = tuple(a.reshape(1, edges) for a in (enc_dev, proc_dev, dec_dev))

    def mats(number):
        return arr((number, width, width), BF)

    def kept(parts):
        return arr((parts * count, width), BF)

    places_of, request = run(
        functools.partial(ask_kernel, cap, devices),
        (lines,),
        far=(*devs, enc_row, proc_row, dec_row),
        held=(across,) * 3 + (row,) * 3 + (ask, square, spare),
        copies=7,
        macs=3 * devices * edges * (edges + LANES),
        away=(ask,),
    )
    asked = request.reshape(devices, 1, LANES)
    wanted = lax.all_to_all(asked, AXES, split_axis=0, concat_axis=0, tiled=True).reshape(devices, LANES)
    table, enc_kept, w2, w10, ends, w16, dec_far = run(
        prepare_kernel,
        (nodes, kept(2), mat, mat, lines),
        far=(grid_latent, mesh_latent, enc_dst, proc_dst, loc_src, loc_dst, weights),
        held=(nodes, row, row, loc, loc, mats(2), mats(2), mat, mat, mat, kept(3)),
        copies=15,
        macs=6 * count * width * width,
        away=(mat, kept(3)),
    )
    (sent,) = run(
        functools.partial(serve_kernel, cap),
        (flat,),
        near=(wanted, table),
        held=(flat32,),
        macs=total * count * width,
    )
    enc_rows = exchange(sent, devices)
    sent, proc_kept = run(
        functools.partial(enc_kernel, cap),
        (flat, kept(4)),
        near=(enc_rows, wanted, places_of, ends, enc_kept, w2),
        far=(weights,),
        held=(mats(2), mat, mats(2), mat, flat32, rows),
        copies=4,
        macs=edge_macs,
    )
    proc_rows = exchange(sent, devices)
    sent, dec_kept = run(
        functools.partial(proc_kernel, cap, loc_src.shape[0]),
        (flat, kept(3)),
        near=(proc_rows, wanted, places_of, ends, proc_kept, w10),
        far=(weights, dec_far),
        held=(mats(3), flat32, rows),
        copies=2,
        macs=edge_macs,
    )
    dec_rows = exchange(sent, devices)
    (decoded,) = run(
        functools.partial(dec_kernel, cap, devices),
        (nodes,),
        near=(dec_rows, places_of, dec_kept),
        far=(weights, w16),
        held=(mat, mats(2), flat32, rows),
        copies=2,
        macs=edge_macs,
        last=True,
    )
    return decoded


def solution(mesh):
    rows = P(AXES, None)
    edge = P(AXES)
    in_specs = (rows, rows, P(), rows, edge, edge, rows, edge, edge, edge, edge, rows, edge)
    return jax.shard_map(body, mesh=mesh, in_specs=in_specs, out_specs=rows, check_vma=False)
```

```python
import functools

import jax
import jax.numpy as jnp
from jax import lax
from jax.experimental import pallas as pl
from jax.experimental.pallas import tpu as pltpu
from jax.sharding import PartitionSpec as P

AXES = ("band", "patch")
EPSILON = 1e-05
LANES = 128
BF = jnp.bfloat16
F32 = jnp.float32
I32 = jnp.int32


def dot(a, b):
    return jnp.dot(a, b, preferred_element_type=F32)


def dot_lanes(a, b):
    return lax.dot_general(a, b, (((1,), (1,)), ((), ())), preferred_element_type=F32)


def iota(shape, axis):
    return lax.broadcasted_iota(I32, shape, axis)


def flag(condition):
    return jnp.where(condition, 1.0, 0.0).astype(BF)


def column(row):
    count = row.shape[1]
    same = iota((count, count), 0) == iota((count, count), 1)
    return jnp.sum(jnp.where(same, row.astype(F32), 0.0), axis=1, keepdims=True).astype(I32)


def choose(row, count):
    return flag(iota((row.shape[1], count), 1) == column(row))


def choose_t(row, count):
    return flag(iota((count, row.shape[1]), 0) == row)


def line(ref):
    return ref[...].reshape(1, ref.shape[0])


def silu(v):
    return 0.5 * v * (1.0 + jnp.tanh(0.5 * v))


def centred(matrix):
    wide = matrix.astype(F32)
    return (wide - jnp.mean(wide, axis=-1, keepdims=True)).astype(BF)


def finish(summed, second, zero_mean=False):
    out = dot(silu(summed).astype(BF), second)
    if not zero_mean:
        out = out - jnp.mean(out, axis=-1, keepdims=True)
    return out * lax.rsqrt(jnp.mean(out * out, axis=-1, keepdims=True) + EPSILON)


def residual(base, update):
    return (base.astype(F32) + update).astype(BF)


def start(sems, first, *pairs):
    copies = [pltpu.make_async_copy(src, dst, sems.at[first + n]) for n, (src, dst) in enumerate(pairs)]
    for copy in copies:
        copy.start()
    return copies


def wait(*copies):
    for copy in copies:
        copy.wait()


def places(source, devices):
    edges = source.shape[1]
    earlier = flag(iota((edges, edges), 0) < iota((edges, edges), 1))
    hit = iota((devices, edges), 0) == source
    hits = flag(hit)
    return jnp.sum(jnp.where(hit, dot(hits, earlier), 0.0), axis=0, keepdims=True).astype(I32), hits


def fence(ref):
    def step(n, carry):
        ref[pl.ds(pl.multiple_of(n * 8, 8), 8), :] = jnp.zeros((8, ref.shape[1]), ref.dtype)
        return carry

    lax.fori_loop(0, 2, step, 0)


def serve(asked, kind, cap, table, wide, out):
    devices = asked.shape[0]
    blocks = table.shape[1] // LANES
    each, pitch = cap * blocks, wide.shape[0] // devices
    lanes = iota((devices, table.shape[0]), 1)
    hot = [flag(asked[:, lane : lane + 1] == lanes) for lane in range(kind * cap, kind * cap + cap)]
    got = dot(jnp.concatenate(hot, axis=0), table)
    for slot in range(cap):
        for block in range(blocks):
            target = pl.ds(slot * blocks + block, devices, stride=pitch)
            wide[target, :] = got[slot * devices : (slot + 1) * devices, block * LANES : (block + 1) * LANES]
    for first in range(0, devices, 2):
        pair = [wide[pitch * n : pitch * n + each, :] for n in (first, first + 1)]
        out[each * first : each * (first + 2), :] = jnp.concatenate(pair, axis=0).astype(BF)


def take_in(cap, devices, packed, ends, wide, rows):
    blocks = rows.shape[1] // LANES
    each, pitch = cap * blocks, wide.shape[0] // devices
    rows[cap * devices :, :] = ends
    for first in range(0, devices, 2):
        pair = packed[each * first : each * (first + 2), :].astype(F32)
        wide[pitch * first : pitch * first + each, :] = pair[:each]
        wide[pitch * (first + 1) : pitch * (first + 1) + each, :] = pair[each:]
    for slot in range(cap):
        for block in range(blocks):
            source = pl.ds(slot * blocks + block, devices, stride=pitch)
            target = pl.ds(slot * devices, devices)
            rows[target, block * LANES : (block + 1) * LANES] = wide[source, :].astype(BF)


def ask_kernel(
    cap, devices, dev0, dev1, dev2, row0, row1, row2, lines, request,
    d0, d1, d2, r0, r1, r2, asking, earlier, spare, sems,
):
    edges = lines.shape[1]
    devs, rows = (d0, d1, d2), (r0, r1, r2)
    copies = start(sems, 0, *zip((dev0, dev1, dev2, row0, row1, row2), devs + rows))
    earlier[...] = flag(iota((edges, edges), 0) < iota((edges, edges), 1))
    fence(spare)
    wait(*copies[:3])
    hits = [iota((devices, edges), 0) == dev[...] for dev in devs]
    before = dot(flag(jnp.concatenate(hits, axis=0)), earlier[...])
    wait(*copies[3:])
    few = -(-3 * cap // 16) * 16
    values = []
    for kind in range(3):
        mine = jnp.where(hits[kind], before[kind * devices : (kind + 1) * devices, :], 0.0)
        place = jnp.sum(mine, axis=0, keepdims=True).astype(I32)
        lines[kind : kind + 1, :] = place * devices + devs[kind][...]
        row = line(rows[kind]).astype(F32)
        values.append(jnp.where(iota((few, edges), 0) == place + kind * cap, row, 0.0).astype(BF))
    hits = flag(jnp.concatenate(hits, axis=1))
    asking[:, :few] = dot_lanes(hits, jnp.concatenate(values, axis=1)).astype(I32)
    asking[:, few:] = jnp.zeros((devices, LANES - few), I32)
    wait(*start(sems, 6, (asking, request)))


def prepare_kernel(
    grid, mesh, dst0, dst1, src2, dst2, w, table, kept, w2, w10, ends, w16, dec_kept,
    g, e0, e1, e2, e3, w01, w67, w16_v, w15, w17, dec_kept_v, spare, sems,
):
    count = g.shape[0]
    m = kept.at[pl.ds(count, count)]
    one = dec_kept_v.at[pl.ds(2 * count, count)]
    copies = start(sems, 0, (grid, g), (w.at[pl.ds(6, 2)], w67))
    fence(spare)
    copies += start(sems, 2, (w.at[15], w15), (w.at[17], w17), (w.at[16], w16_v))
    fence(spare)
    copies += start(
        sems, 5, (mesh, m), (w.at[pl.ds(0, 2)], w01), (w.at[2], w2), (w.at[10], w10), (dst0, e0), (dst1, e1),
        (src2, e2), (dst2, e3),
    )
    fence(spare)
    wait(*copies[:2])
    one[...] = residual(g[...], finish(dot(g[...], w67[0]), w67[1]))
    wait(*copies[2:5])
    dec_kept_v[:count, :] = dot(one[...], w15[...]).astype(BF)
    dec_kept_v[count : 2 * count, :] = dot(one[...], w17[...]).astype(BF)
    w16_v[...] = centred(w16_v[...])
    out = start(sems, len(copies), (w16_v, w16), (dec_kept_v, dec_kept))
    fence(spare)
    wait(*copies[5:])
    table[...] = dot(g[...], w01[0]).astype(BF)
    kept[:count, :] = dot(m[...], w01[1]).astype(BF)
    w2[...] = centred(w2[...])
    w10[...] = centred(w10[...])
    for n, row in enumerate((e0, e1, e2, e3)):
        ends[n : n + 1, : row.shape[0]] = line(row)
    wait(*out)


def serve_kernel(cap, asked, table, out, wide):
    serve(asked[...], 0, cap, table[...], wide, out)


def enc_kernel(
    cap, received, asked, lines, ends, kept, w2, w, out, proc_kept, w34, w5, w89, w11, wide, rows, sems
):
    copies = start(sems, 0, (w.at[pl.ds(3, 2)], w34), (w.at[5], w5))
    fence(wide)
    copies += start(sems, 2, (w.at[pl.ds(8, 2)], w89), (w.at[11], w11))
    fence(wide)
    count = kept.shape[0] // 2
    others = asked.shape[0]
    pick = choose(lines[0:1, :], cap * others)
    to = choose(ends[0:1, :], count)
    to_t = choose_t(ends[0:1, :], count)
    take_in(cap, others, received, kept[:count, :], wide, rows)
    summed = dot(jnp.concatenate([pick, to], axis=1), rows[...])
    message = finish(summed, w2[...], True).astype(BF)
    summed = dot(to_t, message).astype(BF)
    wait(copies[0])
    m = kept[count:, :]
    summed = dot(jnp.concatenate([m, summed], axis=1), w34[...].reshape(2 * m.shape[1], m.shape[1]))
    wait(copies[1])
    mine = residual(m, finish(summed, w5[...]))
    wait(*copies[2:])
    table = dot(mine, w89[0]).astype(BF)
    serve(asked[...], 1, cap, table, wide, out)
    proc_kept[:count, :] = dot(mine, w89[1]).astype(BF)
    proc_kept[count : 2 * count, :] = table
    proc_kept[2 * count : 3 * count, :] = dot(mine, w11[...]).astype(BF)
    proc_kept[3 * count :, :] = mine


def proc_kernel(
    cap, local, received, asked, lines, ends, kept, w10, w, dec_far, w16_far, out, dec_kept, w16, ws, wide, rows, sems
):
    copies = start(sems, 0, (w.at[pl.ds(12, 3)], ws))
    fence(wide)
    copies += start(sems, 1, (dec_far, dec_kept), (w16_far, w16))
    fence(wide)
    count = kept.shape[0] // 4
    others = asked.shape[0]
    pick = choose(lines[1:2, :], cap * others)
    to, near_to = choose(ends[1:2, :], count), choose(ends[3:4, :local], count)
    near_from = choose(ends[2:3, :local], count)
    to_t = jnp.concatenate([choose_t(ends[1:2, :], count), choose_t(ends[3:4, :local], count)], axis=1)
    near = dot(jnp.concatenate([near_to, near_from], axis=1), kept[: 2 * count, :])
    take_in(cap, others, received, kept[:count, :], wide, rows)
    far = dot(jnp.concatenate([pick, to], axis=1), rows[...])
    message = finish(jnp.concatenate([far, near], axis=0), w10[...], True).astype(BF)
    summed = dot(to_t, message).astype(BF)
    wait(copies[0])
    summed = kept[2 * count : 3 * count, :].astype(F32) + dot(summed, ws[0])
    two = residual(kept[3 * count :, :], finish(summed, ws[1]))
    serve(asked[...], 2, cap, dot(two, ws[2]).astype(BF), wide, out)
    wait(*copies[1:])


def dec_kernel(cap, others, received, lines, kept, w16, w, out, ws, wide, rows, sems):
    copies = start(sems, 0, (w.at[pl.ds(18, 2)], ws))
    fence(wide)
    edges = lines.shape[1]
    count = kept.shape[0] // 3
    pick = choose(lines[2:3, :], cap * others)
    near = iota((edges, count), 0) - 3 * iota((edges, count), 1)
    to = flag((near >= 0) & (near < 3))
    near = iota((count, edges), 1) - 3 * iota((count, edges), 0)
    to_t = flag((near >= 0) & (near < 3))
    take_in(cap, others, received, kept[:count, :], wide, rows)
    summed = dot(jnp.concatenate([pick, to], axis=1), rows[...])
    message = finish(summed, w16[...], True).astype(BF)
    summed = dot(to_t, message).astype(BF)
    wait(*copies)
    summed = kept[count : 2 * count, :].astype(F32) + dot(summed, ws[0])
    out[...] = residual(kept[2 * count :, :], finish(summed, ws[1]))


def run(kernel, outs=(), near=(), far=(), held=(), copies=0, macs=0, away=(), last=False):
    inside = pl.BlockSpec(memory_space=pltpu.VMEM)
    outside = pl.BlockSpec(memory_space=pltpu.HBM)
    moved = sum(a.size * a.dtype.itemsize for a in list(held) + list(outs))
    return pl.pallas_call(
        kernel,
        out_shape=(
            *(a if last else pltpu.VMEM(a.shape, a.dtype) for a in outs),
            *(pltpu.HBM(a.shape, a.dtype) for a in away),
        ),
        in_specs=[inside] * len(near) + [outside] * len(far),
        out_specs=(inside,) * len(outs) + (outside,) * len(away),
        scratch_shapes=[pltpu.VMEM(a.shape, a.dtype) for a in held]
        + ([pltpu.SemaphoreType.DMA((copies,))] if copies else []),
        compiler_params=pltpu.CompilerParams(vmem_limit_bytes=16 * 2**20),
        cost_estimate=pl.CostEstimate(flops=2 * macs, bytes_accessed=moved, transcendentals=0),
    )(
        *(pltpu.with_memory_space_constraint(a, pltpu.VMEM) for a in near),
        *(pltpu.with_memory_space_constraint(a, pltpu.HBM) for a in far),
    )


def exchange(rows, devices):
    parts = rows.reshape(devices, rows.shape[0] // devices, LANES)
    moved = lax.all_to_all(parts, AXES, split_axis=0, concat_axis=0, tiled=True)
    return moved.reshape(rows.shape)


def body(
    grid_latent,
    mesh_latent,
    weights,
    enc_dev,
    enc_row,
    enc_dst,
    proc_dev,
    proc_row,
    proc_dst,
    loc_src,
    loc_dst,
    dec_dev,
    dec_row,
):
    devices = lax.axis_size("band") * lax.axis_size("patch")
    edges = enc_dev.shape[0]
    cap = max(2, 2 * edges // devices)
    count, width = mesh_latent.shape
    total = devices * cap

    def arr(shape, dtype):
        return jax.ShapeDtypeStruct(shape, dtype)

    across = arr((1, edges), I32)
    row = arr((edges,), I32)
    loc = arr(loc_src.shape, I32)
    mat = arr((width, width), BF)
    square = arr((edges, edges), BF)
    spare = arr((16, LANES), F32)
    nodes = arr((count, width), BF)
    lines = arr((8, edges), I32)
    ask = arr((devices, LANES), I32)
    flat = arr((total * width // LANES, LANES), BF)
    flat32 = arr((devices * (cap * width // LANES + 1), LANES), F32)
    rows = arr((total + count, width), BF)
    edge_macs = edges * width * (total + 3 * width)
    devs = tuple(a.reshape(1, edges) for a in (enc_dev, proc_dev, dec_dev))

    def mats(number):
        return arr((number, width, width), BF)

    def kept(parts):
        return arr((parts * count, width), BF)

    places_of, request = run(
        functools.partial(ask_kernel, cap, devices),
        (lines,),
        far=(*devs, enc_row, proc_row, dec_row),
        held=(across,) * 3 + (row,) * 3 + (ask, square, spare),
        copies=7,
        macs=3 * devices * edges * (edges + LANES),
        away=(ask,),
    )
    asked = request.reshape(devices, 1, LANES)
    wanted = lax.all_to_all(asked, AXES, split_axis=0, concat_axis=0, tiled=True).reshape(devices, LANES)
    table, enc_kept, w2, w10, ends, w16_far, dec_far = run(
        prepare_kernel,
        (nodes, kept(2), mat, mat, lines),
        far=(grid_latent, mesh_latent, enc_dst, proc_dst, loc_src, loc_dst, weights),
        held=(nodes, row, row, loc, loc, mats(2), mats(2), mat, mat, mat, kept(3), spare),
        copies=15,
        macs=6 * count * width * width,
        away=(mat, kept(3)),
    )
    (sent,) = run(
        functools.partial(serve_kernel, cap),
        (flat,),
        near=(wanted, table),
        held=(flat32,),
        macs=total * count * width,
    )
    enc_rows = exchange(sent, devices)
    sent, proc_kept = run(
        functools.partial(enc_kernel, cap),
        (flat, kept(4)),
        near=(enc_rows, wanted, places_of, ends, enc_kept, w2),
        far=(weights,),
        held=(mats(2), mat, mats(2), mat, flat32, rows),
        copies=4,
        macs=edge_macs,
    )
    proc_rows = exchange(sent, devices)
    sent, dec_kept, w16 = run(
        functools.partial(proc_kernel, cap, loc_src.shape[0]),
        (flat, kept(3), mat),
        near=(proc_rows, wanted, places_of, ends, proc_kept, w10),
        far=(weights, dec_far, w16_far),
        held=(mats(3), flat32, rows),
        copies=3,
        macs=edge_macs,
    )
    dec_rows = exchange(sent, devices)
    (decoded,) = run(
        functools.partial(dec_kernel, cap, devices),
        (nodes,),
        near=(dec_rows, places_of, dec_kept, w16),
        far=(weights,),
        held=(mats(2), flat32, rows),
        copies=1,
        macs=edge_macs,
        last=True,
    )
    return decoded


def solution(mesh):
    rows = P(AXES, None)
    edge = P(AXES)
    in_specs = (rows, rows, P(), rows, edge, edge, rows, edge, edge, edge, edge, rows, edge)
    return jax.shard_map(body, mesh=mesh, in_specs=in_specs, out_specs=rows, check_vma=False)
```

```python
import functools

import jax
import jax.numpy as jnp
from jax import lax
from jax.experimental import pallas as pl
from jax.experimental.pallas import tpu as pltpu
from jax.sharding import PartitionSpec as P

AXES = ("band", "patch")
EPSILON = 1e-05
LANES = 128
BF = jnp.bfloat16
F32 = jnp.float32
I32 = jnp.int32


def dot(a, b):
    return jnp.dot(a, b, preferred_element_type=F32)


def dot_lanes(a, b):
    return lax.dot_general(a, b, (((1,), (1,)), ((), ())), preferred_element_type=F32)


def iota(shape, axis):
    return lax.broadcasted_iota(I32, shape, axis)


def flag(condition):
    return jnp.where(condition, 1.0, 0.0).astype(BF)


def column(row):
    count = row.shape[1]
    same = iota((count, count), 0) == iota((count, count), 1)
    return jnp.sum(jnp.where(same, row.astype(F32), 0.0), axis=1, keepdims=True).astype(I32)


def choose(row, count):
    return flag(iota((row.shape[1], count), 1) == column(row))


def choose_t(row, count):
    return flag(iota((count, row.shape[1]), 0) == row)


def line(ref):
    return ref[...].reshape(1, ref.shape[0])


def silu(v):
    return 0.5 * v * (1.0 + jnp.tanh(0.5 * v))


def centred(matrix):
    wide = matrix.astype(F32)
    return (wide - jnp.mean(wide, axis=-1, keepdims=True)).astype(BF)


def finish(summed, second, zero_mean=False):
    out = dot(silu(summed).astype(BF), second)
    if not zero_mean:
        out = out - jnp.mean(out, axis=-1, keepdims=True)
    return out * lax.rsqrt(jnp.mean(out * out, axis=-1, keepdims=True) + EPSILON)


def residual(base, update):
    return (base.astype(F32) + update).astype(BF)


def start(sems, first, *pairs):
    copies = [pltpu.make_async_copy(src, dst, sems.at[first + n]) for n, (src, dst) in enumerate(pairs)]
    for copy in copies:
        copy.start()
    return copies


def wait(*copies):
    for copy in copies:
        copy.wait()


def places(source, devices):
    edges = source.shape[1]
    earlier = flag(iota((edges, edges), 0) < iota((edges, edges), 1))
    hit = iota((devices, edges), 0) == source
    hits = flag(hit)
    return jnp.sum(jnp.where(hit, dot(hits, earlier), 0.0), axis=0, keepdims=True).astype(I32), hits


def fence(ref):
    def step(n, carry):
        ref[pl.ds(pl.multiple_of(n * 8, 8), 8), :] = jnp.zeros((8, ref.shape[1]), ref.dtype)
        return carry

    lax.fori_loop(0, 2, step, 0)


def serve(asked, kind, cap, table, wide, out):
    devices = asked.shape[0]
    blocks = table.shape[1] // LANES
    each, pitch = cap * blocks, wide.shape[0] // devices
    lanes = iota((devices, table.shape[0]), 1)
    hot = [flag(asked[:, lane : lane + 1] == lanes) for lane in range(kind * cap, kind * cap + cap)]
    got = dot(jnp.concatenate(hot, axis=0), table)
    for slot in range(cap):
        for block in range(blocks):
            target = pl.ds(slot * blocks + block, devices, stride=pitch)
            wide[target, :] = got[slot * devices : (slot + 1) * devices, block * LANES : (block + 1) * LANES]
    for first in range(0, devices, 2):
        pair = [wide[pitch * n : pitch * n + each, :] for n in (first, first + 1)]
        out[each * first : each * (first + 2), :] = jnp.concatenate(pair, axis=0).astype(BF)


def take_in(cap, devices, packed, ends, wide, rows):
    blocks = rows.shape[1] // LANES
    each, pitch = cap * blocks, wide.shape[0] // devices
    rows[cap * devices :, :] = ends
    for first in range(0, devices, 2):
        pair = packed[each * first : each * (first + 2), :].astype(F32)
        wide[pitch * first : pitch * first + each, :] = pair[:each]
        wide[pitch * (first + 1) : pitch * (first + 1) + each, :] = pair[each:]
    for slot in range(cap):
        for block in range(blocks):
            source = pl.ds(slot * blocks + block, devices, stride=pitch)
            target = pl.ds(slot * devices, devices)
            rows[target, block * LANES : (block + 1) * LANES] = wide[source, :].astype(BF)


def ask_kernel(
    cap, devices, dev0, dev1, dev2, row0, row1, row2, lines, request,
    d0, d1, d2, r0, r1, r2, asking, earlier, spare, sems,
):
    edges = lines.shape[1]
    devs, rows = (d0, d1, d2), (r0, r1, r2)
    copies = start(sems, 0, *zip((dev0, dev1, dev2, row0, row1, row2), devs + rows))
    earlier[...] = flag(iota((edges, edges), 0) < iota((edges, edges), 1))
    fence(spare)
    wait(*copies[:3])
    hits = [iota((devices, edges), 0) == dev[...] for dev in devs]
    before = dot(flag(jnp.concatenate(hits, axis=0)), earlier[...])
    wait(*copies[3:])
    few = -(-3 * cap // 16) * 16
    values = []
    for kind in range(3):
        mine = jnp.where(hits[kind], before[kind * devices : (kind + 1) * devices, :], 0.0)
        place = jnp.sum(mine, axis=0, keepdims=True).astype(I32)
        lines[kind : kind + 1, :] = place * devices + devs[kind][...]
        row = line(rows[kind]).astype(F32)
        values.append(jnp.where(iota((few, edges), 0) == place + kind * cap, row, 0.0).astype(BF))
    hits = flag(jnp.concatenate(hits, axis=1))
    asking[:, :few] = dot_lanes(hits, jnp.concatenate(values, axis=1)).astype(I32)
    asking[:, few:] = jnp.zeros((devices, LANES - few), I32)
    wait(*start(sems, 6, (asking, request)))


def prepare_kernel(
    grid, mesh, dst0, dst1, src2, dst2, w, table, kept, w2, w10, ends, w16, dec_kept,
    g, e0, e1, e2, e3, w01, w3, w67, w16_v, w15, w17, dec_kept_v, spare, sems,
):
    count = g.shape[0]
    m = kept.at[pl.ds(count, count)]
    one = dec_kept_v.at[pl.ds(2 * count, count)]
    copies = start(sems, 0, (grid, g), (w.at[pl.ds(6, 2)], w67))
    fence(spare)
    copies += start(sems, 2, (w.at[15], w15), (w.at[17], w17), (w.at[16], w16_v))
    fence(spare)
    copies += start(
        sems, 5, (mesh, m), (w.at[pl.ds(0, 2)], w01), (w.at[3], w3), (w.at[2], w2), (w.at[10], w10), (dst0, e0), (dst1, e1),
        (src2, e2), (dst2, e3),
    )
    fence(spare)
    wait(*copies[:2])
    one[...] = residual(g[...], finish(dot(g[...], w67[0]), w67[1]))
    wait(*copies[2:5])
    dec_kept_v[:count, :] = dot(one[...], w15[...]).astype(BF)
    dec_kept_v[count : 2 * count, :] = dot(one[...], w17[...]).astype(BF)
    w16_v[...] = centred(w16_v[...])
    out = start(sems, len(copies), (w16_v, w16), (dec_kept_v, dec_kept))
    fence(spare)
    wait(*copies[5:])
    table[...] = dot(g[...], w01[0]).astype(BF)
    kept[:count, :] = dot(m[...], w01[1]).astype(BF)
    kept[2 * count :, :] = dot(m[...], w3[...]).astype(BF)
    w2[...] = centred(w2[...])
    w10[...] = centred(w10[...])
    for n, row in enumerate((e0, e1, e2, e3)):
        ends[n : n + 1, : row.shape[0]] = line(row)
    wait(*out)


def serve_kernel(cap, asked, table, out, wide):
    serve(asked[...], 0, cap, table[...], wide, out)


def enc_kernel(
    cap, received, asked, lines, ends, kept, w2, w, out, proc_kept, w45, w89, w11, wide, rows, sems
):
    copies = start(sems, 0, (w.at[pl.ds(4, 2)], w45))
    fence(wide)
    copies += start(sems, 1, (w.at[pl.ds(8, 2)], w89), (w.at[11], w11))
    fence(wide)
    count = kept.shape[0] // 3
    others = asked.shape[0]
    pick = choose(lines[0:1, :], cap * others)
    to = choose(ends[0:1, :], count)
    to_t = choose_t(ends[0:1, :], count)
    take_in(cap, others, received, kept[:count, :], wide, rows)
    summed = dot(jnp.concatenate([pick, to], axis=1), rows[...])
    message = finish(summed, w2[...], True).astype(BF)
    summed = dot(to_t, message).astype(BF)
    wait(copies[0])
    summed = kept[2 * count :, :].astype(F32) + dot(summed, w45[0])
    mine = residual(kept[count : 2 * count, :], finish(summed, w45[1]))
    wait(*copies[1:])
    table = dot(mine, w89[0]).astype(BF)
    serve(asked[...], 1, cap, table, wide, out)
    proc_kept[:count, :] = dot(mine, w89[1]).astype(BF)
    proc_kept[count : 2 * count, :] = table
    proc_kept[2 * count : 3 * count, :] = dot(mine, w11[...]).astype(BF)
    proc_kept[3 * count :, :] = mine


def proc_kernel(
    cap, local, received, asked, lines, ends, kept, w10, w, dec_far, w16_far, out, dec_kept, w16, ws, wide, rows, sems
):
    copies = start(sems, 0, (w.at[pl.ds(12, 3)], ws))
    fence(wide)
    copies += start(sems, 1, (dec_far, dec_kept), (w16_far, w16))
    fence(wide)
    count = kept.shape[0] // 4
    others = asked.shape[0]
    pick = choose(lines[1:2, :], cap * others)
    to, near_to = choose(ends[1:2, :], count), choose(ends[3:4, :local], count)
    near_from = choose(ends[2:3, :local], count)
    to_t = jnp.concatenate([choose_t(ends[1:2, :], count), choose_t(ends[3:4, :local], count)], axis=1)
    near = dot(jnp.concatenate([near_to, near_from], axis=1), kept[: 2 * count, :])
    take_in(cap, others, received, kept[:count, :], wide, rows)
    far = dot(jnp.concatenate([pick, to], axis=1), rows[...])
    message = finish(jnp.concatenate([far, near], axis=0), w10[...], True).astype(BF)
    summed = dot(to_t, message).astype(BF)
    wait(copies[0])
    summed = kept[2 * count : 3 * count, :].astype(F32) + dot(summed, ws[0])
    two = residual(kept[3 * count :, :], finish(summed, ws[1]))
    serve(asked[...], 2, cap, dot(two, ws[2]).astype(BF), wide, out)
    wait(*copies[1:])


def dec_kernel(cap, others, received, lines, kept, w16, w, out, ws, wide, rows, sems):
    copies = start(sems, 0, (w.at[pl.ds(18, 2)], ws))
    fence(wide)
    edges = lines.shape[1]
    count = kept.shape[0] // 3
    pick = choose(lines[2:3, :], cap * others)
    near = iota((edges, count), 0) - 3 * iota((edges, count), 1)
    to = flag((near >= 0) & (near < 3))
    near = iota((count, edges), 1) - 3 * iota((count, edges), 0)
    to_t = flag((near >= 0) & (near < 3))
    take_in(cap, others, received, kept[:count, :], wide, rows)
    summed = dot(jnp.concatenate([pick, to], axis=1), rows[...])
    message = finish(summed, w16[...], True).astype(BF)
    summed = dot(to_t, message).astype(BF)
    wait(*copies)
    summed = kept[count : 2 * count, :].astype(F32) + dot(summed, ws[0])
    out[...] = residual(kept[2 * count :, :], finish(summed, ws[1]))


def run(kernel, outs=(), near=(), far=(), held=(), copies=0, macs=0, away=(), last=False):
    inside = pl.BlockSpec(memory_space=pltpu.VMEM)
    outside = pl.BlockSpec(memory_space=pltpu.HBM)
    moved = sum(a.size * a.dtype.itemsize for a in list(held) + list(outs))
    return pl.pallas_call(
        kernel,
        out_shape=(
            *(a if last else pltpu.VMEM(a.shape, a.dtype) for a in outs),
            *(pltpu.HBM(a.shape, a.dtype) for a in away),
        ),
        in_specs=[inside] * len(near) + [outside] * len(far),
        out_specs=(inside,) * len(outs) + (outside,) * len(away),
        scratch_shapes=[pltpu.VMEM(a.shape, a.dtype) for a in held]
        + ([pltpu.SemaphoreType.DMA((copies,))] if copies else []),
        compiler_params=pltpu.CompilerParams(vmem_limit_bytes=16 * 2**20),
        cost_estimate=pl.CostEstimate(flops=2 * macs, bytes_accessed=moved, transcendentals=0),
    )(
        *(pltpu.with_memory_space_constraint(a, pltpu.VMEM) for a in near),
        *(pltpu.with_memory_space_constraint(a, pltpu.HBM) for a in far),
    )


def exchange(rows, devices):
    parts = rows.reshape(devices, rows.shape[0] // devices, LANES)
    moved = lax.all_to_all(parts, AXES, split_axis=0, concat_axis=0, tiled=True)
    return moved.reshape(rows.shape)


def body(
    grid_latent,
    mesh_latent,
    weights,
    enc_dev,
    enc_row,
    enc_dst,
    proc_dev,
    proc_row,
    proc_dst,
    loc_src,
    loc_dst,
    dec_dev,
    dec_row,
):
    devices = lax.axis_size("band") * lax.axis_size("patch")
    edges = enc_dev.shape[0]
    cap = max(2, 2 * edges // devices)
    count, width = mesh_latent.shape
    total = devices * cap

    def arr(shape, dtype):
        return jax.ShapeDtypeStruct(shape, dtype)

    across = arr((1, edges), I32)
    row = arr((edges,), I32)
    loc = arr(loc_src.shape, I32)
    mat = arr((width, width), BF)
    square = arr((edges, edges), BF)
    spare = arr((16, LANES), F32)
    nodes = arr((count, width), BF)
    lines = arr((8, edges), I32)
    ask = arr((devices, LANES), I32)
    flat = arr((total * width // LANES, LANES), BF)
    spread = devices * (cap * width // LANES + 1)
    flat32 = arr((spread + 32, LANES), F32)
    rows = arr((total + count, width), BF)
    edge_macs = edges * width * (total + 3 * width)
    devs = tuple(a.reshape(1, edges) for a in (enc_dev, proc_dev, dec_dev))

    def mats(number):
        return arr((number, width, width), BF)

    def kept(parts):
        return arr((parts * count, width), BF)

    places_of, request = run(
        functools.partial(ask_kernel, cap, devices),
        (lines,),
        far=(*devs, enc_row, proc_row, dec_row),
        held=(across,) * 3 + (row,) * 3 + (ask, square, spare),
        copies=7,
        macs=3 * devices * edges * (edges + LANES),
        away=(ask,),
    )
    asked = request.reshape(devices, 1, LANES)
    wanted = lax.all_to_all(asked, AXES, split_axis=0, concat_axis=0, tiled=True).reshape(devices, LANES)
    table, enc_kept, w2, w10, ends, w16_far, dec_far = run(
        prepare_kernel,
        (nodes, kept(3), mat, mat, lines),
        far=(grid_latent, mesh_latent, enc_dst, proc_dst, loc_src, loc_dst, weights),
        held=(nodes, row, row, loc, loc, mats(2), mat, mats(2), mat, mat, mat, kept(3), spare),
        copies=16,
        macs=6 * count * width * width,
        away=(mat, kept(3)),
    )
    (sent,) = run(
        functools.partial(serve_kernel, cap),
        (flat,),
        near=(wanted, table),
        held=(flat32,),
        macs=total * count * width,
    )
    enc_rows = exchange(sent, devices)
    sent, proc_kept = run(
        functools.partial(enc_kernel, cap),
        (flat, kept(4)),
        near=(enc_rows, wanted, places_of, ends, enc_kept, w2),
        far=(weights,),
        held=(mats(2), mats(2), mat, flat32, rows),
        copies=3,
        macs=edge_macs,
    )
    proc_rows = exchange(sent, devices)
    sent, dec_kept, w16 = run(
        functools.partial(proc_kernel, cap, loc_src.shape[0]),
        (flat, kept(3), mat),
        near=(proc_rows, wanted, places_of, ends, proc_kept, w10),
        far=(weights, dec_far, w16_far),
        held=(mats(3), flat32, rows),
        copies=3,
        macs=edge_macs,
    )
    dec_rows = exchange(sent, devices)
    (decoded,) = run(
        functools.partial(dec_kernel, cap, devices),
        (nodes,),
        near=(dec_rows, places_of, dec_kept, w16),
        far=(weights,),
        held=(mats(2), flat32, rows),
        copies=1,
        macs=edge_macs,
        last=True,
    )
    return decoded


def solution(mesh):
    rows = P(AXES, None)
    edge = P(AXES)
    in_specs = (rows, rows, P(), rows, edge, edge, rows, edge, edge, edge, edge, rows, edge)
    return jax.shard_map(body, mesh=mesh, in_specs=in_specs, out_specs=rows, check_vma=False)
```

```python
import functools

import jax
import jax.numpy as jnp
from jax import lax
from jax.experimental import pallas as pl
from jax.experimental.pallas import tpu as pltpu
from jax.sharding import PartitionSpec as P

AXES = ("band", "patch")
EPSILON = 1e-05
LANES = 128
BF = jnp.bfloat16
F32 = jnp.float32
I32 = jnp.int32


def dot(a, b):
    return jnp.dot(a, b, preferred_element_type=F32)


def dot_lanes(a, b):
    return lax.dot_general(a, b, (((1,), (1,)), ((), ())), preferred_element_type=F32)


def iota(shape, axis):
    return lax.broadcasted_iota(I32, shape, axis)


def flag(condition):
    return jnp.where(condition, 1.0, 0.0).astype(BF)


def column(row):
    count = row.shape[1]
    same = iota((count, count), 0) == iota((count, count), 1)
    return jnp.sum(jnp.where(same, row.astype(F32), 0.0), axis=1, keepdims=True).astype(I32)


def choose(row, count):
    return flag(iota((row.shape[1], count), 1) == column(row))


def choose_t(row, count):
    return flag(iota((count, row.shape[1]), 0) == row)


def line(ref):
    return ref[...].reshape(1, ref.shape[0])


def silu(v):
    return 0.5 * v * (1.0 + jnp.tanh(0.5 * v))


def centred(matrix):
    wide = matrix.astype(F32)
    return (wide - jnp.mean(wide, axis=-1, keepdims=True)).astype(BF)


def finish(summed, second, zero_mean=False):
    out = dot(silu(summed).astype(BF), second)
    if not zero_mean:
        out = out - jnp.mean(out, axis=-1, keepdims=True)
    return out * lax.rsqrt(jnp.mean(out * out, axis=-1, keepdims=True) + EPSILON)


def residual(base, update):
    return (base.astype(F32) + update).astype(BF)


def start(sems, first, *pairs):
    copies = [pltpu.make_async_copy(src, dst, sems.at[first + n]) for n, (src, dst) in enumerate(pairs)]
    for copy in copies:
        copy.start()
    return copies


def wait(*copies):
    for copy in copies:
        copy.wait()


def places(source, devices):
    edges = source.shape[1]
    earlier = flag(iota((edges, edges), 0) < iota((edges, edges), 1))
    hit = iota((devices, edges), 0) == source
    hits = flag(hit)
    return jnp.sum(jnp.where(hit, dot(hits, earlier), 0.0), axis=0, keepdims=True).astype(I32), hits


def fence(ref):
    def step(n, carry):
        ref[pl.ds(pl.multiple_of(n * 8, 8), 8), :] = jnp.zeros((8, ref.shape[1]), ref.dtype)
        return carry

    lax.fori_loop(0, 2, step, 0)


def serve(asked, kind, cap, table, wide, out):
    devices = asked.shape[0]
    blocks = table.shape[1] // LANES
    each, pitch = cap * blocks, wide.shape[0] // devices
    lanes = iota((devices, table.shape[0]), 1)
    hot = [flag(asked[:, lane : lane + 1] == lanes) for lane in range(kind * cap, kind * cap + cap)]
    got = dot(jnp.concatenate(hot, axis=0), table)
    for slot in range(cap):
        for block in range(blocks):
            target = pl.ds(slot * blocks + block, devices, stride=pitch)
            wide[target, :] = got[slot * devices : (slot + 1) * devices, block * LANES : (block + 1) * LANES]
    for first in range(0, devices, 2):
        pair = [wide[pitch * n : pitch * n + each, :] for n in (first, first + 1)]
        out[each * first : each * (first + 2), :] = jnp.concatenate(pair, axis=0).astype(BF)


def take_in(cap, devices, packed, ends, wide, rows):
    blocks = rows.shape[1] // LANES
    each, pitch = cap * blocks, wide.shape[0] // devices
    rows[cap * devices :, :] = ends
    for first in range(0, devices, 2):
        pair = packed[each * first : each * (first + 2), :].astype(F32)
        wide[pitch * first : pitch * first + each, :] = pair[:each]
        wide[pitch * (first + 1) : pitch * (first + 1) + each, :] = pair[each:]
    for slot in range(cap):
        for block in range(blocks):
            source = pl.ds(slot * blocks + block, devices, stride=pitch)
            target = pl.ds(slot * devices, devices)
            rows[target, block * LANES : (block + 1) * LANES] = wide[source, :].astype(BF)


def ask_kernel(
    cap, devices, dev0, dev1, dev2, row0, row1, row2, lines, request,
    d0, d1, d2, r0, r1, r2, asking, earlier, spare, sems,
):
    edges = lines.shape[1]
    devs, rows = (d0, d1, d2), (r0, r1, r2)
    copies = start(sems, 0, *zip((dev0, dev1, dev2, row0, row1, row2), devs + rows))
    earlier[...] = flag(iota((edges, edges), 0) < iota((edges, edges), 1))
    fence(spare)
    wait(*copies[:3])
    hits = [iota((devices, edges), 0) == dev[...] for dev in devs]
    before = dot(flag(jnp.concatenate(hits, axis=0)), earlier[...])
    wait(*copies[3:])
    few = -(-3 * cap // 16) * 16
    values = []
    for kind in range(3):
        mine = jnp.where(hits[kind], before[kind * devices : (kind + 1) * devices, :], 0.0)
        place = jnp.sum(mine, axis=0, keepdims=True).astype(I32)
        lines[kind : kind + 1, :] = place * devices + devs[kind][...]
        row = line(rows[kind]).astype(F32)
        values.append(jnp.where(iota((few, edges), 0) == place + kind * cap, row, 0.0).astype(BF))
    hits = flag(jnp.concatenate(hits, axis=1))
    asking[:, :few] = dot_lanes(hits, jnp.concatenate(values, axis=1)).astype(I32)
    asking[:, few:] = jnp.zeros((devices, LANES - few), I32)
    wait(*start(sems, 6, (asking, request)))


def prepare_kernel(
    grid, mesh, dst0, dst1, src2, dst2, w, table, kept, w2, w10, ends, w16, dec_kept,
    g, e0, e1, e2, e3, w01, w67, w16_v, w15, w17, dec_kept_v, spare, sems,
):
    count = g.shape[0]
    m = kept.at[pl.ds(count, count)]
    one = dec_kept_v.at[pl.ds(2 * count, count)]
    copies = start(sems, 0, (grid, g), (w.at[pl.ds(6, 2)], w67))
    fence(spare)
    copies += start(sems, 2, (w.at[15], w15), (w.at[17], w17), (w.at[16], w16_v))
    fence(spare)
    copies += start(
        sems, 5, (mesh, m), (w.at[pl.ds(0, 2)], w01), (w.at[2], w2), (w.at[10], w10), (dst0, e0), (dst1, e1),
        (src2, e2), (dst2, e3),
    )
    fence(spare)
    wait(*copies[:2])
    one[...] = residual(g[...], finish(dot(g[...], w67[0]), w67[1]))
    wait(*copies[2:5])
    dec_kept_v[:count, :] = dot(one[...], w15[...]).astype(BF)
    dec_kept_v[count : 2 * count, :] = dot(one[...], w17[...]).astype(BF)
    w16_v[...] = centred(w16_v[...])
    out = start(sems, len(copies), (w16_v, w16), (dec_kept_v, dec_kept))
    fence(spare)
    wait(*copies[5:])
    table[...] = dot(g[...], w01[0]).astype(BF)
    kept[:count, :] = dot(m[...], w01[1]).astype(BF)
    w2[...] = centred(w2[...])
    w10[...] = centred(w10[...])
    for n, row in enumerate((e0, e1, e2, e3)):
        ends[n : n + 1, : row.shape[0]] = line(row)
    wait(*out)


def serve_kernel(cap, asked, table, out, wide):
    serve(asked[...], 0, cap, table[...], wide, out)


def enc_kernel(
    cap, received, asked, lines, ends, kept, w2, w, out, proc_kept, w34, w5, w89, w11, wide, rows, sems
):
    copies = start(sems, 0, (w.at[pl.ds(3, 2)], w34), (w.at[5], w5))
    fence(wide)
    copies += start(sems, 2, (w.at[pl.ds(8, 2)], w89), (w.at[11], w11))
    fence(wide)
    count = kept.shape[0] // 2
    others = asked.shape[0]
    pick = choose(lines[0:1, :], cap * others)
    to = choose(ends[0:1, :], count)
    to_t = choose_t(ends[0:1, :], count)
    take_in(cap, others, received, kept[:count, :], wide, rows)
    summed = dot(jnp.concatenate([pick, to], axis=1), rows[...])
    message = finish(summed, w2[...], True).astype(BF)
    summed = dot(to_t, message).astype(BF)
    wait(copies[0])
    m = kept[count:, :]
    summed = dot(jnp.concatenate([m, summed], axis=1), w34[...].reshape(2 * m.shape[1], m.shape[1]))
    wait(copies[1])
    mine = residual(m, finish(summed, w5[...]))
    wait(*copies[2:])
    table = dot(mine, w89[0]).astype(BF)
    serve(asked[...], 1, cap, table, wide, out)
    proc_kept[:count, :] = dot(mine, w89[1]).astype(BF)
    proc_kept[count : 2 * count, :] = table
    proc_kept[2 * count : 3 * count, :] = dot(mine, w11[...]).astype(BF)
    proc_kept[3 * count :, :] = mine


def proc_kernel(
    cap, local, received, asked, lines, ends, kept, w10, w, dec_far, w16_far, out, dec_kept, w16, ws, wide, rows, sems
):
    copies = start(sems, 0, (w.at[pl.ds(12, 3)], ws))
    fence(wide)
    copies += start(sems, 1, (dec_far, dec_kept), (w16_far, w16))
    fence(wide)
    count = kept.shape[0] // 4
    others = asked.shape[0]
    pick = choose(lines[1:2, :], cap * others)
    to, near_to = choose(ends[1:2, :], count), choose(ends[3:4, :local], count)
    near_from = choose(ends[2:3, :local], count)
    to_t = jnp.concatenate([choose_t(ends[1:2, :], count), choose_t(ends[3:4, :local], count)], axis=1)
    near = dot(jnp.concatenate([near_to, near_from], axis=1), kept[: 2 * count, :])
    take_in(cap, others, received, kept[:count, :], wide, rows)
    far = dot(jnp.concatenate([pick, to], axis=1), rows[...])
    message = finish(jnp.concatenate([far, near], axis=0), w10[...], True).astype(BF)
    summed = dot(to_t, message).astype(BF)
    wait(copies[0])
    summed = kept[2 * count : 3 * count, :].astype(F32) + dot(summed, ws[0])
    two = residual(kept[3 * count :, :], finish(summed, ws[1]))
    serve(asked[...], 2, cap, dot(two, ws[2]).astype(BF), wide, out)
    wait(*copies[1:])


def dec_kernel(cap, others, received, lines, kept, w16, w, out, ws, wide, rows, sems):
    copies = start(sems, 0, (w.at[pl.ds(18, 2)], ws))
    fence(wide)
    edges = lines.shape[1]
    count = kept.shape[0] // 3
    pick = choose(lines[2:3, :], cap * others)
    near = iota((edges, count), 0) - 3 * iota((edges, count), 1)
    to = flag((near >= 0) & (near < 3))
    near = iota((count, edges), 1) - 3 * iota((count, edges), 0)
    to_t = flag((near >= 0) & (near < 3))
    take_in(cap, others, received, kept[:count, :], wide, rows)
    summed = dot(jnp.concatenate([pick, to], axis=1), rows[...])
    message = finish(summed, w16[...], True).astype(BF)
    summed = dot(to_t, message).astype(BF)
    wait(*copies)
    summed = kept[count : 2 * count, :].astype(F32) + dot(summed, ws[0])
    out[...] = residual(kept[2 * count :, :], finish(summed, ws[1]))


def run(kernel, outs=(), near=(), far=(), held=(), copies=0, macs=0, away=(), last=False):
    inside = pl.BlockSpec(memory_space=pltpu.VMEM)
    outside = pl.BlockSpec(memory_space=pltpu.HBM)
    moved = sum(a.size * a.dtype.itemsize for a in list(held) + list(outs))
    return pl.pallas_call(
        kernel,
        out_shape=(
            *(a if last else pltpu.VMEM(a.shape, a.dtype) for a in outs),
            *(pltpu.HBM(a.shape, a.dtype) for a in away),
        ),
        in_specs=[inside] * len(near) + [outside] * len(far),
        out_specs=(inside,) * len(outs) + (outside,) * len(away),
        scratch_shapes=[pltpu.VMEM(a.shape, a.dtype) for a in held]
        + ([pltpu.SemaphoreType.DMA((copies,))] if copies else []),
        compiler_params=pltpu.CompilerParams(vmem_limit_bytes=16 * 2**20),
        cost_estimate=pl.CostEstimate(flops=2 * macs, bytes_accessed=moved, transcendentals=0),
    )(
        *(pltpu.with_memory_space_constraint(a, pltpu.VMEM) for a in near),
        *(pltpu.with_memory_space_constraint(a, pltpu.HBM) for a in far),
    )


def exchange(rows, devices):
    parts = rows.reshape(devices, rows.shape[0] // devices, LANES)
    moved = lax.all_to_all(parts, AXES, split_axis=0, concat_axis=0, tiled=True)
    return moved.reshape(rows.shape)


def body(
    grid_latent,
    mesh_latent,
    weights,
    enc_dev,
    enc_row,
    enc_dst,
    proc_dev,
    proc_row,
    proc_dst,
    loc_src,
    loc_dst,
    dec_dev,
    dec_row,
):
    devices = lax.axis_size("band") * lax.axis_size("patch")
    edges = enc_dev.shape[0]
    cap = max(2, 2 * edges // devices)
    count, width = mesh_latent.shape
    total = devices * cap

    def arr(shape, dtype):
        return jax.ShapeDtypeStruct(shape, dtype)

    across = arr((1, edges), I32)
    row = arr((edges,), I32)
    loc = arr(loc_src.shape, I32)
    mat = arr((width, width), BF)
    square = arr((edges, edges), BF)
    spare = arr((16, LANES), F32)
    nodes = arr((count, width), BF)
    lines = arr((8, edges), I32)
    ask = arr((devices, LANES), I32)
    flat = arr((total * width // LANES, LANES), BF)
    spread = devices * (cap * width // LANES + 1)
    flat32 = arr((spread + 32, LANES), F32)
    rows = arr((total + count, width), BF)
    edge_macs = edges * width * (total + 3 * width)
    devs = tuple(a.reshape(1, edges) for a in (enc_dev, proc_dev, dec_dev))

    def mats(number):
        return arr((number, width, width), BF)

    def kept(parts):
        return arr((parts * count, width), BF)

    places_of, request = run(
        functools.partial(ask_kernel, cap, devices),
        (lines,),
        far=(*devs, enc_row, proc_row, dec_row),
        held=(across,) * 3 + (row,) * 3 + (ask, square, spare),
        copies=7,
        macs=3 * devices * edges * (edges + LANES),
        away=(ask,),
    )
    asked = request.reshape(devices, 1, LANES)
    wanted = lax.all_to_all(asked, AXES, split_axis=0, concat_axis=0, tiled=True).reshape(devices, LANES)
    table, enc_kept, w2, w10, ends, w16_far, dec_far = run(
        prepare_kernel,
        (nodes, kept(2), mat, mat, lines),
        far=(grid_latent, mesh_latent, enc_dst, proc_dst, loc_src, loc_dst, weights),
        held=(nodes, row, row, loc, loc, mats(2), mats(2), mat, mat, mat, kept(3), spare),
        copies=15,
        macs=6 * count * width * width,
        away=(mat, kept(3)),
    )
    (sent,) = run(
        functools.partial(serve_kernel, cap),
        (flat,),
        near=(wanted, table),
        held=(flat32,),
        macs=total * count * width,
    )
    enc_rows = exchange(sent, devices)
    sent, proc_kept = run(
        functools.partial(enc_kernel, cap),
        (flat, kept(4)),
        near=(enc_rows, wanted, places_of, ends, enc_kept, w2),
        far=(weights,),
        held=(mats(2), mat, mats(2), mat, flat32, rows),
        copies=4,
        macs=edge_macs,
    )
    proc_rows = exchange(sent, devices)
    sent, dec_kept, w16 = run(
        functools.partial(proc_kernel, cap, loc_src.shape[0]),
        (flat, kept(3), mat),
        near=(proc_rows, wanted, places_of, ends, proc_kept, w10),
        far=(weights, dec_far, w16_far),
        held=(mats(3), flat32, rows),
        copies=3,
        macs=edge_macs,
    )
    dec_rows = exchange(sent, devices)
    (decoded,) = run(
        functools.partial(dec_kernel, cap, devices),
        (nodes,),
        near=(dec_rows, places_of, dec_kept, w16),
        far=(weights,),
        held=(mats(2), flat32, rows),
        copies=1,
        macs=edge_macs,
        last=True,
    )
    return decoded


def solution(mesh):
    rows = P(AXES, None)
    edge = P(AXES)
    in_specs = (rows, rows, P(), rows, edge, edge, rows, edge, edge, edge, edge, rows, edge)
    return jax.shard_map(body, mesh=mesh, in_specs=in_specs, out_specs=rows, check_vma=False)
```

```python
import functools

import jax
import jax.numpy as jnp
from jax import lax
from jax.experimental import pallas as pl
from jax.experimental.pallas import tpu as pltpu
from jax.sharding import PartitionSpec as P

AXES = ("band", "patch")
EPSILON = 1e-05
LANES = 128
BF = jnp.bfloat16
F32 = jnp.float32
I32 = jnp.int32


def dot(a, b):
    return jnp.dot(a, b, preferred_element_type=F32)


def dot_lanes(a, b):
    return lax.dot_general(a, b, (((1,), (1,)), ((), ())), preferred_element_type=F32)


def iota(shape, axis):
    return lax.broadcasted_iota(I32, shape, axis)


def flag(condition):
    return jnp.where(condition, 1.0, 0.0).astype(BF)


def column(row):
    count = row.shape[1]
    same = iota((count, count), 0) == iota((count, count), 1)
    return jnp.sum(jnp.where(same, row.astype(F32), 0.0), axis=1, keepdims=True).astype(I32)


def choose(row, count):
    return flag(iota((row.shape[1], count), 1) == column(row))


def choose_t(row, count):
    return flag(iota((count, row.shape[1]), 0) == row)


def line(ref):
    return ref[...].reshape(1, ref.shape[0])


def silu(v):
    return 0.5 * v * (1.0 + jnp.tanh(0.5 * v))


def centred(matrix):
    wide = matrix.astype(F32)
    return (wide - jnp.mean(wide, axis=-1, keepdims=True)).astype(BF)


def finish(summed, second, zero_mean=False):
    out = dot(silu(summed).astype(BF), second)
    if not zero_mean:
        out = out - jnp.mean(out, axis=-1, keepdims=True)
    return out * lax.rsqrt(jnp.mean(out * out, axis=-1, keepdims=True) + EPSILON)


def residual(base, update):
    return (base.astype(F32) + update).astype(BF)


def start(sems, first, *pairs):
    copies = [pltpu.make_async_copy(src, dst, sems.at[first + n]) for n, (src, dst) in enumerate(pairs)]
    for copy in copies:
        copy.start()
    return copies


def wait(*copies):
    for copy in copies:
        copy.wait()


def places(source, devices):
    edges = source.shape[1]
    earlier = flag(iota((edges, edges), 0) < iota((edges, edges), 1))
    hit = iota((devices, edges), 0) == source
    hits = flag(hit)
    return jnp.sum(jnp.where(hit, dot(hits, earlier), 0.0), axis=0, keepdims=True).astype(I32), hits


def fence(ref):
    def step(n, carry):
        ref[pl.ds(pl.multiple_of(n * 8, 8), 8), :] = jnp.zeros((8, ref.shape[1]), ref.dtype)
        return carry

    lax.fori_loop(0, 2, step, 0)


def serve(asked, kind, cap, table, wide, out):
    devices = asked.shape[0]
    blocks = table.shape[1] // LANES
    each, pitch = cap * blocks, wide.shape[0] // devices
    lanes = iota((devices, table.shape[0]), 1)
    hot = [flag(asked[:, lane : lane + 1] == lanes) for lane in range(kind * cap, kind * cap + cap)]
    got = dot(jnp.concatenate(hot, axis=0), table)
    for slot in range(cap):
        for block in range(blocks):
            target = pl.ds(slot * blocks + block, devices, stride=pitch)
            wide[target, :] = got[slot * devices : (slot + 1) * devices, block * LANES : (block + 1) * LANES]
    for first in range(0, devices, 2):
        pair = [wide[pitch * n : pitch * n + each, :] for n in (first, first + 1)]
        out[each * first : each * (first + 2), :] = jnp.concatenate(pair, axis=0).astype(BF)


def take_in(cap, devices, packed, ends, wide, rows):
    blocks = rows.shape[1] // LANES
    each, pitch = cap * blocks, wide.shape[0] // devices
    rows[cap * devices :, :] = ends
    for first in range(0, devices, 2):
        pair = packed[each * first : each * (first + 2), :].astype(F32)
        wide[pitch * first : pitch * first + each, :] = pair[:each]
        wide[pitch * (first + 1) : pitch * (first + 1) + each, :] = pair[each:]
    for slot in range(cap):
        for block in range(blocks):
            source = pl.ds(slot * blocks + block, devices, stride=pitch)
            target = pl.ds(slot * devices, devices)
            rows[target, block * LANES : (block + 1) * LANES] = wide[source, :].astype(BF)


def ask_kernel(
    cap, devices, dev0, dev1, dev2, row0, row1, row2, lines, request,
    d0, d1, d2, r0, r1, r2, asking, earlier, spare, sems,
):
    edges = lines.shape[1]
    devs, rows = (d0, d1, d2), (r0, r1, r2)
    copies = start(sems, 0, *zip((dev0, dev1, dev2, row0, row1, row2), devs + rows))
    earlier[...] = flag(iota((edges, edges), 0) < iota((edges, edges), 1))
    fence(spare)
    wait(*copies[:3])
    hits = [iota((devices, edges), 0) == dev[...] for dev in devs]
    before = dot(flag(jnp.concatenate(hits, axis=0)), earlier[...])
    wait(*copies[3:])
    few = -(-3 * cap // 16) * 16
    values = []
    for kind in range(3):
        mine = jnp.where(hits[kind], before[kind * devices : (kind + 1) * devices, :], 0.0)
        place = jnp.sum(mine, axis=0, keepdims=True).astype(I32)
        lines[kind : kind + 1, :] = place * devices + devs[kind][...]
        row = line(rows[kind]).astype(F32)
        values.append(jnp.where(iota((few, edges), 0) == place + kind * cap, row, 0.0).astype(BF))
    hits = flag(jnp.concatenate(hits, axis=1))
    asking[:, :few] = dot_lanes(hits, jnp.concatenate(values, axis=1)).astype(I32)
    asking[:, few:] = jnp.zeros((devices, LANES - few), I32)
    wait(*start(sems, 6, (asking, request)))


def prepare_kernel(
    grid, mesh, dst0, dst1, src2, dst2, w, table, kept, w2, w10, ends, w16, dec_kept,
    g, e0, e1, e2, e3, first, w67, mid, dec_kept_v, spare, sems,
):
    count = g.shape[0]
    m = kept.at[pl.ds(count, count)]
    one = dec_kept_v.at[pl.ds(2 * count, count)]
    copies = start(sems, 0, (grid, g), (w.at[pl.ds(6, 2)], w67))
    fence(spare)
    copies += start(sems, 2, (w.at[pl.ds(15, 3)], mid))
    fence(spare)
    copies += start(
        sems, 3, (mesh, m), (w.at[pl.ds(0, 3)], first), (w.at[10], w10), (dst0, e0), (dst1, e1), (src2, e2), (dst2, e3)
    )
    fence(spare)
    wait(*copies[:2])
    one[...] = residual(g[...], finish(dot(g[...], w67[0]), w67[1]))
    wait(copies[2])
    dec_kept_v[:count, :] = dot(one[...], mid[0]).astype(BF)
    dec_kept_v[count : 2 * count, :] = dot(one[...], mid[2]).astype(BF)
    mid[1] = centred(mid[1])
    out = start(sems, len(copies), (mid.at[1], w16), (dec_kept_v, dec_kept))
    fence(spare)
    wait(*copies[3:])
    table[...] = dot(g[...], first[0]).astype(BF)
    kept[:count, :] = dot(m[...], first[1]).astype(BF)
    w2[...] = centred(first[2])
    w10[...] = centred(w10[...])
    for n, row in enumerate((e0, e1, e2, e3)):
        ends[n : n + 1, : row.shape[0]] = line(row)
    wait(*out)


def serve_kernel(cap, asked, table, out, wide):
    serve(asked[...], 0, cap, table[...], wide, out)


def enc_kernel(
    cap, received, asked, lines, ends, kept, w2, w, out, proc_kept, w34, w5, w89, w11, wide, rows, sems
):
    copies = start(sems, 0, (w.at[pl.ds(3, 2)], w34), (w.at[5], w5))
    fence(wide)
    copies += start(sems, 2, (w.at[pl.ds(8, 2)], w89), (w.at[11], w11))
    fence(wide)
    count = kept.shape[0] // 2
    others = asked.shape[0]
    pick = choose(lines[0:1, :], cap * others)
    to = choose(ends[0:1, :], count)
    to_t = choose_t(ends[0:1, :], count)
    take_in(cap, others, received, kept[:count, :], wide, rows)
    summed = dot(jnp.concatenate([pick, to], axis=1), rows[...])
    message = finish(summed, w2[...], True).astype(BF)
    summed = dot(to_t, message).astype(BF)
    wait(copies[0])
    m = kept[count:, :]
    summed = dot(jnp.concatenate([m, summed], axis=1), w34[...].reshape(2 * m.shape[1], m.shape[1]))
    wait(copies[1])
    mine = residual(m, finish(summed, w5[...]))
    wait(*copies[2:])
    table = dot(mine, w89[0]).astype(BF)
    serve(asked[...], 1, cap, table, wide, out)
    proc_kept[:count, :] = dot(mine, w89[1]).astype(BF)
    proc_kept[count : 2 * count, :] = table
    proc_kept[2 * count : 3 * count, :] = dot(mine, w11[...]).astype(BF)
    proc_kept[3 * count :, :] = mine


def proc_kernel(
    cap, local, received, asked, lines, ends, kept, w10, w, dec_far, w16_far, out, dec_kept, w16, ws, wide, rows, sems
):
    copies = start(sems, 0, (w.at[pl.ds(12, 3)], ws))
    fence(wide)
    copies += start(sems, 1, (dec_far, dec_kept), (w16_far, w16))
    fence(wide)
    count = kept.shape[0] // 4
    others = asked.shape[0]
    pick = choose(lines[1:2, :], cap * others)
    to, near_to = choose(ends[1:2, :], count), choose(ends[3:4, :local], count)
    near_from = choose(ends[2:3, :local], count)
    to_t = jnp.concatenate([choose_t(ends[1:2, :], count), choose_t(ends[3:4, :local], count)], axis=1)
    near = dot(jnp.concatenate([near_to, near_from], axis=1), kept[: 2 * count, :])
    take_in(cap, others, received, kept[:count, :], wide, rows)
    far = dot(jnp.concatenate([pick, to], axis=1), rows[...])
    message = finish(jnp.concatenate([far, near], axis=0), w10[...], True).astype(BF)
    summed = dot(to_t, message).astype(BF)
    wait(copies[0])
    summed = kept[2 * count : 3 * count, :].astype(F32) + dot(summed, ws[0])
    two = residual(kept[3 * count :, :], finish(summed, ws[1]))
    serve(asked[...], 2, cap, dot(two, ws[2]).astype(BF), wide, out)
    wait(*copies[1:])


def dec_kernel(cap, others, received, lines, kept, w16, w, out, ws, wide, rows, sems):
    copies = start(sems, 0, (w.at[pl.ds(18, 2)], ws))
    fence(wide)
    edges = lines.shape[1]
    count = kept.shape[0] // 3
    pick = choose(lines[2:3, :], cap * others)
    near = iota((edges, count), 0) - 3 * iota((edges, count), 1)
    to = flag((near >= 0) & (near < 3))
    near = iota((count, edges), 1) - 3 * iota((count, edges), 0)
    to_t = flag((near >= 0) & (near < 3))
    take_in(cap, others, received, kept[:count, :], wide, rows)
    summed = dot(jnp.concatenate([pick, to], axis=1), rows[...])
    message = finish(summed, w16[...], True).astype(BF)
    summed = dot(to_t, message).astype(BF)
    wait(*copies)
    summed = kept[count : 2 * count, :].astype(F32) + dot(summed, ws[0])
    out[...] = residual(kept[2 * count :, :], finish(summed, ws[1]))


def run(kernel, outs=(), near=(), far=(), held=(), copies=0, macs=0, away=(), last=False):
    inside = pl.BlockSpec(memory_space=pltpu.VMEM)
    outside = pl.BlockSpec(memory_space=pltpu.HBM)
    moved = sum(a.size * a.dtype.itemsize for a in list(held) + list(outs))
    return pl.pallas_call(
        kernel,
        out_shape=(
            *(a if last else pltpu.VMEM(a.shape, a.dtype) for a in outs),
            *(pltpu.HBM(a.shape, a.dtype) for a in away),
        ),
        in_specs=[inside] * len(near) + [outside] * len(far),
        out_specs=(inside,) * len(outs) + (outside,) * len(away),
        scratch_shapes=[pltpu.VMEM(a.shape, a.dtype) for a in held]
        + ([pltpu.SemaphoreType.DMA((copies,))] if copies else []),
        compiler_params=pltpu.CompilerParams(vmem_limit_bytes=16 * 2**20),
        cost_estimate=pl.CostEstimate(flops=2 * macs, bytes_accessed=moved, transcendentals=0),
    )(
        *(pltpu.with_memory_space_constraint(a, pltpu.VMEM) for a in near),
        *(pltpu.with_memory_space_constraint(a, pltpu.HBM) for a in far),
    )


def exchange(rows, devices):
    parts = rows.reshape(devices, rows.shape[0] // devices, LANES)
    moved = lax.all_to_all(parts, AXES, split_axis=0, concat_axis=0, tiled=True)
    return moved.reshape(rows.shape)


def body(
    grid_latent,
    mesh_latent,
    weights,
    enc_dev,
    enc_row,
    enc_dst,
    proc_dev,
    proc_row,
    proc_dst,
    loc_src,
    loc_dst,
    dec_dev,
    dec_row,
):
    devices = lax.axis_size("band") * lax.axis_size("patch")
    edges = enc_dev.shape[0]
    cap = max(2, 2 * edges // devices)
    count, width = mesh_latent.shape
    total = devices * cap

    def arr(shape, dtype):
        return jax.ShapeDtypeStruct(shape, dtype)

    across = arr((1, edges), I32)
    row = arr((edges,), I32)
    loc = arr(loc_src.shape, I32)
    mat = arr((width, width), BF)
    square = arr((edges, edges), BF)
    spare = arr((16, LANES), F32)
    nodes = arr((count, width), BF)
    lines = arr((8, edges), I32)
    ask = arr((devices, LANES), I32)
    flat = arr((total * width // LANES, LANES), BF)
    spread = devices * (cap * width // LANES + 1)
    flat32 = arr((spread + 32, LANES), F32)
    rows = arr((total + count, width), BF)
    edge_macs = edges * width * (total + 3 * width)
    devs = tuple(a.reshape(1, edges) for a in (enc_dev, proc_dev, dec_dev))

    def mats(number):
        return arr((number, width, width), BF)

    def kept(parts):
        return arr((parts * count, width), BF)

    places_of, request = run(
        functools.partial(ask_kernel, cap, devices),
        (lines,),
        far=(*devs, enc_row, proc_row, dec_row),
        held=(across,) * 3 + (row,) * 3 + (ask, square, spare),
        copies=7,
        macs=3 * devices * edges * (edges + LANES),
        away=(ask,),
    )
    asked = request.reshape(devices, 1, LANES)
    wanted = lax.all_to_all(asked, AXES, split_axis=0, concat_axis=0, tiled=True).reshape(devices, LANES)
    table, enc_kept, w2, w10, ends, w16_far, dec_far = run(
        prepare_kernel,
        (nodes, kept(2), mat, mat, lines),
        far=(grid_latent, mesh_latent, enc_dst, proc_dst, loc_src, loc_dst, weights),
        held=(nodes, row, row, loc, loc, mats(3), mats(2), mats(3), kept(3), spare),
        copies=12,
        macs=6 * count * width * width,
        away=(mat, kept(3)),
    )
    (sent,) = run(
        functools.partial(serve_kernel, cap),
        (flat,),
        near=(wanted, table),
        held=(flat32,),
        macs=total * count * width,
    )
    enc_rows = exchange(sent, devices)
    sent, proc_kept = run(
        functools.partial(enc_kernel, cap),
        (flat, kept(4)),
        near=(enc_rows, wanted, places_of, ends, enc_kept, w2),
        far=(weights,),
        held=(mats(2), mat, mats(2), mat, flat32, rows),
        copies=4,
        macs=edge_macs,
    )
    proc_rows = exchange(sent, devices)
    sent, dec_kept, w16 = run(
        functools.partial(proc_kernel, cap, loc_src.shape[0]),
        (flat, kept(3), mat),
        near=(proc_rows, wanted, places_of, ends, proc_kept, w10),
        far=(weights, dec_far, w16_far),
        held=(mats(3), flat32, rows),
        copies=3,
        macs=edge_macs,
    )
    dec_rows = exchange(sent, devices)
    (decoded,) = run(
        functools.partial(dec_kernel, cap, devices),
        (nodes,),
        near=(dec_rows, places_of, dec_kept, w16),
        far=(weights,),
        held=(mats(2), flat32, rows),
        copies=1,
        macs=edge_macs,
        last=True,
    )
    return decoded


def solution(mesh):
    rows = P(AXES, None)
    edge = P(AXES)
    in_specs = (rows, rows, P(), rows, edge, edge, rows, edge, edge, edge, edge, rows, edge)
    return jax.shard_map(body, mesh=mesh, in_specs=in_specs, out_specs=rows, check_vma=False)
```

```python
import functools

import jax
import jax.numpy as jnp
from jax import lax
from jax.experimental import pallas as pl
from jax.experimental.pallas import tpu as pltpu
from jax.sharding import PartitionSpec as P

AXES = ("band", "patch")
EPSILON = 1e-05
LANES = 128
BF = jnp.bfloat16
F32 = jnp.float32
I32 = jnp.int32


def dot(a, b):
    return jnp.dot(a, b, preferred_element_type=F32)


def dot_lanes(a, b):
    return lax.dot_general(a, b, (((1,), (1,)), ((), ())), preferred_element_type=F32)


def iota(shape, axis):
    return lax.broadcasted_iota(I32, shape, axis)


def flag(condition):
    return jnp.where(condition, 1.0, 0.0).astype(BF)


def column(row):
    count = row.shape[1]
    same = iota((count, count), 0) == iota((count, count), 1)
    return jnp.sum(jnp.where(same, row.astype(F32), 0.0), axis=1, keepdims=True).astype(I32)


def choose(row, count):
    return flag(iota((row.shape[1], count), 1) == column(row))


def choose_t(row, count):
    return flag(iota((count, row.shape[1]), 0) == row)


def line(ref):
    return ref[...].reshape(1, ref.shape[0])


def silu(v):
    return 0.5 * v * (1.0 + jnp.tanh(0.5 * v))


def centred(matrix):
    wide = matrix.astype(F32)
    return (wide - jnp.mean(wide, axis=-1, keepdims=True)).astype(BF)


def finish(summed, second, zero_mean=False):
    out = dot(silu(summed).astype(BF), second)
    if not zero_mean:
        out = out - jnp.mean(out, axis=-1, keepdims=True)
    return out * lax.rsqrt(jnp.mean(out * out, axis=-1, keepdims=True) + EPSILON)


def residual(base, update):
    return (base.astype(F32) + update).astype(BF)


def start(sems, first, *pairs):
    copies = [pltpu.make_async_copy(src, dst, sems.at[first + n]) for n, (src, dst) in enumerate(pairs)]
    for copy in copies:
        copy.start()
    return copies


def wait(*copies):
    for copy in copies:
        copy.wait()


def places(source, devices):
    edges = source.shape[1]
    earlier = flag(iota((edges, edges), 0) < iota((edges, edges), 1))
    hit = iota((devices, edges), 0) == source
    hits = flag(hit)
    return jnp.sum(jnp.where(hit, dot(hits, earlier), 0.0), axis=0, keepdims=True).astype(I32), hits


def fence(ref):
    def step(n, carry):
        ref[pl.ds(pl.multiple_of(n * 8, 8), 8), :] = jnp.zeros((8, ref.shape[1]), ref.dtype)
        return carry

    lax.fori_loop(0, 2, step, 0)


def serve(asked, kind, cap, table, wide, out):
    devices = asked.shape[0]
    blocks = table.shape[1] // LANES
    each, pitch = cap * blocks, wide.shape[0] // devices
    lanes = iota((devices, table.shape[0]), 1)
    hot = [flag(asked[:, lane : lane + 1] == lanes) for lane in range(kind * cap, kind * cap + cap)]
    got = dot(jnp.concatenate(hot, axis=0), table)
    for slot in range(cap):
        for block in range(blocks):
            target = pl.ds(slot * blocks + block, devices, stride=pitch)
            wide[target, :] = got[slot * devices : (slot + 1) * devices, block * LANES : (block + 1) * LANES]
    for first in range(0, devices, 2):
        pair = [wide[pitch * n : pitch * n + each, :] for n in (first, first + 1)]
        out[each * first : each * (first + 2), :] = jnp.concatenate(pair, axis=0).astype(BF)


def take_in(cap, devices, packed, ends, wide, rows):
    blocks = rows.shape[1] // LANES
    each, pitch = cap * blocks, wide.shape[0] // devices
    rows[cap * devices :, :] = ends
    for first in range(0, devices, 2):
        pair = packed[each * first : each * (first + 2), :].astype(F32)
        wide[pitch * first : pitch * first + each, :] = pair[:each]
        wide[pitch * (first + 1) : pitch * (first + 1) + each, :] = pair[each:]
    for slot in range(cap):
        for block in range(blocks):
            source = pl.ds(slot * blocks + block, devices, stride=pitch)
            target = pl.ds(slot * devices, devices)
            rows[target, block * LANES : (block + 1) * LANES] = wide[source, :].astype(BF)


def ask_kernel(
    cap, devices, dev0, dev1, dev2, row0, row1, row2, lines, request,
    d0, d1, d2, r0, r1, r2, asking, earlier, spare, sems,
):
    edges = lines.shape[1]
    devs, rows = (d0, d1, d2), (r0, r1, r2)
    copies = start(sems, 0, *zip((dev0, dev1, dev2, row0, row1, row2), devs + rows))
    earlier[...] = flag(iota((edges, edges), 0) < iota((edges, edges), 1))
    fence(spare)
    wait(*copies[:3])
    hits = [iota((devices, edges), 0) == dev[...] for dev in devs]
    before = dot(flag(jnp.concatenate(hits, axis=0)), earlier[...])
    wait(*copies[3:])
    few = -(-3 * cap // 16) * 16
    values = []
    for kind in range(3):
        mine = jnp.where(hits[kind], before[kind * devices : (kind + 1) * devices, :], 0.0)
        place = jnp.sum(mine, axis=0, keepdims=True).astype(I32)
        lines[kind : kind + 1, :] = place * devices + devs[kind][...]
        row = line(rows[kind]).astype(F32)
        values.append(jnp.where(iota((few, edges), 0) == place + kind * cap, row, 0.0).astype(BF))
    hits = flag(jnp.concatenate(hits, axis=1))
    asking[:, :few] = dot_lanes(hits, jnp.concatenate(values, axis=1)).astype(I32)
    asking[:, few:] = jnp.zeros((devices, LANES - few), I32)
    wait(*start(sems, 6, (asking, request)))


def prepare_kernel(
    grid, mesh, dst0, dst1, src2, dst2, w, table, kept, w2, w10, ends, w16, dec_kept,
    g, e0, e1, e2, e3, first, w67, mid, dec_kept_v, spare, sems,
):
    count = g.shape[0]
    m = kept.at[pl.ds(count, count)]
    one = dec_kept_v.at[pl.ds(2 * count, count)]
    copies = start(sems, 0, (grid, g), (w.at[pl.ds(6, 2)], w67))
    fence(spare)
    copies += start(sems, 2, (w.at[pl.ds(15, 3)], mid))
    fence(spare)
    copies += start(
        sems, 3, (mesh, m), (w.at[pl.ds(0, 4)], first), (w.at[10], w10), (dst0, e0), (dst1, e1), (src2, e2), (dst2, e3)
    )
    fence(spare)
    wait(*copies[:2])
    one[...] = residual(g[...], finish(dot(g[...], w67[0]), w67[1]))
    wait(copies[2])
    dec_kept_v[:count, :] = dot(one[...], mid[0]).astype(BF)
    dec_kept_v[count : 2 * count, :] = dot(one[...], mid[2]).astype(BF)
    mid[1] = centred(mid[1])
    out = start(sems, len(copies), (mid.at[1], w16), (dec_kept_v, dec_kept))
    fence(spare)
    wait(*copies[3:])
    table[...] = dot(g[...], first[0]).astype(BF)
    kept[:count, :] = dot(m[...], first[1]).astype(BF)
    kept[2 * count :, :] = dot(m[...], first[3]).astype(BF)
    w2[...] = centred(first[2])
    w10[...] = centred(w10[...])
    for n, row in enumerate((e0, e1, e2, e3)):
        ends[n : n + 1, : row.shape[0]] = line(row)
    wait(*out)


def serve_kernel(cap, asked, table, out, wide):
    serve(asked[...], 0, cap, table[...], wide, out)


def enc_kernel(
    cap, received, asked, lines, ends, kept, w2, w, out, proc_kept, w45, w89, w11, wide, rows, sems
):
    copies = start(sems, 0, (w.at[pl.ds(4, 2)], w45))
    fence(wide)
    copies += start(sems, 1, (w.at[pl.ds(8, 2)], w89), (w.at[11], w11))
    fence(wide)
    count = kept.shape[0] // 3
    others = asked.shape[0]
    pick = choose(lines[0:1, :], cap * others)
    to = choose(ends[0:1, :], count)
    to_t = choose_t(ends[0:1, :], count)
    take_in(cap, others, received, kept[:count, :], wide, rows)
    summed = dot(jnp.concatenate([pick, to], axis=1), rows[...])
    message = finish(summed, w2[...], True).astype(BF)
    summed = dot(to_t, message).astype(BF)
    wait(copies[0])
    summed = kept[2 * count :, :].astype(F32) + dot(summed, w45[0])
    mine = residual(kept[count : 2 * count, :], finish(summed, w45[1]))
    wait(*copies[1:])
    table = dot(mine, w89[0]).astype(BF)
    serve(asked[...], 1, cap, table, wide, out)
    proc_kept[:count, :] = dot(mine, w89[1]).astype(BF)
    proc_kept[count : 2 * count, :] = table
    proc_kept[2 * count : 3 * count, :] = dot(mine, w11[...]).astype(BF)
    proc_kept[3 * count :, :] = mine


def proc_kernel(
    cap, local, received, asked, lines, ends, kept, w10, w, dec_far, w16_far, out, dec_kept, w16, ws, wide, rows, sems
):
    copies = start(sems, 0, (w.at[pl.ds(12, 3)], ws))
    fence(wide)
    copies += start(sems, 1, (dec_far, dec_kept), (w16_far, w16))
    fence(wide)
    count = kept.shape[0] // 4
    others = asked.shape[0]
    pick = choose(lines[1:2, :], cap * others)
    to, near_to = choose(ends[1:2, :], count), choose(ends[3:4, :local], count)
    near_from = choose(ends[2:3, :local], count)
    to_t = jnp.concatenate([choose_t(ends[1:2, :], count), choose_t(ends[3:4, :local], count)], axis=1)
    near = dot(jnp.concatenate([near_to, near_from], axis=1), kept[: 2 * count, :])
    take_in(cap, others, received, kept[:count, :], wide, rows)
    far = dot(jnp.concatenate([pick, to], axis=1), rows[...])
    message = finish(jnp.concatenate([far, near], axis=0), w10[...], True).astype(BF)
    summed = dot(to_t, message).astype(BF)
    wait(copies[0])
    summed = kept[2 * count : 3 * count, :].astype(F32) + dot(summed, ws[0])
    two = residual(kept[3 * count :, :], finish(summed, ws[1]))
    serve(asked[...], 2, cap, dot(two, ws[2]).astype(BF), wide, out)
    wait(*copies[1:])


def dec_kernel(cap, others, received, lines, kept, w16, w, out, ws, wide, rows, sems):
    copies = start(sems, 0, (w.at[pl.ds(18, 2)], ws))
    fence(wide)
    edges = lines.shape[1]
    count = kept.shape[0] // 3
    pick = choose(lines[2:3, :], cap * others)
    near = iota((edges, count), 0) - 3 * iota((edges, count), 1)
    to = flag((near >= 0) & (near < 3))
    near = iota((count, edges), 1) - 3 * iota((count, edges), 0)
    to_t = flag((near >= 0) & (near < 3))
    take_in(cap, others, received, kept[:count, :], wide, rows)
    summed = dot(jnp.concatenate([pick, to], axis=1), rows[...])
    message = finish(summed, w16[...], True).astype(BF)
    summed = dot(to_t, message).astype(BF)
    wait(*copies)
    summed = kept[count : 2 * count, :].astype(F32) + dot(summed, ws[0])
    out[...] = residual(kept[2 * count :, :], finish(summed, ws[1]))


def run(kernel, outs=(), near=(), far=(), held=(), copies=0, macs=0, away=(), last=False):
    inside = pl.BlockSpec(memory_space=pltpu.VMEM)
    outside = pl.BlockSpec(memory_space=pltpu.HBM)
    moved = sum(a.size * a.dtype.itemsize for a in list(held) + list(outs))
    return pl.pallas_call(
        kernel,
        out_shape=(
            *(a if last else pltpu.VMEM(a.shape, a.dtype) for a in outs),
            *(pltpu.HBM(a.shape, a.dtype) for a in away),
        ),
        in_specs=[inside] * len(near) + [outside] * len(far),
        out_specs=(inside,) * len(outs) + (outside,) * len(away),
        scratch_shapes=[pltpu.VMEM(a.shape, a.dtype) for a in held]
        + ([pltpu.SemaphoreType.DMA((copies,))] if copies else []),
        compiler_params=pltpu.CompilerParams(vmem_limit_bytes=16 * 2**20),
        cost_estimate=pl.CostEstimate(flops=2 * macs, bytes_accessed=moved, transcendentals=0),
    )(
        *(pltpu.with_memory_space_constraint(a, pltpu.VMEM) for a in near),
        *(pltpu.with_memory_space_constraint(a, pltpu.HBM) for a in far),
    )


def exchange(rows, devices):
    parts = rows.reshape(devices, rows.shape[0] // devices, LANES)
    moved = lax.all_to_all(parts, AXES, split_axis=0, concat_axis=0, tiled=True)
    return moved.reshape(rows.shape)


def body(
    grid_latent,
    mesh_latent,
    weights,
    enc_dev,
    enc_row,
    enc_dst,
    proc_dev,
    proc_row,
    proc_dst,
    loc_src,
    loc_dst,
    dec_dev,
    dec_row,
):
    devices = lax.axis_size("band") * lax.axis_size("patch")
    edges = enc_dev.shape[0]
    cap = max(2, 2 * edges // devices)
    count, width = mesh_latent.shape
    total = devices * cap

    def arr(shape, dtype):
        return jax.ShapeDtypeStruct(shape, dtype)

    across = arr((1, edges), I32)
    row = arr((edges,), I32)
    loc = arr(loc_src.shape, I32)
    mat = arr((width, width), BF)
    square = arr((edges, edges), BF)
    spare = arr((16, LANES), F32)
    nodes = arr((count, width), BF)
    lines = arr((8, edges), I32)
    ask = arr((devices, LANES), I32)
    flat = arr((total * width // LANES, LANES), BF)
    spread = devices * (cap * width // LANES + 1)
    flat32 = arr((spread + 32, LANES), F32)
    rows = arr((total + count, width), BF)
    edge_macs = edges * width * (total + 3 * width)
    devs = tuple(a.reshape(1, edges) for a in (enc_dev, proc_dev, dec_dev))

    def mats(number):
        return arr((number, width, width), BF)

    def kept(parts):
        return arr((parts * count, width), BF)

    places_of, request = run(
        functools.partial(ask_kernel, cap, devices),
        (lines,),
        far=(*devs, enc_row, proc_row, dec_row),
        held=(across,) * 3 + (row,) * 3 + (ask, square, spare),
        copies=7,
        macs=3 * devices * edges * (edges + LANES),
        away=(ask,),
    )
    asked = request.reshape(devices, 1, LANES)
    wanted = lax.all_to_all(asked, AXES, split_axis=0, concat_axis=0, tiled=True).reshape(devices, LANES)
    table, enc_kept, w2, w10, ends, w16_far, dec_far = run(
        prepare_kernel,
        (nodes, kept(3), mat, mat, lines),
        far=(grid_latent, mesh_latent, enc_dst, proc_dst, loc_src, loc_dst, weights),
        held=(nodes, row, row, loc, loc, mats(4), mats(2), mats(3), kept(3), spare),
        copies=12,
        macs=6 * count * width * width,
        away=(mat, kept(3)),
    )
    (sent,) = run(
        functools.partial(serve_kernel, cap),
        (flat,),
        near=(wanted, table),
        held=(flat32,),
        macs=total * count * width,
    )
    enc_rows = exchange(sent, devices)
    sent, proc_kept = run(
        functools.partial(enc_kernel, cap),
        (flat, kept(4)),
        near=(enc_rows, wanted, places_of, ends, enc_kept, w2),
        far=(weights,),
        held=(mats(2), mats(2), mat, flat32, rows),
        copies=3,
        macs=edge_macs,
    )
    proc_rows = exchange(sent, devices)
    sent, dec_kept, w16 = run(
        functools.partial(proc_kernel, cap, loc_src.shape[0]),
        (flat, kept(3), mat),
        near=(proc_rows, wanted, places_of, ends, proc_kept, w10),
        far=(weights, dec_far, w16_far),
        held=(mats(3), flat32, rows),
        copies=3,
        macs=edge_macs,
    )
    dec_rows = exchange(sent, devices)
    (decoded,) = run(
        functools.partial(dec_kernel, cap, devices),
        (nodes,),
        near=(dec_rows, places_of, dec_kept, w16),
        far=(weights,),
        held=(mats(2), flat32, rows),
        copies=1,
        macs=edge_macs,
        last=True,
    )
    return decoded


def solution(mesh):
    rows = P(AXES, None)
    edge = P(AXES)
    in_specs = (rows, rows, P(), rows, edge, edge, rows, edge, edge, edge, edge, rows, edge)
    return jax.shard_map(body, mesh=mesh, in_specs=in_specs, out_specs=rows, check_vma=False)
```

```python
import functools

import jax
import jax.numpy as jnp
from jax import lax
from jax.experimental import pallas as pl
from jax.experimental.pallas import tpu as pltpu
from jax.sharding import PartitionSpec as P

AXES = ("band", "patch")
EPSILON = 1e-05
LANES = 128
BF = jnp.bfloat16
F32 = jnp.float32
I32 = jnp.int32


def dot(a, b):
    return jnp.dot(a, b, preferred_element_type=F32)


def dot_lanes(a, b):
    return lax.dot_general(a, b, (((1,), (1,)), ((), ())), preferred_element_type=F32)


def iota(shape, axis):
    return lax.broadcasted_iota(I32, shape, axis)


def flag(condition):
    return jnp.where(condition, 1.0, 0.0).astype(BF)


def column(row):
    count = row.shape[1]
    same = iota((count, count), 0) == iota((count, count), 1)
    return jnp.sum(jnp.where(same, row.astype(F32), 0.0), axis=1, keepdims=True).astype(I32)


def choose(row, count):
    return flag(iota((row.shape[1], count), 1) == column(row))


def choose_t(row, count):
    return flag(iota((count, row.shape[1]), 0) == row)


def line(ref):
    return ref[...].reshape(1, ref.shape[0])


def silu(v):
    return 0.5 * v * (1.0 + jnp.tanh(0.5 * v))


def centred(matrix):
    wide = matrix.astype(F32)
    return (wide - jnp.mean(wide, axis=-1, keepdims=True)).astype(BF)


def finish(summed, second, zero_mean=False):
    out = dot(silu(summed).astype(BF), second)
    if not zero_mean:
        out = out - jnp.mean(out, axis=-1, keepdims=True)
    return out * lax.rsqrt(jnp.mean(out * out, axis=-1, keepdims=True) + EPSILON)


def residual(base, update):
    return (base.astype(F32) + update).astype(BF)


def start(sems, first, *pairs):
    copies = [pltpu.make_async_copy(src, dst, sems.at[first + n]) for n, (src, dst) in enumerate(pairs)]
    for copy in copies:
        copy.start()
    return copies


def wait(*copies):
    for copy in copies:
        copy.wait()


def places(source, devices):
    edges = source.shape[1]
    earlier = flag(iota((edges, edges), 0) < iota((edges, edges), 1))
    hit = iota((devices, edges), 0) == source
    hits = flag(hit)
    return jnp.sum(jnp.where(hit, dot(hits, earlier), 0.0), axis=0, keepdims=True).astype(I32), hits


def fence(ref):
    def step(n, carry):
        ref[pl.ds(pl.multiple_of(n * 8, 8), 8), :] = jnp.zeros((8, ref.shape[1]), ref.dtype)
        return carry

    lax.fori_loop(0, 2, step, 0)


def serve(asked, kind, cap, table, wide, out):
    devices = asked.shape[0]
    blocks = table.shape[1] // LANES
    each, pitch = cap * blocks, wide.shape[0] // devices
    lanes = iota((devices, table.shape[0]), 1)
    hot = [flag(asked[:, lane : lane + 1] == lanes) for lane in range(kind * cap, kind * cap + cap)]
    got = dot(jnp.concatenate(hot, axis=0), table)
    for slot in range(cap):
        for block in range(blocks):
            target = pl.ds(slot * blocks + block, devices, stride=pitch)
            wide[target, :] = got[slot * devices : (slot + 1) * devices, block * LANES : (block + 1) * LANES]
    for first in range(0, devices, 2):
        pair = [wide[pitch * n : pitch * n + each, :] for n in (first, first + 1)]
        out[each * first : each * (first + 2), :] = jnp.concatenate(pair, axis=0).astype(BF)


def take_in(cap, devices, packed, ends, wide, rows):
    blocks = rows.shape[1] // LANES
    each, pitch = cap * blocks, wide.shape[0] // devices
    rows[cap * devices :, :] = ends
    for first in range(0, devices, 2):
        pair = packed[each * first : each * (first + 2), :].astype(F32)
        wide[pitch * first : pitch * first + each, :] = pair[:each]
        wide[pitch * (first + 1) : pitch * (first + 1) + each, :] = pair[each:]
    for slot in range(cap):
        for block in range(blocks):
            source = pl.ds(slot * blocks + block, devices, stride=pitch)
            target = pl.ds(slot * devices, devices)
            rows[target, block * LANES : (block + 1) * LANES] = wide[source, :].astype(BF)


def ask_kernel(
    cap, devices, dev0, dev1, dev2, row0, row1, row2, lines, request,
    d0, d1, d2, r0, r1, r2, asking, earlier, spare, sems,
):
    edges = lines.shape[1]
    devs, rows = (d0, d1, d2), (r0, r1, r2)
    copies = start(sems, 0, *zip((dev0, dev1, dev2, row0, row1, row2), devs + rows))
    earlier[...] = flag(iota((edges, edges), 0) < iota((edges, edges), 1))
    fence(spare)
    wait(*copies[:3])
    hits = [iota((devices, edges), 0) == dev[...] for dev in devs]
    before = dot(flag(jnp.concatenate(hits, axis=0)), earlier[...])
    wait(*copies[3:])
    few = -(-3 * cap // 16) * 16
    values = []
    for kind in range(3):
        mine = jnp.where(hits[kind], before[kind * devices : (kind + 1) * devices, :], 0.0)
        place = jnp.sum(mine, axis=0, keepdims=True).astype(I32)
        lines[kind : kind + 1, :] = place * devices + devs[kind][...]
        row = line(rows[kind]).astype(F32)
        values.append(jnp.where(iota((few, edges), 0) == place + kind * cap, row, 0.0).astype(BF))
    hits = flag(jnp.concatenate(hits, axis=1))
    asking[:, :few] = dot_lanes(hits, jnp.concatenate(values, axis=1)).astype(I32)
    asking[:, few:] = jnp.zeros((devices, LANES - few), I32)
    wait(*start(sems, 6, (asking, request)))


def prepare_kernel(
    grid, mesh, dst0, dst1, src2, dst2, w, table, kept, w2, w10, ends, w16, dec_kept,
    g, e0, e1, e2, e3, first, w67, mid, dec_kept_v, spare, sems,
):
    count = g.shape[0]
    m = kept.at[pl.ds(count, count)]
    one = dec_kept_v.at[pl.ds(2 * count, count)]
    copies = start(sems, 0, (grid, g), (w.at[pl.ds(6, 2)], w67))
    fence(spare)
    copies += start(sems, 2, (w.at[pl.ds(15, 3)], mid))
    fence(spare)
    copies += start(
        sems, 3, (mesh, m), (w.at[pl.ds(0, 4)], first), (w.at[10], w10), (dst0, e0), (dst1, e1), (src2, e2), (dst2, e3)
    )
    fence(spare)
    wait(*copies[:2])
    one[...] = residual(g[...], finish(dot(g[...], w67[0]), w67[1]))
    wait(copies[2])
    dec_kept_v[:count, :] = dot(one[...], mid[0]).astype(BF)
    dec_kept_v[count : 2 * count, :] = dot(one[...], mid[2]).astype(BF)
    mid[1] = centred(mid[1])
    out = start(sems, len(copies), (mid.at[1], w16), (dec_kept_v, dec_kept))
    fence(spare)
    wait(*copies[3:])
    table[...] = dot(g[...], first[0]).astype(BF)
    kept[:count, :] = dot(m[...], first[1]).astype(BF)
    kept[2 * count :, :] = dot(m[...], first[3]).astype(BF)
    w2[...] = centred(first[2])
    w10[...] = centred(w10[...])
    for n, row in enumerate((e0, e1, e2, e3)):
        ends[n : n + 1, : row.shape[0]] = line(row)
    wait(*out)


def serve_kernel(cap, asked, table, out, wide):
    serve(asked[...], 0, cap, table[...], wide, out)


def enc_kernel(
    cap, received, asked, lines, ends, kept, w2, w, out, proc_kept, w45, w89, w11, wide, rows, sems
):
    copies = start(sems, 0, (w.at[pl.ds(4, 2)], w45))
    copies += start(sems, 1, (w.at[pl.ds(8, 2)], w89), (w.at[11], w11))
    count = kept.shape[0] // 3
    others = asked.shape[0]
    pick = choose(lines[0:1, :], cap * others)
    to = choose(ends[0:1, :], count)
    to_t = choose_t(ends[0:1, :], count)
    take_in(cap, others, received, kept[:count, :], wide, rows)
    summed = dot(jnp.concatenate([pick, to], axis=1), rows[...])
    message = finish(summed, w2[...], True).astype(BF)
    summed = dot(to_t, message).astype(BF)
    wait(copies[0])
    summed = kept[2 * count :, :].astype(F32) + dot(summed, w45[0])
    mine = residual(kept[count : 2 * count, :], finish(summed, w45[1]))
    wait(*copies[1:])
    table = dot(mine, w89[0]).astype(BF)
    serve(asked[...], 1, cap, table, wide, out)
    proc_kept[:count, :] = dot(mine, w89[1]).astype(BF)
    proc_kept[count : 2 * count, :] = table
    proc_kept[2 * count : 3 * count, :] = dot(mine, w11[...]).astype(BF)
    proc_kept[3 * count :, :] = mine


def proc_kernel(
    cap, local, received, asked, lines, ends, kept, w10, w, dec_far, w16_far, out, dec_kept, w16, ws, wide, rows, sems
):
    copies = start(sems, 0, (w.at[pl.ds(12, 3)], ws))
    copies += start(sems, 1, (dec_far, dec_kept), (w16_far, w16))
    count = kept.shape[0] // 4
    others = asked.shape[0]
    pick = choose(lines[1:2, :], cap * others)
    to, near_to = choose(ends[1:2, :], count), choose(ends[3:4, :local], count)
    near_from = choose(ends[2:3, :local], count)
    to_t = jnp.concatenate([choose_t(ends[1:2, :], count), choose_t(ends[3:4, :local], count)], axis=1)
    near = dot(jnp.concatenate([near_to, near_from], axis=1), kept[: 2 * count, :])
    take_in(cap, others, received, kept[:count, :], wide, rows)
    far = dot(jnp.concatenate([pick, to], axis=1), rows[...])
    message = finish(jnp.concatenate([far, near], axis=0), w10[...], True).astype(BF)
    summed = dot(to_t, message).astype(BF)
    wait(copies[0])
    summed = kept[2 * count : 3 * count, :].astype(F32) + dot(summed, ws[0])
    two = residual(kept[3 * count :, :], finish(summed, ws[1]))
    serve(asked[...], 2, cap, dot(two, ws[2]).astype(BF), wide, out)
    wait(*copies[1:])


def dec_kernel(cap, others, received, lines, kept, w16, w, out, ws, wide, rows, sems):
    copies = start(sems, 0, (w.at[pl.ds(18, 2)], ws))
    fence(wide)
    edges = lines.shape[1]
    count = kept.shape[0] // 3
    pick = choose(lines[2:3, :], cap * others)
    near = iota((edges, count), 0) - 3 * iota((edges, count), 1)
    to = flag((near >= 0) & (near < 3))
    near = iota((count, edges), 1) - 3 * iota((count, edges), 0)
    to_t = flag((near >= 0) & (near < 3))
    take_in(cap, others, received, kept[:count, :], wide, rows)
    summed = dot(jnp.concatenate([pick, to], axis=1), rows[...])
    message = finish(summed, w16[...], True).astype(BF)
    summed = dot(to_t, message).astype(BF)
    wait(*copies)
    summed = kept[count : 2 * count, :].astype(F32) + dot(summed, ws[0])
    out[...] = residual(kept[2 * count :, :], finish(summed, ws[1]))


def run(kernel, outs=(), near=(), far=(), held=(), copies=0, macs=0, away=(), last=False):
    inside = pl.BlockSpec(memory_space=pltpu.VMEM)
    outside = pl.BlockSpec(memory_space=pltpu.HBM)
    moved = sum(a.size * a.dtype.itemsize for a in list(held) + list(outs))
    return pl.pallas_call(
        kernel,
        out_shape=(
            *(a if last else pltpu.VMEM(a.shape, a.dtype) for a in outs),
            *(pltpu.HBM(a.shape, a.dtype) for a in away),
        ),
        in_specs=[inside] * len(near) + [outside] * len(far),
        out_specs=(inside,) * len(outs) + (outside,) * len(away),
        scratch_shapes=[pltpu.VMEM(a.shape, a.dtype) for a in held]
        + ([pltpu.SemaphoreType.DMA((copies,))] if copies else []),
        compiler_params=pltpu.CompilerParams(vmem_limit_bytes=16 * 2**20),
        cost_estimate=pl.CostEstimate(flops=2 * macs, bytes_accessed=moved, transcendentals=0),
    )(
        *(pltpu.with_memory_space_constraint(a, pltpu.VMEM) for a in near),
        *(pltpu.with_memory_space_constraint(a, pltpu.HBM) for a in far),
    )


def exchange(rows, devices):
    parts = rows.reshape(devices, rows.shape[0] // devices, LANES)
    moved = lax.all_to_all(parts, AXES, split_axis=0, concat_axis=0, tiled=True)
    return moved.reshape(rows.shape)


def body(
    grid_latent,
    mesh_latent,
    weights,
    enc_dev,
    enc_row,
    enc_dst,
    proc_dev,
    proc_row,
    proc_dst,
    loc_src,
    loc_dst,
    dec_dev,
    dec_row,
):
    devices = lax.axis_size("band") * lax.axis_size("patch")
    edges = enc_dev.shape[0]
    cap = max(2, 2 * edges // devices)
    count, width = mesh_latent.shape
    total = devices * cap

    def arr(shape, dtype):
        return jax.ShapeDtypeStruct(shape, dtype)

    across = arr((1, edges), I32)
    row = arr((edges,), I32)
    loc = arr(loc_src.shape, I32)
    mat = arr((width, width), BF)
    square = arr((edges, edges), BF)
    spare = arr((16, LANES), F32)
    nodes = arr((count, width), BF)
    lines = arr((8, edges), I32)
    ask = arr((devices, LANES), I32)
    flat = arr((total * width // LANES, LANES), BF)
    spread = devices * (cap * width // LANES + 1)
    flat32 = arr((spread + 32, LANES), F32)
    rows = arr((total + count, width), BF)
    edge_macs = edges * width * (total + 3 * width)
    devs = tuple(a.reshape(1, edges) for a in (enc_dev, proc_dev, dec_dev))

    def mats(number):
        return arr((number, width, width), BF)

    def kept(parts):
        return arr((parts * count, width), BF)

    places_of, request = run(
        functools.partial(ask_kernel, cap, devices),
        (lines,),
        far=(*devs, enc_row, proc_row, dec_row),
        held=(across,) * 3 + (row,) * 3 + (ask, square, spare),
        copies=7,
        macs=3 * devices * edges * (edges + LANES),
        away=(ask,),
    )
    asked = request.reshape(devices, 1, LANES)
    wanted = lax.all_to_all(asked, AXES, split_axis=0, concat_axis=0, tiled=True).reshape(devices, LANES)
    table, enc_kept, w2, w10, ends, w16_far, dec_far = run(
        prepare_kernel,
        (nodes, kept(3), mat, mat, lines),
        far=(grid_latent, mesh_latent, enc_dst, proc_dst, loc_src, loc_dst, weights),
        held=(nodes, row, row, loc, loc, mats(4), mats(2), mats(3), kept(3), spare),
        copies=12,
        macs=6 * count * width * width,
        away=(mat, kept(3)),
    )
    (sent,) = run(
        functools.partial(serve_kernel, cap),
        (flat,),
        near=(wanted, table),
        held=(flat32,),
        macs=total * count * width,
    )
    enc_rows = exchange(sent, devices)
    sent, proc_kept = run(
        functools.partial(enc_kernel, cap),
        (flat, kept(4)),
        near=(enc_rows, wanted, places_of, ends, enc_kept, w2),
        far=(weights,),
        held=(mats(2), mats(2), mat, flat32, rows),
        copies=3,
        macs=edge_macs,
    )
    proc_rows = exchange(sent, devices)
    sent, dec_kept, w16 = run(
        functools.partial(proc_kernel, cap, loc_src.shape[0]),
        (flat, kept(3), mat),
        near=(proc_rows, wanted, places_of, ends, proc_kept, w10),
        far=(weights, dec_far, w16_far),
        held=(mats(3), flat32, rows),
        copies=3,
        macs=edge_macs,
    )
    dec_rows = exchange(sent, devices)
    (decoded,) = run(
        functools.partial(dec_kernel, cap, devices),
        (nodes,),
        near=(dec_rows, places_of, dec_kept, w16),
        far=(weights,),
        held=(mats(2), flat32, rows),
        copies=1,
        macs=edge_macs,
        last=True,
    )
    return decoded


def solution(mesh):
    rows = P(AXES, None)
    edge = P(AXES)
    in_specs = (rows, rows, P(), rows, edge, edge, rows, edge, edge, edge, edge, rows, edge)
    return jax.shard_map(body, mesh=mesh, in_specs=in_specs, out_specs=rows, check_vma=False)
```
